32 devices in a mesh: groups: 2 (over y), wide: 4 (over x, core), narrow: 4 (over z).
Axes of the slice: x: 2, y: 2, z: 4, core: 2. Of those that a mesh axis runs over, the one named last changes fastest.
Arguments:
- inputs: bfloat16 [512, 6144], P(('groups', 'narrow'), 'wide'), parts along dimension 0, may hold values from -6 to 6
- up_weight: bfloat16 [6144, 12288], P('wide', 'narrow'), may hold values from -0.078125 to 0.078125
- down_weight: bfloat16 [12288, 6144], P('narrow', 'wide'), may hold values from -0.0546875 to 0.0546875
- out_grad: bfloat16 [512, 6144], P(('groups', 'narrow'), 'wide'), parts along dimension 0, may hold values from -6 to 6
Outputs:
- input_grad: bfloat16 [512, 6144], P(('groups', 'narrow'), 'wide'), parts along dimension 0
- up_grad: float32 [12288, 12288], P(('groups', 'wide'), 'narrow'), parts along dimension 0
- down_grad: float32 [24576, 6144], P(('groups', 'narrow'), 'wide'), parts along dimension 0
The draws below stay inside these ranges and needn't reach their ends.
There are 2 independent parts, one for each index of `groups`. The reference program is written for one: setup_inputs(seed, part) draws one part's arguments, and reference() takes and returns one part's arrays. A program takes and returns all parts, laid end to end along the dimension named above; an argument that names none is the same for every part. Nothing has to cross between parts.
All inputs are finite; a program needn't handle non-finite values.
Results may differ from the reference program's by a relative error of at most 0.018.
Values may be sent and summed in bfloat16 or wider, within the bound.
No kernel may reach another device: no remote copies, remote signals or barrier semaphores. Data moves between devices by JAX's collectives and lax.ppermute only.
A program may use at most 128 MiB of HBM per device.

```python
import jax
import jax.numpy as jnp
from jax import lax

D = 6144
FW = 12288
TOKENS = 256
N_WIDE = 4
N_NARROW = 4


def raised(result, rng, source, target, shards_of, factor):
    def block_of(dim):
        return (jnp.arange(result.shape[dim]) // (result.shape[dim] // shards_of)).reshape((-1,) + (1,) * (result.ndim - 1 - dim))

    first = jax.random.permutation(rng, shards_of)[block_of(target)]
    second = (block_of(target) + shards_of // 2) % shards_of
    return jnp.where((block_of(source) == first) | (block_of(source) == second), factor * result, result)


def shard_levels(own_key, extent, split, smallest, high):
    def one(position, blocks):
        heights = jax.random.uniform(jax.random.fold_in(jax.random.fold_in(own_key, 6), position), (blocks,), jnp.float32, smallest / len(split), high / len(split))
        return jnp.repeat(jnp.exp(heights), extent[position] // blocks).reshape((-1,) + (1,) * (len(extent) - position - 1))

    level = one(*split[0])
    for cut in split[1:]:
        level = level * one(*cut)
    return level


def centred(key, shape, scale, bound, cuts=(), kind=jnp.bfloat16):
    entries = scale * jax.random.normal(key, shape, jnp.float32)
    if cuts:
        entries = entries * shard_levels(key, shape, cuts, -0.22, 0.18)
    return jnp.clip(entries, -bound, bound).astype(kind)


def heavy_noise(rng, shape, spread, bound, cuts, heavy, dtype=jnp.bfloat16):
    entries = spread * jax.random.normal(rng, shape, jnp.float32)
    if cuts:
        entries = entries * shard_levels(rng, shape, cuts, -0.22, 0.18)
    return jnp.clip(raised(entries, jax.random.fold_in(rng, 3), *heavy), -bound, bound).astype(dtype)


def setup_inputs(seed: int = 0, part: int = 0) -> dict:
    streams_of = jax.random.split(jax.random.key(seed), 5)
    part_keys = jax.random.split(jax.random.fold_in(streams_of[4], part), 5)
    return {
        "inputs": heavy_noise(part_keys[0], (TOKENS, D), 1.0, 6.0, ((0, 4), (1, 4)), (1, 0, 4, 2.0)),
        "up_weight": centred(streams_of[1], (D, FW), D ** -0.5, 0.078125, ((0, 4), (1, 4))),
        "down_weight": centred(streams_of[2], (FW, D), FW ** -0.5, 0.0546875, ((0, 4), (1, 4))),
        "out_grad": heavy_noise(part_keys[3], (TOKENS, D), 1.0, 6.0, ((0, 4), (1, 4)), (1, 0, 4, 2.0)),
    }


def gelu_parts(hidden):
    normal_cdf = 0.5 * (1.0 + jax.scipy.special.erf(hidden * 0.7071067811865476))
    normal_pdf = jnp.exp(-0.5 * hidden * hidden) * 0.3989422804014327
    return hidden * normal_cdf, normal_cdf + hidden * normal_pdf


def rounded(values):
    narrowed = lax.optimization_barrier(values.astype(jnp.bfloat16))
    return narrowed.astype(jnp.float32)


def reference(inputs, up_weight, down_weight, out_grad):
    feat_block = D // N_WIDE
    unit_block = FW // N_NARROW
    hidden = jnp.zeros((TOKENS, FW), jnp.float32)
    grad_hidden = jnp.zeros((TOKENS, FW), jnp.float32)
    for block_idx in range(N_WIDE):
        lower = block_idx * feat_block
        upper = lower + feat_block
        hidden = hidden + rounded(jnp.dot(inputs[:, lower:upper], up_weight[lower:upper, :], preferred_element_type=jnp.float32))
        grad_hidden = grad_hidden + rounded(jnp.dot(out_grad[:, lower:upper], down_weight[:, lower:upper].T, preferred_element_type=jnp.float32))
    gelu_value, gelu_slope = gelu_parts(hidden)
    activation = gelu_value.astype(jnp.bfloat16)
    grad_act = (grad_hidden * gelu_slope).astype(jnp.bfloat16)
    input_sum = jnp.zeros((TOKENS, D), jnp.float32)
    for block_idx in range(N_NARROW):
        lower = block_idx * unit_block
        upper = lower + unit_block
        input_sum = input_sum + rounded(jnp.dot(grad_act[:, lower:upper], up_weight[:, lower:upper].T, preferred_element_type=jnp.float32))
    input_grad = input_sum.astype(jnp.bfloat16)
    loss_scale = TOKENS ** -0.5
    up_grad = jnp.dot(inputs.T, grad_act, preferred_element_type=jnp.float32) * loss_scale
    down_grad = jnp.dot(activation.T, out_grad, preferred_element_type=jnp.float32) * loss_scale
    return (input_grad, up_grad, down_grad)
```

```python
import functools

import jax
import jax.numpy as jnp
from jax import lax
from jax.experimental import pallas as pl
from jax.experimental.pallas import tpu as pltpu
from jax.sharding import PartitionSpec as P

F32, BF16 = jnp.float32, jnp.bfloat16
MIB = 1 << 20
VMEM = pltpu.VMEM
NN = (((1,), (0,)), ((), ()))
NT = (((1,), (1,)), ((), ()))
TN = (((0,), (0,)), ((), ()))


def dot(a, b, dims):
    return lax.dot_general(a, b, dims, preferred_element_type=F32)


def call(body, outs, args, flops, bytes_accessed, limit=24 * MIB, transcendentals=0, scratch=(), name=None):
    return pl.pallas_call(
        body,
        out_shape=outs,
        in_specs=[pl.BlockSpec(memory_space=pltpu.SMEM if a.dtype == jnp.int32 else VMEM) for a in args],
        out_specs=jax.tree.map(lambda _: pl.BlockSpec(memory_space=VMEM), outs),
        scratch_shapes=scratch,
        compiler_params=pltpu.CompilerParams(vmem_limit_bytes=limit),
        cost_estimate=pl.CostEstimate(flops=flops, bytes_accessed=bytes_accessed, transcendentals=transcendentals),
        name=name,
    )(*args)


def hidden_products(core, tokens, up_weight, down_weight):
    _, rows, features = tokens.shape
    half = up_weight.shape[1] // 2
    tile = 512 if half % 512 == 0 else half

    def body(core_ref, tokens_ref, up_ref, down_ref, give_ref, keep_ref):
        me = core_ref[0]
        for out_ref, base in ((give_ref, (1 - me) * half), (keep_ref, me * half)):
            for start in range(0, half, tile):
                units = pl.ds(pl.multiple_of(base + start, tile), tile)
                out_ref[0, :, start : start + tile] = dot(tokens_ref[0], up_ref[:, units], NN).astype(BF16)
                out_ref[1, :, start : start + tile] = dot(tokens_ref[1], down_ref[units, :], NT).astype(BF16)

    out = jax.ShapeDtypeStruct((2, rows, half), BF16)
    weights = [pltpu.with_memory_space_constraint(w, VMEM) for w in (up_weight, down_weight)]
    return call(
        body, (out, out), (core, tokens, *weights), 8 * rows * features * half, 4 * 2 * features * half, name="hidden_products"
    )


def input_product(core, mine, other, up_weight):
    rows, half = mine.shape
    features = up_weight.shape[0]
    tile = 512 if features % 512 == 0 else features

    def body(core_ref, mine_ref, other_ref, up_ref, out_ref):
        me = core_ref[0]
        own_units = pl.ds(pl.multiple_of(me * half, half), half)
        other_units = pl.ds(pl.multiple_of((1 - me) * half, half), half)
        for start in range(0, features, tile):
            part = slice(start, start + tile)
            out_ref[:, part] = (
                dot(mine_ref[...], up_ref[part, own_units], NT) + dot(other_ref[...], up_ref[part, other_units], NT)
            ).astype(BF16)

    weight = pltpu.with_memory_space_constraint(up_weight, VMEM)
    return call(
        body,
        jax.ShapeDtypeStruct((rows, features), BF16),
        (core, mine, other, weight),
        4 * rows * features * half,
        4 * features * half,
        name="input_product",
    )


def gelu_kernel(own, peer):
    _, rows, half = own.shape

    def body(own_ref, peer_ref, out_ref):
        hidden = own_ref[0].astype(F32) + peer_ref[0].astype(F32)
        grad_hidden = own_ref[1].astype(F32) + peer_ref[1].astype(F32)
        cdf = 0.5 * (1.0 + lax.erf(hidden * 0.7071067811865476))
        pdf = jnp.exp(-0.5 * hidden * hidden) * 0.3989422804014327
        out_ref[0] = (grad_hidden * (cdf + hidden * pdf)).astype(BF16)
        out_ref[1] = (hidden * cdf).astype(BF16)

    return call(
        body, jax.ShapeDtypeStruct((2, rows, half), BF16), (own, peer), 40 * rows * half, 12 * rows * half, name="gelu"
    )


def weight_grad(core, left_chunks, right_chunks, which, left_split, right_split, scale, name):
    def flat(chunks, split):
        return [a for pair in chunks for a in pair] if split else list(chunks)

    left, right = flat(left_chunks, left_split), flat(right_chunks, right_split)
    count = len(left_chunks)
    rows = left[0].shape[1]
    wide_left = left[0].shape[2] * (2 if left_split else 1)
    wide_right = right[0].shape[2] * (2 if right_split else 1)
    tokens = rows * count
    tile = 256 if wide_left % 256 == 0 else 128

    def fill(me, refs, split, scratch, index):
        for chunk in range(count):
            at = slice(chunk * rows, (chunk + 1) * rows)
            if split:
                half = scratch.shape[1] // 2
                scratch[at, pl.ds(pl.multiple_of(me * half, half), half)] = refs[2 * chunk][index]
                scratch[at, pl.ds(pl.multiple_of((1 - me) * half, half), half)] = refs[2 * chunk + 1][index]
            else:
                scratch[at, :] = refs[chunk][index]

    def body(core_ref, *refs):
        left_refs, right_refs = refs[: len(left)], refs[len(left) : len(left) + len(right)]
        out_ref, left_all, right_all = refs[len(left) + len(right) :]

        @pl.when(pl.program_id(0) == 0)
        def _():
            fill(core_ref[0], left_refs, left_split, left_all, which[0])
            fill(core_ref[0], right_refs, right_split, right_all, which[1])

        part = pl.ds(pl.multiple_of(pl.program_id(0) * tile, tile), tile)
        out_ref[...] = dot(left_all[:, part], right_all[...], TN) * scale

    return pl.pallas_call(
        body,
        grid=(wide_left // tile,),
        out_shape=jax.ShapeDtypeStruct((wide_left, wide_right), F32),
        in_specs=[pl.BlockSpec(memory_space=pltpu.SMEM)] + [pl.BlockSpec(memory_space=VMEM)] * (len(left) + len(right)),
        out_specs=pl.BlockSpec((tile, wide_right), lambda i: (i, 0)),
        scratch_shapes=[VMEM((tokens, wide_left), BF16), VMEM((tokens, wide_right), BF16)],
        compiler_params=pltpu.CompilerParams(vmem_limit_bytes=24 * MIB),
        cost_estimate=pl.CostEstimate(
            flops=2 * tokens * wide_left * wide_right, bytes_accessed=4 * wide_left * wide_right, transcendentals=0
        ),
        name=name,
    )(core, *left, *right)


def per_device(wide, narrow, inputs, up_weight, down_weight, out_grad):
    rows = inputs.shape[0]
    chips = wide // 2
    place = lax.axis_index("narrow")
    core = (lax.axis_index("wide") % 2).astype(jnp.int32).reshape(1)

    def swap_cores(x):
        return lax.ppermute(x, "wide", [(i, i ^ 1) for i in range(wide)])

    tokens = jnp.stack([inputs, out_grad])

    below, above = [tokens], [tokens]
    for step in range(1, narrow):
        below.append(lax.ppermute(below[-1], "narrow", [(i, i + 1) for i in range(step - 1, narrow - 1)]))
        above.append(lax.ppermute(above[-1], "narrow", [(i + 1, i) for i in range(0, narrow - step)]))

    chunks = [tokens]
    for step in range(1, narrow):
        value = None
        for d in range(1, step + 1):
            if any(i - (i ^ step) == d for i in range(narrow)):
                value = below[d] if value is None else jnp.where(place - (place ^ step) == d, below[d], value)
            if any((i ^ step) - i == d for i in range(narrow)):
                value = above[d] if value is None else jnp.where((place ^ step) - place == d, above[d], value)
        chunks.append(value)

    mine, other, returned = [], [], None
    for step, chunk in enumerate(chunks):
        give, keep = hidden_products(core, chunk, up_weight, down_weight)
        got = swap_cores(give)
        partial = (keep.astype(F32) + got.astype(F32)).astype(BF16)
        hop = 1
        while hop < chips:
            peer = lax.ppermute(partial, "wide", [(i, i ^ (2 * hop)) for i in range(wide)])
            if 2 * hop < chips:
                partial = (partial.astype(F32) + peer.astype(F32)).astype(BF16)
            hop *= 2
        own_half = gelu_kernel(partial, peer)
        other_half = swap_cores(own_half)
        mine.append(own_half)
        other.append(other_half)
        share = input_product(core, own_half[0], other_half[0], up_weight)
        if step:
            share = lax.ppermute(share, "narrow", [(i, i ^ step) for i in range(narrow)])
        returned = share.astype(F32) if returned is None else returned + share.astype(F32)
    scale = (rows * narrow) ** -0.5
    acts = list(zip(mine, other))
    up_grad = weight_grad(core, chunks, acts, (0, 0), False, True, scale, "up_grad")
    down_grad = weight_grad(core, acts, chunks, (1, 1), True, False, scale, "down_grad")
    return returned.astype(BF16), up_grad, down_grad


def solution(mesh):
    placed = (
        P(("groups", "narrow"), "wide"),
        P("wide", "narrow"),
        P("narrow", "wide"),
        P(("groups", "narrow"), "wide"),
    )
    return jax.shard_map(
        functools.partial(per_device, mesh.shape["wide"], mesh.shape["narrow"]),
        mesh=mesh,
        in_specs=placed,
        out_specs=(
            P(("groups", "narrow"), "wide"),
            P(("groups", "wide"), "narrow"),
            P(("groups", "narrow"), "wide"),
        ),
        check_vma=False,
    )
```

```python
import functools

import jax
import jax.numpy as jnp
from jax import lax
from jax.experimental import pallas as pl
from jax.experimental.pallas import tpu as pltpu
from jax.sharding import PartitionSpec as P

F32, BF16 = jnp.float32, jnp.bfloat16
MIB = 1 << 20
VMEM = pltpu.VMEM
NN = (((1,), (0,)), ((), ()))
NT = (((1,), (1,)), ((), ()))
TN = (((0,), (0,)), ((), ()))


def dot(a, b, dims):
    return lax.dot_general(a, b, dims, preferred_element_type=F32)


def in_vmem(x):
    return pltpu.with_memory_space_constraint(x, VMEM)


def in_hbm(x):
    return pltpu.with_memory_space_constraint(x, pltpu.HBM)


def whole(x):
    return pl.BlockSpec(memory_space=pltpu.SMEM if x.dtype == jnp.int32 else VMEM)


def params(limit_mib):
    return pltpu.CompilerParams(vmem_limit_bytes=limit_mib * MIB)


def cost(flops, bytes_accessed):
    return pl.CostEstimate(flops=flops, bytes_accessed=bytes_accessed, transcendentals=0)


def tile_of(extent):
    return next(t for t in (512, 384, 256, 128) if extent % t == 0)


def load_and_product(core, other, tokens, up_weight, down_weight, name):
    _, rows, features = tokens.shape
    half = up_weight.shape[1] // 2
    tile = tile_of(half)
    pieces = half // tile

    def body(core_ref, tokens_ref, up_hbm, down_hbm, up_ref, down_ref, out_ref, sems):
        side = 1 - core_ref[0] if other else core_ref[0]
        base = side * half
        copies = []
        for i in range(pieces):
            units = pl.ds(pl.multiple_of(base + i * tile, tile), tile)
            part = pl.ds(i * tile, tile)
            copies.append(
                (
                    pltpu.make_async_copy(up_hbm.at[:, units], up_ref.at[:, part], sems.at[2 * i]),
                    pltpu.make_async_copy(down_hbm.at[units, :], down_ref.at[part, :], sems.at[2 * i + 1]),
                )
            )
        for first, second in copies:
            first.start()
            second.start()
        for i, (first, second) in enumerate(copies):
            part = slice(i * tile, (i + 1) * tile)
            first.wait()
            out_ref[0, :, part] = dot(tokens_ref[0], up_ref[:, part], NN).astype(BF16)
            second.wait()
            out_ref[1, :, part] = dot(tokens_ref[1], down_ref[part, :], NT).astype(BF16)

    hbm = pl.BlockSpec(memory_space=pl.ANY)
    return pl.pallas_call(
        body,
        out_shape=(
            VMEM((features, half), BF16),
            VMEM((half, features), BF16),
            jax.ShapeDtypeStruct((2, rows, half), BF16),
        ),
        in_specs=[whole(core), whole(tokens), hbm, hbm],
        out_specs=(pl.BlockSpec(memory_space=VMEM),) * 3,
        scratch_shapes=[pltpu.SemaphoreType.DMA((2 * pieces,))],
        compiler_params=params(24),
        cost_estimate=cost(4 * rows * features * half, 4 * features * half),
        name=name,
    )(core, tokens, in_hbm(up_weight), in_hbm(down_weight))


def product(tokens, up_half, down_half, name):
    _, rows, features = tokens.shape
    half = up_half.shape[1]
    tile = tile_of(half)

    def body(tokens_ref, up_ref, down_ref, out_ref):
        for start in range(0, half, tile):
            part = slice(start, start + tile)
            out_ref[0, :, part] = dot(tokens_ref[0], up_ref[:, part], NN).astype(BF16)
            out_ref[1, :, part] = dot(tokens_ref[1], down_ref[part, :], NT).astype(BF16)

    args = (tokens, in_vmem(up_half), in_vmem(down_half))
    return pl.pallas_call(
        body,
        out_shape=jax.ShapeDtypeStruct((2, rows, half), BF16),
        in_specs=[whole(a) for a in args],
        out_specs=pl.BlockSpec(memory_space=VMEM),
        compiler_params=params(16),
        cost_estimate=cost(4 * rows * features * half, 4 * features * half),
        name=name,
    )(*args)


def input_product(mine, other, up_mine, up_other, so_far):
    _, rows, half = mine.shape
    features = up_mine.shape[0]
    tile = tile_of(features)

    def body(mine_ref, other_ref, up_mine_ref, up_other_ref, *refs):
        for start in range(0, features, tile):
            part = slice(start, start + tile)
            share = dot(mine_ref[0], up_mine_ref[part, :], NT) + dot(other_ref[0], up_other_ref[part, :], NT)
            if so_far is not None:
                share = share + refs[0][:, part].astype(F32)
            refs[-1][:, part] = share.astype(BF16)

    args = (mine, other, in_vmem(up_mine), in_vmem(up_other)) + (() if so_far is None else (so_far,))
    return pl.pallas_call(
        body,
        out_shape=jax.ShapeDtypeStruct((rows, features), BF16),
        in_specs=[whole(a) for a in args],
        out_specs=pl.BlockSpec(memory_space=VMEM),
        compiler_params=params(16),
        cost_estimate=cost(4 * rows * features * half, 4 * features * half),
        name="input_product",
    )(*args)


def gelu_kernel(own, peer):
    _, rows, half = own.shape

    def body(own_ref, peer_ref, out_ref):
        hidden = own_ref[0].astype(F32) + peer_ref[0].astype(F32)
        grad_hidden = own_ref[1].astype(F32) + peer_ref[1].astype(F32)
        cdf = 0.5 * (1.0 + lax.erf(hidden * 0.7071067811865476))
        pdf = jnp.exp(-0.5 * hidden * hidden) * 0.3989422804014327
        out_ref[0] = (grad_hidden * (cdf + hidden * pdf)).astype(BF16)
        out_ref[1] = (hidden * cdf).astype(BF16)

    return pl.pallas_call(
        body,
        out_shape=jax.ShapeDtypeStruct((2, rows, half), BF16),
        in_specs=[whole(own), whole(peer)],
        out_specs=pl.BlockSpec(memory_space=VMEM),
        compiler_params=params(16),
        cost_estimate=cost(40 * rows * half, 12 * rows * half),
        name="gelu",
    )(own, peer)


def weight_grad(core, left_chunks, right_chunks, which, left_split, right_split, tile, scale, name):
    def flat(chunks, split):
        return [a for pair in chunks for a in pair] if split else list(chunks)

    left, right = flat(left_chunks, left_split), flat(right_chunks, right_split)
    count = len(left_chunks)
    rows = left[0].shape[1]
    wide_left = left[0].shape[2] * (2 if left_split else 1)
    wide_right = right[0].shape[2] * (2 if right_split else 1)
    tokens = rows * count
    tile = next(t for t in (tile, 256, 128) if wide_left % t == 0)

    def fill(me, refs, split, scratch, index):
        for chunk in range(count):
            at = slice(chunk * rows, (chunk + 1) * rows)
            if split:
                half = scratch.shape[1] // 2
                scratch[at, pl.ds(pl.multiple_of(me * half, half), half)] = refs[2 * chunk][index]
                scratch[at, pl.ds(pl.multiple_of((1 - me) * half, half), half)] = refs[2 * chunk + 1][index]
            else:
                scratch[at, :] = refs[chunk][index]

    def body(core_ref, *refs):
        left_refs, right_refs = refs[: len(left)], refs[len(left) : len(left) + len(right)]
        out_ref, left_all, right_all = refs[len(left) + len(right) :]

        @pl.when(pl.program_id(0) == 0)
        def _():
            fill(core_ref[0], left_refs, left_split, left_all, which[0])
            fill(core_ref[0], right_refs, right_split, right_all, which[1])

        part = pl.ds(pl.multiple_of(pl.program_id(0) * tile, tile), tile)
        out_ref[...] = dot(left_all[:, part], right_all[...], TN) * scale

    return pl.pallas_call(
        body,
        grid=(wide_left // tile,),
        out_shape=jax.ShapeDtypeStruct((wide_left, wide_right), F32),
        in_specs=[whole(core)] + [pl.BlockSpec(memory_space=VMEM)] * (len(left) + len(right)),
        out_specs=pl.BlockSpec((tile, wide_right), lambda i: (i, 0)),
        scratch_shapes=[VMEM((tokens, wide_left), BF16), VMEM((tokens, wide_right), BF16)],
        compiler_params=params(24),
        cost_estimate=cost(2 * tokens * wide_left * wide_right, 4 * wide_left * wide_right),
        name=name,
    )(core, *left, *right)


def per_device(wide, narrow, inputs, up_weight, down_weight, out_grad):
    rows = inputs.shape[0]
    chips = wide // 2
    core = (lax.axis_index("wide") & 1).astype(jnp.int32).reshape(1)

    def swap_cores(x):
        return lax.ppermute(x, "wide", [(i, i ^ 1) for i in range(wide)])

    def pass_on(x):
        return lax.ppermute(x, "narrow", [(i, (i + 1) % narrow) for i in range(narrow)])

    chunks = [jnp.stack([inputs, out_grad])]
    for _ in range(1, narrow):
        chunks.append(pass_on(chunks[-1]))

    acts = []
    share = kept = None
    for step, chunk in enumerate(chunks):
        if step == 0:
            up_other, down_other, give = load_and_product(core, True, chunk, up_weight, down_weight, "give_first")
            got = swap_cores(give)
            up_mine, down_mine, keep = load_and_product(core, False, chunk, up_weight, down_weight, "keep_first")
        else:
            give = product(chunk, up_other, down_other, "give")
            got = swap_cores(give)
            keep = product(chunk, up_mine, down_mine, "keep")
        partial = (keep.astype(F32) + got.astype(F32)).astype(BF16)
        hop = 1
        while hop < chips:
            peer = lax.ppermute(partial, "wide", [(i, i ^ (2 * hop)) for i in range(wide)])
            if 2 * hop < chips:
                partial = (partial.astype(F32) + peer.astype(F32)).astype(BF16)
            hop *= 2
        mine = gelu_kernel(partial, peer)
        other = swap_cores(mine)
        acts.append((mine, other))
        if step == 0:
            kept = input_product(mine, other, up_mine, up_other, None)
        else:
            share = pass_on(input_product(mine, other, up_mine, up_other, share))
    input_grad = kept if share is None else (kept.astype(F32) + share.astype(F32)).astype(BF16)
    scale = (rows * narrow) ** -0.5
    up_grad = weight_grad(core, chunks, acts, (0, 0), False, True, 256, scale, "up_grad")
    down_grad = weight_grad(core, acts, chunks, (1, 1), True, False, 512, scale, "down_grad")
    return input_grad, up_grad, down_grad


def solution(mesh):
    placed = (
        P(("groups", "narrow"), "wide"),
        P("wide", "narrow"),
        P("narrow", "wide"),
        P(("groups", "narrow"), "wide"),
    )
    return jax.shard_map(
        functools.partial(per_device, mesh.shape["wide"], mesh.shape["narrow"]),
        mesh=mesh,
        in_specs=placed,
        out_specs=(
            P(("groups", "narrow"), "wide"),
            P(("groups", "wide"), "narrow"),
            P(("groups", "narrow"), "wide"),
        ),
        check_vma=False,
    )
```

```python
import functools

import jax
import jax.numpy as jnp
from jax import lax
from jax.experimental import pallas as pl
from jax.experimental.pallas import tpu as pltpu
from jax.sharding import PartitionSpec as P

F32, BF16 = jnp.float32, jnp.bfloat16
MIB = 1 << 20
WEIGHT = 262144
VMEM = pltpu.VMEM
NN = (((1,), (0,)), ((), ()))
NT = (((1,), (1,)), ((), ()))
TN = (((0,), (0,)), ((), ()))


def dot(a, b, dims):
    return lax.dot_general(a, b, dims, preferred_element_type=F32)


def in_vmem(x):
    return pltpu.with_memory_space_constraint(x, VMEM)


def in_hbm(x):
    return pltpu.with_memory_space_constraint(x, pltpu.HBM)


def tile_of(extent, largest=512):
    return next(t for t in (768, 512, 384, 256, 128) if t <= largest and extent % t == 0)


class Ordered:
    def __init__(self):
        self.last = None

    def __call__(self, body, args, outs, name, micros, limit=16, spaces=None, out_spaces=None, scratch=(), aliases=None):
        args = list(args)
        spaces = spaces or [None] * len(args)
        specs = [
            pl.BlockSpec(memory_space=pltpu.SMEM if a.dtype == jnp.int32 else space or VMEM) for a, space in zip(args, spaces)
        ]
        count = len(args)
        if self.last is not None:
            args.append(self.last)
            specs.append(pl.BlockSpec(memory_space=pl.ANY))
        extra = len(args) - count

        def kernel(*refs):
            body(*refs[:count], *refs[count + extra :])

        result = pl.pallas_call(
            kernel,
            out_shape=outs,
            in_specs=specs,
            out_specs=[pl.BlockSpec(memory_space=s) for s in out_spaces or [VMEM] * len(outs)],
            scratch_shapes=scratch,
            input_output_aliases=aliases or {},
            compiler_params=pltpu.CompilerParams(vmem_limit_bytes=limit * MIB),
            cost_estimate=pl.CostEstimate(flops=0, bytes_accessed=int(micros * WEIGHT), transcendentals=0),
            name=name,
        )(*args)
        self.last = result[-1]
        return result


def first_product(ordered, core, other, tokens, weight, units_dim, name):
    rows, features = tokens.shape
    half = weight.shape[units_dim] // 2
    tile = tile_of(half, 256)
    pieces = half // tile

    def body(core_ref, tokens_ref, weight_hbm, weight_ref, out_ref, sems):
        side = 1 - core_ref[0] if other else core_ref[0]
        copies = []
        for i in range(pieces):
            units = pl.ds(pl.multiple_of(side * half + i * tile, tile), tile)
            part = pl.ds(i * tile, tile)
            at = (lambda u: (slice(None), u)) if units_dim else (lambda u: (u, slice(None)))
            copies.append(pltpu.make_async_copy(weight_hbm.at[at(units)], weight_ref.at[at(part)], sems.at[i]))
        for copy in copies:
            copy.start()
        for i, copy in enumerate(copies):
            part = slice(i * tile, (i + 1) * tile)
            copy.wait()
            if units_dim:
                out_ref[:, part] = dot(tokens_ref[...], weight_ref[:, part], NN).astype(BF16)
            else:
                out_ref[:, part] = dot(tokens_ref[...], weight_ref[part, :], NT).astype(BF16)

    shape = (features, half) if units_dim else (half, features)
    return ordered(
        body,
        (core, tokens, in_hbm(weight)),
        [VMEM(shape, BF16), jax.ShapeDtypeStruct((rows, half), BF16)],
        name,
        2.5,
        spaces=[None, None, pl.ANY],
        scratch=[pltpu.SemaphoreType.DMA((pieces,))],
    )


def product(ordered, tokens, grads, up_half, down_half, name):
    rows, features = tokens.shape
    half = up_half.shape[1]
    tile = tile_of(half)

    def body(tokens_ref, grads_ref, up_ref, down_ref, out_ref):
        for start in range(0, half, tile):
            part = slice(start, start + tile)
            out_ref[0, :, part] = dot(tokens_ref[...], up_ref[:, part], NN).astype(BF16)
            out_ref[1, :, part] = dot(grads_ref[...], down_ref[part, :], NT).astype(BF16)

    args = (tokens, grads, in_vmem(up_half), in_vmem(down_half))
    return ordered(body, args, [jax.ShapeDtypeStruct((2, rows, half), BF16)], name, 2.4)[0]


def input_product(ordered, chunks, up_mine, up_other, so_far):
    rows = chunks[0][0][0].shape[1]
    features = up_mine.shape[0]
    tile = tile_of(features)
    flat = [a for chunk in chunks for pair in chunk for a in pair]
    widths = [pair[0].shape[2] for pair in chunks[0]]

    def body(up_mine_ref, up_other_ref, *refs):
        act_refs, out_refs = refs[: len(flat)], refs[len(refs) - len(chunks) :]
        for start in range(0, features, tile):
            part = slice(start, start + tile)
            share = None
            low = 0
            for i, width in enumerate(widths):
                for side, up_ref in enumerate((up_mine_ref, up_other_ref)):
                    acts = [act_refs[(c * len(widths) + i) * 2 + side][0] for c in range(len(chunks))]
                    acts = acts[0] if len(acts) == 1 else jnp.concatenate(acts, axis=0)
                    term = dot(acts, up_ref[part, low : low + width], NT)
                    share = term if share is None else share + term
                low += width
            for c, out_ref in enumerate(out_refs):
                own = share[c * rows : (c + 1) * rows]
                if so_far is not None and c == len(chunks) - 1:
                    own = own + refs[len(flat)][:, part].astype(F32)
                out_ref[:, part] = own.astype(BF16)

    args = (in_vmem(up_mine), in_vmem(up_other), *flat) + (() if so_far is None else (so_far,))
    return ordered(body, args, [jax.ShapeDtypeStruct((rows, features), BF16)] * len(chunks), "input_product", 3.0)


def gelu(ordered, own, peer):
    rows, units = own[0].shape[-2:]
    args = (own, peer) if not isinstance(own, tuple) else (*own, *peer)

    def body(*refs):
        parts = [r[i] for r in refs[:-1] for i in (0, 1)] if len(refs) == 3 else [r[...] for r in refs[:-1]]
        own_hidden, own_grad, peer_hidden, peer_grad = [p.astype(F32) for p in parts]
        hidden, grad_hidden = own_hidden + peer_hidden, own_grad + peer_grad
        cdf = 0.5 * (1.0 + lax.erf(hidden * 0.7071067811865476))
        pdf = jnp.exp(-0.5 * hidden * hidden) * 0.3989422804014327
        refs[-1][0] = (grad_hidden * (cdf + hidden * pdf)).astype(BF16)
        refs[-1][1] = (hidden * cdf).astype(BF16)

    return ordered(body, args, [jax.ShapeDtypeStruct((2, rows, units), BF16)], "gelu", 0.3)[0]


def collect(ordered, tokens, grads):
    count = len(tokens)
    rows, features = tokens[0].shape
    tile = tile_of(features, 256)

    def body(*refs):
        turned_ref, grads_ref, scratch = refs[2 * count :]
        for i in range(count):
            scratch[i * rows : (i + 1) * rows, :] = refs[i][...]
            grads_ref[i * rows : (i + 1) * rows, :] = refs[count + i][...]
        for start in range(0, features, tile):
            turned_ref[start : start + tile, :] = scratch[:, start : start + tile].T

    outs = [VMEM((features, rows * count), BF16), VMEM((rows * count, features), BF16)]
    return ordered(body, (*tokens, *grads), outs, "collect", 1.5, scratch=[VMEM((rows * count, features), BF16)])


def weight_grads(ordered, core, blocks, turned, all_grads, half, scale, before, name):
    features, tokens = turned.shape
    rows = tokens // len(blocks[0][2])
    width = min(a.shape[2] for a, _ in blocks[0][2])
    up_tile, down_tile = tile_of(features), tile_of(width, 256)
    up_steps, down_steps = features // up_tile, width // down_tile
    slots = 3
    flat = [a for block in blocks for a, _ in block[2]]

    def body(core_ref, turned_ref, grads_ref, *refs):
        up_hbm, down_hbm, done_ref, act_g, act_v, up_stage, down_stage, sems = refs[-8:]
        done_ref[...] = jnp.zeros_like(done_ref)
        busy = {}

        def send(kind, index, value, stage, target):
            slot = index % slots
            if (kind, slot) in busy:
                busy[kind, slot].wait()
            stage[slot] = value * scale
            copy = pltpu.make_async_copy(stage.at[slot], target, sems.at[kind, slot])
            copy.start()
            busy[kind, slot] = copy

        for b, (other, first, acts) in enumerate(blocks):
            side = 1 - core_ref[0] if other else core_ref[0]
            base = side * half + first
            for i, (_, column) in enumerate(acts):
                ref = refs[b * len(acts) + i]
                act_g[i * rows : (i + 1) * rows, :] = ref[0, :, column : column + width]
                act_v[i * rows : (i + 1) * rows, :] = ref[1, :, column : column + width]
            for step in range(max(up_steps, down_steps)):
                if step < up_steps:
                    part = slice(step * up_tile, (step + 1) * up_tile)
                    value = dot(turned_ref[part, :], act_g[...], NN)
                    target = up_hbm.at[pl.ds(step * up_tile, up_tile), pl.ds(pl.multiple_of(base, 128), width)]
                    send(0, b * up_steps + step, value, up_stage, target)
                if step < down_steps:
                    part = slice(step * down_tile, (step + 1) * down_tile)
                    value = dot(act_v[:, part], grads_ref[...], TN)
                    target = down_hbm.at[pl.ds(pl.multiple_of(base + step * down_tile, 128), down_tile), :]
                    send(1, b * down_steps + step, value, down_stage, target)
        for copy in busy.values():
            copy.wait()

    args = [core, turned, all_grads, *flat]
    spaces = [None] * len(args)
    aliases = {}
    if before is not None:
        aliases = {len(args): 0, len(args) + 1: 1}
        args += [in_hbm(a) for a in before]
        spaces += [pl.ANY, pl.ANY]
    return ordered(
        body,
        args,
        [pltpu.HBM((features, 2 * half), F32), pltpu.HBM((2 * half, features), F32), jax.ShapeDtypeStruct((8, 128), F32)],
        name,
        4.0 * len(blocks),
        spaces=spaces,
        out_spaces=[pl.ANY, pl.ANY, VMEM],
        scratch=[
            VMEM((tokens, width), BF16),
            VMEM((tokens, width), BF16),
            VMEM((slots, up_tile, width), F32),
            VMEM((slots, down_tile, features), F32),
            pltpu.SemaphoreType.DMA((2, slots)),
        ],
        aliases=aliases,
    )


def per_device(wide, narrow, inputs, up_weight, down_weight, out_grad):
    rows = inputs.shape[0]
    half = up_weight.shape[1] // 2
    chips = wide // 2
    core = (lax.axis_index("wide") & 1).astype(jnp.int32).reshape(1)
    ordered = Ordered()

    def swap_cores(x):
        return lax.ppermute(x, "wide", [(i, i ^ 1) for i in range(wide)])

    def pass_on(x):
        return lax.ppermute(x, "narrow", [(i, (i + 1) % narrow) for i in range(narrow)])

    def across_chips(partial):
        hop = 1
        while True:
            peer = lax.ppermute(partial, "wide", [(i, i ^ (2 * hop)) for i in range(wide)])
            hop *= 2
            if hop >= chips:
                return partial, peer
            partial = (partial.astype(F32) + peer.astype(F32)).astype(BF16)

    def added(keep, got):
        return (keep.astype(F32) + got.astype(F32)).astype(BF16)

    tokens, grads = [inputs], [out_grad]
    for _ in range(1, narrow):
        tokens.append(pass_on(tokens[-1]))
        grads.append(pass_on(grads[-1]))

    slices = 2 if half % 256 == 0 else 1
    width = half // slices

    def send_acts(own_peer):
        mine = gelu(ordered, *own_peer)
        return mine, swap_cores(mine)

    up_other, give_h = first_product(ordered, core, True, inputs, up_weight, 1, "give_hidden")
    got_h = swap_cores(give_h)
    up_mine, keep_h = first_product(ordered, core, False, inputs, up_weight, 1, "keep_hidden")
    own_h, peer_h = across_chips(added(keep_h, got_h))
    down_other, give_g = first_product(ordered, core, True, out_grad, down_weight, 0, "give_grad")
    got_g = swap_cores(give_g)
    down_mine, keep_g = first_product(ordered, core, False, out_grad, down_weight, 0, "keep_grad")
    own_g, peer_g = across_chips(added(keep_g, got_g))
    pending = ((own_h, own_g), (peer_h, peer_g))

    acts = []
    kept = share = None
    for step in range(1, narrow):
        give = product(ordered, tokens[step], grads[step], up_other, down_other, "give")
        got = swap_cores(give)
        if step > 1:
            acts.append([send_acts(pending)])
        keep = product(ordered, tokens[step], grads[step], up_mine, down_mine, "keep")
        if step < narrow - 1:
            sent = across_chips(added(keep, got))
        else:
            sent = [
                across_chips(added(keep[:, :, i * width : (i + 1) * width], got[:, :, i * width : (i + 1) * width]))
                for i in range(slices)
            ]
        if step == 1:
            acts.append([send_acts(pending)])
        elif step == 2:
            pass
        pending = sent
        if step == 3:
            kept, share = input_product(ordered, acts[:2], up_mine, up_other, None)
            share = pass_on(share)
        elif step > 3:
            share = pass_on(input_product(ordered, [acts[step - 2]], up_mine, up_other, share)[0])
    turned, all_grads = collect(ordered, tokens, grads)
    if narrow > 2:
        share = pass_on(input_product(ordered, [acts[narrow - 2]], up_mine, up_other, share)[0])

    scale = (rows * narrow) ** -0.5

    def block(other, i):
        earlier = [(chunk[0][other], i * width) for chunk in acts]
        return (other, i * width, earlier + [(last[i][other], 0)])

    last = []
    result = None
    for i in range(slices):
        last.append(send_acts(pending[i]))
        blocks = [block(0, i)] if i == 0 else [block(1, i - 1), block(0, i)]
        result = weight_grads(ordered, core, blocks, turned, all_grads, half, scale, result, "weight_grads")[:2]
    share = pass_on(input_product(ordered, [last], up_mine, up_other, share)[0])
    result = weight_grads(ordered, core, [block(1, slices - 1)], turned, all_grads, half, scale, result, "weight_grads")[:2]
    return (kept.astype(F32) + share.astype(F32)).astype(BF16), *result


def solution(mesh):
    placed = (
        P(("groups", "narrow"), "wide"),
        P("wide", "narrow"),
        P("narrow", "wide"),
        P(("groups", "narrow"), "wide"),
    )
    return jax.shard_map(
        functools.partial(per_device, mesh.shape["wide"], mesh.shape["narrow"]),
        mesh=mesh,
        in_specs=placed,
        out_specs=(
            P(("groups", "narrow"), "wide"),
            P(("groups", "wide"), "narrow"),
            P(("groups", "narrow"), "wide"),
        ),
        check_vma=False,
    )
```

```python
import functools

import jax
import jax.numpy as jnp
from jax import lax
from jax.experimental import pallas as pl
from jax.experimental.pallas import tpu as pltpu
from jax.sharding import PartitionSpec as P

F32, BF16 = jnp.float32, jnp.bfloat16
MIB = 1 << 20
VMEM = pltpu.VMEM
NN = (((1,), (0,)), ((), ()))
NT = (((1,), (1,)), ((), ()))
TN = (((0,), (0,)), ((), ()))


def dot(a, b, dims):
    return lax.dot_general(a, b, dims, preferred_element_type=F32)


def in_vmem(x):
    return pltpu.with_memory_space_constraint(x, VMEM)


def in_hbm(x):
    return pltpu.with_memory_space_constraint(x, pltpu.HBM)


def tile_of(extent, largest=512):
    return next(t for t in (768, 512, 384, 256, 128) if t <= largest and extent % t == 0)


class Ordered:
    def __init__(self):
        self.last = None

    def __call__(self, body, args, outs, name, micros, limit=16, spaces=None, out_spaces=None, scratch=(), aliases=None, after=()):
        args = list(args)
        spaces = spaces or [None] * len(args)
        specs = [
            pl.BlockSpec(memory_space=pltpu.SMEM if a.dtype == jnp.int32 else space or VMEM) for a, space in zip(args, spaces)
        ]
        count = len(args)
        for waited in (*after, *([] if self.last is None else [self.last])):
            args.append(waited)
            specs.append(pl.BlockSpec(memory_space=pl.ANY))
        extra = len(args) - count

        def kernel(*refs):
            body(*refs[:count], *refs[count + extra :])

        result = pl.pallas_call(
            kernel,
            out_shape=outs,
            in_specs=specs,
            out_specs=[pl.BlockSpec(memory_space=s) for s in out_spaces or [VMEM] * len(outs)],
            scratch_shapes=scratch,
            input_output_aliases=aliases or {},
            compiler_params=pltpu.CompilerParams(vmem_limit_bytes=limit * MIB),
            cost_estimate=pl.CostEstimate(flops=int(micros * 4e9), bytes_accessed=0, transcendentals=0),
            name=name,
        )(*args)
        self.last = result[-1]
        return result


def first_product(ordered, core, other, chunk, weight, units_dim, name, after=()):
    _, rows, features = chunk.shape
    half = weight.shape[units_dim] // 2
    tile = tile_of(half)
    pieces = half // tile

    def body(core_ref, chunk_ref, weight_hbm, weight_ref, out_ref, sems):
        side = 1 - core_ref[0] if other else core_ref[0]
        copies = []
        for i in range(pieces):
            units = pl.ds(pl.multiple_of(side * half + i * tile, tile), tile)
            part = pl.ds(i * tile, tile)
            at = (lambda u: (slice(None), u)) if units_dim else (lambda u: (u, slice(None)))
            copies.append(pltpu.make_async_copy(weight_hbm.at[at(units)], weight_ref.at[at(part)], sems.at[i]))
        for copy in copies:
            copy.start()
        for i, copy in enumerate(copies):
            part = slice(i * tile, (i + 1) * tile)
            copy.wait()
            if units_dim:
                out_ref[:, part] = dot(chunk_ref[0], weight_ref[:, part], NN).astype(BF16)
            else:
                out_ref[:, part] = dot(chunk_ref[1], weight_ref[part, :], NT).astype(BF16)

    shape = (features, half) if units_dim else (half, features)
    return ordered(
        body,
        (core, chunk, in_hbm(weight)),
        [VMEM(shape, BF16), jax.ShapeDtypeStruct((rows, half), BF16)],
        name,
        2.5,
        spaces=[None, None, pl.ANY],
        scratch=[pltpu.SemaphoreType.DMA((pieces,))],
        after=after,
    )


def product(ordered, chunk, up_half, down_half, name, after=()):
    _, rows, features = chunk.shape
    half = up_half.shape[1]
    tile = tile_of(half)

    def body(chunk_ref, up_ref, down_ref, out_ref):
        for start in range(0, half, tile):
            part = slice(start, start + tile)
            out_ref[0, :, part] = dot(chunk_ref[0], up_ref[:, part], NN).astype(BF16)
            out_ref[1, :, part] = dot(chunk_ref[1], down_ref[part, :], NT).astype(BF16)

    args = (chunk, in_vmem(up_half), in_vmem(down_half))
    return ordered(body, args, [jax.ShapeDtypeStruct((2, rows, half), BF16)], name, 2.4, after=after)[0]


def input_product(ordered, mine, other, up_mine, up_other, chunks, micros, returned=()):
    rows = mine[0].shape[1] // chunks
    features = up_mine.shape[0]
    tile = tile_of(features)
    widths = [a.shape[2] for a in mine]

    def body(up_mine_ref, up_other_ref, *refs):
        returned_refs, out_refs = refs[2 * len(widths) :][: len(returned)], refs[-chunks:]
        if returned:
            total = returned_refs[0][...].astype(F32)
            for ref in returned_refs[1:]:
                total = total + ref[...].astype(F32)
            refs[-chunks - 1][...] = total
        for start in range(0, features, tile):
            part = slice(start, start + tile)
            share = None
            for side, up_ref in enumerate((up_mine_ref, up_other_ref)):
                low = 0
                for i, width in enumerate(widths):
                    term = dot(refs[side * len(widths) + i][0], up_ref[part, low : low + width], NT)
                    share = term if share is None else share + term
                    low += width
            for c, out_ref in enumerate(out_refs):
                out_ref[:, part] = share[c * rows : (c + 1) * rows].astype(BF16)

    args = (in_vmem(up_mine), in_vmem(up_other), *mine, *other, *returned)
    outs = [jax.ShapeDtypeStruct((rows, features), F32)] if returned else []
    return ordered(body, args, outs + [jax.ShapeDtypeStruct((rows, features), BF16)] * chunks, "input_product", micros)


def gelu(ordered, sums, after=()):
    flat, places = [], []
    for own, peer in sums:
        where = []
        for side in (own, peer):
            where += [(len(flat) + i, None) for i in (0, 1)] if len(side) == 2 else [(len(flat), i) for i in (0, 1)]
            flat += side
        places.append(where)
    rows, units = flat[0].shape[-2:]

    def body(*refs):
        out_ref = refs[-1]
        for chunk, where in enumerate(places):
            at = slice(chunk * rows, (chunk + 1) * rows)
            own_h, own_g, peer_h, peer_g = [(refs[r][...] if i is None else refs[r][i]).astype(F32) for r, i in where]
            hidden, grad_hidden = own_h + peer_h, own_g + peer_g
            cdf = 0.5 * (1.0 + lax.erf(hidden * 0.7071067811865476))
            pdf = jnp.exp(-0.5 * hidden * hidden) * 0.3989422804014327
            out_ref[0, at] = (grad_hidden * (cdf + hidden * pdf)).astype(BF16)
            out_ref[1, at] = (hidden * cdf).astype(BF16)

    out = jax.ShapeDtypeStruct((2, rows * len(sums), units), BF16)
    return ordered(body, flat, [out], "gelu", 0.1, after=after)[0]


def collect(ordered, chunks, after):
    count = len(chunks)
    _, rows, features = chunks[0].shape
    tile = tile_of(features, 256)

    def body(*refs):
        turned_ref, grads_ref, scratch = refs[count:]
        for i in range(count):
            scratch[i * rows : (i + 1) * rows, :] = refs[i][0]
            grads_ref[i * rows : (i + 1) * rows, :] = refs[i][1]
        for start in range(0, features, tile):
            turned_ref[start : start + tile, :] = scratch[:, start : start + tile].T

    outs = [VMEM((features, rows * count), BF16), VMEM((rows * count, features), BF16)]
    return ordered(body, chunks, outs, "collect", 0.1, scratch=[VMEM((rows * count, features), BF16)], after=after)


def weight_grads(ordered, core, blocks, turned, all_grads, half, scale, before, name):
    features, tokens = turned.shape
    width = min(a.shape[2] for a, _ in blocks[0][2])
    up_tile, down_tile = tile_of(features), tile_of(width, 256)
    up_steps, down_steps = features // up_tile, width // down_tile
    slots = 3
    flat = [a for block in blocks for a, _ in block[2]]

    def body(core_ref, turned_ref, grads_ref, *refs):
        up_hbm, down_hbm, done_ref, act_g, act_v, up_stage, down_stage, sems = refs[-8:]
        done_ref[...] = jnp.zeros_like(done_ref)
        busy = {}

        def send(kind, index, value, stage, target):
            slot = index % slots
            if (kind, slot) in busy:
                busy[kind, slot].wait()
            stage[slot] = value * scale
            copy = pltpu.make_async_copy(stage.at[slot], target, sems.at[kind, slot])
            copy.start()
            busy[kind, slot] = copy

        for b, (other, first, acts) in enumerate(blocks):
            side = 1 - core_ref[0] if other else core_ref[0]
            base = side * half + first
            row = 0
            for i, (array, column) in enumerate(acts):
                ref, rows = refs[b * len(acts) + i], slice(row, row + array.shape[1])
                act_g[rows, :] = ref[0, :, column : column + width]
                act_v[rows, :] = ref[1, :, column : column + width]
                row += array.shape[1]
            for step in range(max(up_steps, down_steps)):
                if step < up_steps:
                    part = slice(step * up_tile, (step + 1) * up_tile)
                    value = dot(turned_ref[part, :], act_g[...], NN)
                    target = up_hbm.at[pl.ds(step * up_tile, up_tile), pl.ds(pl.multiple_of(base, 128), width)]
                    send(0, b * up_steps + step, value, up_stage, target)
                if step < down_steps:
                    part = slice(step * down_tile, (step + 1) * down_tile)
                    value = dot(act_v[:, part], grads_ref[...], TN)
                    target = down_hbm.at[pl.ds(pl.multiple_of(base + step * down_tile, 128), down_tile), :]
                    send(1, b * down_steps + step, value, down_stage, target)
        for copy in busy.values():
            copy.wait()

    args = [core, turned, all_grads, *flat]
    spaces = [None] * len(args)
    aliases = {}
    if before is not None:
        aliases = {len(args): 0, len(args) + 1: 1}
        args += [in_hbm(a) for a in before]
        spaces += [pl.ANY, pl.ANY]
    return ordered(
        body,
        args,
        [pltpu.HBM((features, 2 * half), F32), pltpu.HBM((2 * half, features), F32), jax.ShapeDtypeStruct((8, 128), F32)],
        name,
        4.0 * len(blocks),
        spaces=spaces,
        out_spaces=[pl.ANY, pl.ANY, VMEM],
        scratch=[
            VMEM((tokens, width), BF16),
            VMEM((tokens, width), BF16),
            VMEM((slots, up_tile, width), F32),
            VMEM((slots, down_tile, features), F32),
            pltpu.SemaphoreType.DMA((2, slots)),
        ],
        aliases=aliases,
    )


def per_device(wide, narrow, inputs, up_weight, down_weight, out_grad):
    rows = inputs.shape[0]
    half = up_weight.shape[1] // 2
    chips = wide // 2
    core = (lax.axis_index("wide") & 1).astype(jnp.int32).reshape(1)
    ordered = Ordered()

    def swap_cores(x):
        return lax.ppermute(x, "wide", [(i, i ^ 1) for i in range(wide)])

    def shift(x, places):
        return lax.ppermute(x, "narrow", [(i, (i + places) % narrow) for i in range(narrow)])

    def across_chips(keep, got):
        partial = (keep.astype(F32) + got.astype(F32)).astype(BF16)
        hop = 1
        while True:
            peer = lax.ppermute(partial, "wide", [(i, i ^ (2 * hop)) for i in range(wide)])
            hop *= 2
            if hop >= chips:
                return partial, peer
            partial = (partial.astype(F32) + peer.astype(F32)).astype(BF16)

    offsets = sorted(range(narrow // 2 - narrow + 1, narrow // 2 + 1), key=lambda places: (abs(places), -places))
    chunks = {0: jnp.stack([inputs, out_grad])}

    up_other, give_h = first_product(ordered, core, True, chunks[0], up_weight, 1, "give_hidden")
    got_h = swap_cores(give_h)
    up_mine, keep_h = first_product(ordered, core, False, chunks[0], up_weight, 1, "keep_hidden")
    own_h, peer_h = across_chips(keep_h, got_h)
    down_other, give_g = first_product(ordered, core, True, chunks[0], down_weight, 0, "give_grad", after=[own_h])
    got_g = swap_cores(give_g)
    down_mine, keep_g = first_product(ordered, core, False, chunks[0], down_weight, 0, "keep_grad")
    own_g, peer_g = across_chips(keep_g, got_g)

    slices = 2 if half % 256 == 0 else 1
    width = half // slices
    early = [((own_h, own_g), (peer_h, peer_g))]
    late = None
    waiting = [peer_h, peer_g]
    for offset in offsets[1:]:
        places = 1 if offset > 0 else -1
        chunk = chunks[offset] = shift(chunks[offset - places], places)
        give = product(ordered, chunk, up_other, down_other, "give", after=[waiting[0], early[-1][0][-1]])
        waiting = waiting[1:]
        got = swap_cores(give)
        keep = product(ordered, chunk, up_mine, down_mine, "keep")
        if offset != offsets[-1]:
            own, peer = across_chips(keep, got)
            early.append(((own,), (peer,)))
            waiting.append(peer)
        else:
            parts = [slice(i * width, (i + 1) * width) for i in range(slices)]
            late = [[(x,) for x in across_chips(keep[:, :, part], got[:, :, part])] for part in parts]

    turned, all_grads = collect(ordered, [chunks[offset] for offset in offsets], [own for (own,), _ in late])
    mine = gelu(ordered, early)
    other = swap_cores(mine)
    shares = input_product(ordered, [mine], [other], up_mine, up_other, narrow - 1, 0.1)
    shares = [share if offset == 0 else shift(share, -offset) for offset, share in zip(offsets, shares)]

    scale = (rows * narrow) ** -0.5
    late_acts = ([], [])

    def block(side, i):
        return (side, i * width, [((mine, other)[side], i * width), (late_acts[side][i], 0)])

    def grads(blocks, before):
        return weight_grads(ordered, core, blocks, turned, all_grads, half, scale, before, "weight_grads")[:2]

    result = None
    for i in range(slices):
        late_acts[0].append(gelu(ordered, [late[i]]))
        late_acts[1].append(swap_cores(late_acts[0][i]))
        if i < slices - 1:
            result = grads([block(0, i)], result)
    for i in range(slices - 1):
        result = grads([block(1, i)], result)
    so_far, share = input_product(ordered, *late_acts, up_mine, up_other, 1, 3.0, shares)
    share = shift(share, -offsets[-1])
    result = grads([block(0, slices - 1), block(1, slices - 1)], result)
    return (so_far + share.astype(F32)).astype(BF16), *result


def solution(mesh):
    placed = (
        P(("groups", "narrow"), "wide"),
        P("wide", "narrow"),
        P("narrow", "wide"),
        P(("groups", "narrow"), "wide"),
    )
    return jax.shard_map(
        functools.partial(per_device, mesh.shape["wide"], mesh.shape["narrow"]),
        mesh=mesh,
        in_specs=placed,
        out_specs=(
            P(("groups", "narrow"), "wide"),
            P(("groups", "wide"), "narrow"),
            P(("groups", "narrow"), "wide"),
        ),
        check_vma=False,
    )
```

```python
import functools

import jax
import jax.numpy as jnp
from jax import lax
from jax.experimental import pallas as pl
from jax.experimental.pallas import tpu as pltpu
from jax.sharding import PartitionSpec as P

F32, BF16 = jnp.float32, jnp.bfloat16
MIB = 1 << 20
VMEM = pltpu.VMEM
NN = (((1,), (0,)), ((), ()))
NT = (((1,), (1,)), ((), ()))
TN = (((0,), (0,)), ((), ()))


def dot(a, b, dims):
    return lax.dot_general(a, b, dims, preferred_element_type=F32)


def in_vmem(x):
    return pltpu.with_memory_space_constraint(x, VMEM)


def in_hbm(x):
    return pltpu.with_memory_space_constraint(x, pltpu.HBM)


def tile_of(extent, largest=512):
    return next(t for t in (768, 512, 384, 256, 128) if t <= largest and extent % t == 0)


class Ordered:
    def __init__(self):
        self.last = None

    def __call__(self, body, args, outs, name, micros, limit=16, spaces=None, out_spaces=None, scratch=(), aliases=None, after=()):
        args = list(args)
        spaces = spaces or [None] * len(args)
        specs = [
            pl.BlockSpec(memory_space=pltpu.SMEM if a.dtype == jnp.int32 else space or VMEM) for a, space in zip(args, spaces)
        ]
        count = len(args)
        for waited in (*after, *([] if self.last is None else [self.last])):
            args.append(waited)
            specs.append(pl.BlockSpec(memory_space=pl.ANY))
        extra = len(args) - count

        def kernel(*refs):
            body(*refs[:count], *refs[count + extra :])

        result = pl.pallas_call(
            kernel,
            out_shape=outs,
            in_specs=specs,
            out_specs=[pl.BlockSpec(memory_space=s) for s in out_spaces or [VMEM] * len(outs)],
            scratch_shapes=scratch,
            input_output_aliases=aliases or {},
            compiler_params=pltpu.CompilerParams(vmem_limit_bytes=limit * MIB),
            cost_estimate=pl.CostEstimate(flops=int(micros * 4e9), bytes_accessed=0, transcendentals=0),
            name=name,
        )(*args)
        self.last = result[-1]
        return result


def first_product(ordered, core, other, chunk, up_weight, down_weight, name):
    _, rows, features = chunk.shape
    half = up_weight.shape[1] // 2
    tile = tile_of(half)
    pieces = half // tile

    def body(core_ref, chunk_ref, up_hbm, down_hbm, up_ref, down_ref, *refs):
        out_ref, sems = refs[-2:]
        side = 1 - core_ref[0] if other else core_ref[0]
        copies = []
        for i in range(pieces):
            units = pl.ds(pl.multiple_of(side * half + i * tile, tile), tile)
            part = pl.ds(i * tile, tile)
            copies.append(pltpu.make_async_copy(up_hbm.at[:, units], up_ref.at[:, part], sems.at[0, i]))
            copies.append(pltpu.make_async_copy(down_hbm.at[units, :], down_ref.at[part, :], sems.at[1, i]))
        for copy in copies:
            copy.start()
        if other:
            refs[0][...] = chunk_ref[...]
        for i in range(pieces):
            part = slice(i * tile, (i + 1) * tile)
            copies[2 * i].wait()
            out_ref[0, :, part] = dot(chunk_ref[0], up_ref[:, part], NN).astype(BF16)
            copies[2 * i + 1].wait()
            out_ref[1, :, part] = dot(chunk_ref[1], down_ref[part, :], NT).astype(BF16)

    outs = [VMEM((features, half), BF16), VMEM((half, features), BF16)]
    outs += [jax.ShapeDtypeStruct(chunk.shape, BF16)] if other else []
    return ordered(
        body,
        (core, chunk, in_hbm(up_weight), in_hbm(down_weight)),
        outs + [jax.ShapeDtypeStruct((2, rows, half), BF16)],
        name,
        4.5,
        spaces=[None, None, pl.ANY, pl.ANY],
        scratch=[pltpu.SemaphoreType.DMA((2, pieces))],
    )


def product(ordered, chunk, up_half, down_half, name, after=()):
    _, rows, features = chunk.shape
    half = up_half.shape[1]
    tile = tile_of(half)

    def body(chunk_ref, up_ref, down_ref, out_ref):
        for start in range(0, half, tile):
            part = slice(start, start + tile)
            out_ref[0, :, part] = dot(chunk_ref[0], up_ref[:, part], NN).astype(BF16)
            out_ref[1, :, part] = dot(chunk_ref[1], down_ref[part, :], NT).astype(BF16)

    args = (chunk, in_vmem(up_half), in_vmem(down_half))
    return ordered(body, args, [jax.ShapeDtypeStruct((2, rows, half), BF16)], name, 2.4, after=after)[0]


def product_terms(acts, up_refs, part, low):
    terms = [dot(act, up_ref[part, low : low + act.shape[1]], NT) for act, up_ref in zip(acts, up_refs)]
    return terms[0] + terms[1]


def input_product(ordered, mine, other, up_mine, up_other, low, chunks, micros, partial=None, returned=()):
    rows = mine.shape[1] // chunks
    features = up_mine.shape[0]
    tile = tile_of(features)

    def body(up_mine_ref, up_other_ref, mine_ref, other_ref, *refs):
        returned_refs, out_refs = refs[: len(returned)], refs[-chunks:]
        if returned:
            total = returned_refs[0][...].astype(F32)
            for ref in returned_refs[1:]:
                total = total + ref[...].astype(F32)
            refs[-chunks - 1][...] = total
        for start in range(0, features, tile):
            part = slice(start, start + tile)
            share = product_terms((mine_ref[0], other_ref[0]), (up_mine_ref, up_other_ref), part, low)
            if partial is not None:
                share = share + refs[len(returned)][:, part]
            for c, out_ref in enumerate(out_refs):
                out_ref[:, part] = share[c * rows : (c + 1) * rows].astype(BF16)

    args = (in_vmem(up_mine), in_vmem(up_other), mine, other, *returned, *([] if partial is None else [partial]))
    outs = [jax.ShapeDtypeStruct((rows, features), F32)] if returned else []
    return ordered(body, args, outs + [jax.ShapeDtypeStruct((rows, features), BF16)] * chunks, "input_product", micros)


def gelu(ordered, sums, after=()):
    flat = [a for pair in sums for a in pair]
    _, rows, units = flat[0].shape

    def body(*refs):
        out_ref = refs[-1]
        for chunk in range(len(sums)):
            at = slice(chunk * rows, (chunk + 1) * rows)
            own_h, own_g, peer_h, peer_g = [refs[2 * chunk + side][i].astype(F32) for side in (0, 1) for i in (0, 1)]
            hidden, grad_hidden = own_h + peer_h, own_g + peer_g
            cdf = 0.5 * (1.0 + lax.erf(hidden * 0.7071067811865476))
            pdf = jnp.exp(-0.5 * hidden * hidden) * 0.3989422804014327
            out_ref[0, at] = (grad_hidden * (cdf + hidden * pdf)).astype(BF16)
            out_ref[1, at] = (hidden * cdf).astype(BF16)

    out = jax.ShapeDtypeStruct((2, rows * len(sums), units), BF16)
    return ordered(body, flat, [out], "gelu", 0.1, after=after)[0]


def collect(ordered, chunks, after):
    count = len(chunks)
    _, rows, features = chunks[0].shape
    tile = tile_of(features, 256)

    def body(*refs):
        turned_ref, grads_ref, scratch = refs[count:]
        for i in range(count):
            scratch[i * rows : (i + 1) * rows, :] = refs[i][0]
            grads_ref[i * rows : (i + 1) * rows, :] = refs[i][1]
        for start in range(0, features, tile):
            turned_ref[start : start + tile, :] = scratch[:, start : start + tile].T

    outs = [VMEM((features, rows * count), BF16), VMEM((rows * count, features), BF16)]
    return ordered(body, chunks, outs, "collect", 0.1, scratch=[VMEM((rows * count, features), BF16)], after=after)


def weight_grads(ordered, core, blocks, turned, all_grads, half, scale, before, name, share=None):
    features, tokens = turned.shape
    width = min(a.shape[2] for a, _ in blocks[0][2])
    up_tile, down_tile = tile_of(features), tile_of(width, 256)
    up_steps, down_steps = features // up_tile, width // down_tile
    slots = 3
    flat = [a for block in blocks for a, _ in block[2]]

    def body(core_ref, turned_ref, grads_ref, *refs):
        up_hbm, down_hbm = refs[outs_at : outs_at + 2]
        done_ref, act_g, act_v, up_stage, down_stage, sems = refs[-6:]
        done_ref[...] = jnp.zeros_like(done_ref)
        busy = {}

        def send(kind, index, value, stage, target):
            slot = index % slots
            if (kind, slot) in busy:
                busy[kind, slot].wait()
            stage[slot] = value * scale
            copy = pltpu.make_async_copy(stage.at[slot], target, sems.at[kind, slot])
            copy.start()
            busy[kind, slot] = copy

        for b, (other, first, acts) in enumerate(blocks):
            side = 1 - core_ref[0] if other else core_ref[0]
            base = side * half + first
            row = 0
            for i, (array, column) in enumerate(acts):
                ref, rows = refs[b * len(acts) + i], slice(row, row + array.shape[1])
                act_g[rows, :] = ref[0, :, column : column + width]
                act_v[rows, :] = ref[1, :, column : column + width]
                row += array.shape[1]
            for step in range(max(up_steps, down_steps)):
                if step < up_steps:
                    part = slice(step * up_tile, (step + 1) * up_tile)
                    value = dot(turned_ref[part, :], act_g[...], NN)
                    target = up_hbm.at[pl.ds(step * up_tile, up_tile), pl.ds(pl.multiple_of(base, 128), width)]
                    send(0, b * up_steps + step, value, up_stage, target)
                if step < down_steps:
                    part = slice(step * down_tile, (step + 1) * down_tile)
                    value = dot(act_v[:, part], grads_ref[...], TN)
                    target = down_hbm.at[pl.ds(pl.multiple_of(base + step * down_tile, 128), down_tile), :]
                    send(1, b * down_steps + step, value, down_stage, target)
                if share is not None and b == 0 and step < up_steps:
                    part = slice(step * up_tile, (step + 1) * up_tile)
                    mine_ref, other_ref, up_mine_ref, up_other_ref = refs[len(flat) : len(flat) + 4]
                    value = product_terms((mine_ref[0], other_ref[0]), (up_mine_ref, up_other_ref), part, 0)
                    refs[outs_at + 2][:, part] = value.astype(share[4])
        for copy in busy.values():
            copy.wait()

    args = [core, turned, all_grads, *flat]
    outs = [pltpu.HBM((features, 2 * half), F32), pltpu.HBM((2 * half, features), F32)]
    if share is not None:
        args += [*share[:2], in_vmem(share[2]), in_vmem(share[3])]
        outs.append(jax.ShapeDtypeStruct((share[0].shape[1], features), share[4]))
    spaces = [None] * len(args)
    outs_at = len(args) - 3 + (0 if before is None else 2)
    aliases = {}
    if before is not None:
        aliases = {len(args): 0, len(args) + 1: 1}
        args += [in_hbm(a) for a in before]
        spaces += [pl.ANY, pl.ANY]
    return ordered(
        body,
        args,
        [*outs, jax.ShapeDtypeStruct((8, 128), F32)],
        name,
        4.0 * len(blocks),
        spaces=spaces,
        out_spaces=[pl.ANY, pl.ANY] + [VMEM] * (len(outs) - 1),
        scratch=[
            VMEM((tokens, width), BF16),
            VMEM((tokens, width), BF16),
            VMEM((slots, up_tile, width), F32),
            VMEM((slots, down_tile, features), F32),
            pltpu.SemaphoreType.DMA((2, slots)),
        ],
        aliases=aliases,
    )


def per_device(wide, narrow, inputs, up_weight, down_weight, out_grad):
    rows = inputs.shape[0]
    half = up_weight.shape[1] // 2
    chips = wide // 2
    core = (lax.axis_index("wide") & 1).astype(jnp.int32).reshape(1)
    ordered = Ordered()

    def swap_cores(x):
        return lax.ppermute(x, "wide", [(i, i ^ 1) for i in range(wide)])

    def shift(x, places):
        return lax.ppermute(x, "narrow", [(i, (i + places) % narrow) for i in range(narrow)])

    def across_chips(keep, got):
        partial = (keep.astype(F32) + got.astype(F32)).astype(BF16)
        hop = 1
        while True:
            peer = lax.ppermute(partial, "wide", [(i, i ^ (2 * hop)) for i in range(wide)])
            hop *= 2
            if hop >= chips:
                return partial, peer
            partial = (partial.astype(F32) + peer.astype(F32)).astype(BF16)

    offsets = sorted(range(narrow // 2 - narrow + 1, narrow // 2 + 1), key=lambda places: (abs(places), -places))
    chunks = {0: jnp.stack([inputs, out_grad])}

    up_other, down_other, sent_back, give = first_product(ordered, core, True, chunks[0], up_weight, down_weight, "give_first")
    got = swap_cores(give)
    up_mine, down_mine, keep = first_product(ordered, core, False, chunks[0], up_weight, down_weight, "keep_first")
    sums = [across_chips(keep, got)]

    def acts_of(sums):
        mine = gelu(ordered, sums)
        return mine, swap_cores(mine)

    slices = 2 if half % 256 == 0 else 1
    width = half // slices
    for offset in offsets[1:]:
        places = 1 if offset > 0 else -1
        chunk = chunks[offset] = shift(sent_back if offset == -1 else chunks[offset - places], places)
        give = product(ordered, chunk, up_other, down_other, "give", after=[sums[-1][0]] + [peer for _, peer in sums[-2:-1]])
        got = swap_cores(give)
        if offset == offsets[-1]:
            early = acts_of(sums[:-1])
        keep = product(ordered, chunk, up_mine, down_mine, "keep")
        if offset != offsets[-1]:
            sums.append(across_chips(keep, got))
        else:
            parts = [slice(i * width, (i + 1) * width) for i in range(slices)]
            late = [across_chips(keep[:, :, part], got[:, :, part]) for part in parts]

    turned, all_grads = collect(ordered, [chunks[offset] for offset in offsets], [own for own, _ in late])
    shares = input_product(ordered, *early, up_mine, up_other, 0, narrow - 2, 0.1)
    shares = [share if offset == 0 else shift(share, -offset) for offset, share in zip(offsets, shares)]
    middle = acts_of(sums[-1:])

    scale = (rows * narrow) ** -0.5
    late_acts = []

    def grads(places, before, share):
        blocks = [
            (side, i * width, [(early[side], i * width), (middle[side], i * width), (late_acts[i][side], 0)])
            for side, i in places
        ]
        return weight_grads(ordered, core, blocks, turned, all_grads, half, scale, before, "weight_grads", share)

    late_acts.append(acts_of(late[:1]))
    up_grad, down_grad, share, _ = grads([(0, 0)], None, (*middle, up_mine, up_other, BF16))
    shares.append(shift(share, -offsets[-2]))
    partial = None
    if slices > 1:
        late_acts.append(acts_of(late[1:]))
        up_grad, down_grad, partial, _ = grads([(1, 0)], (up_grad, down_grad), (*late_acts[0], up_mine, up_other, F32))
    low = width * (slices - 1)
    so_far, share = input_product(ordered, *late_acts[-1], up_mine, up_other, low, 1, 3.0, partial, shares)
    share = shift(share, -offsets[-1])
    last = [(0, 1), (1, 1)] if slices > 1 else [(1, 0)]
    up_grad, down_grad, _ = grads(last, (up_grad, down_grad), None)
    return (so_far + share.astype(F32)).astype(BF16), up_grad, down_grad


def solution(mesh):
    placed = (
        P(("groups", "narrow"), "wide"),
        P("wide", "narrow"),
        P("narrow", "wide"),
        P(("groups", "narrow"), "wide"),
    )
    return jax.shard_map(
        functools.partial(per_device, mesh.shape["wide"], mesh.shape["narrow"]),
        mesh=mesh,
        in_specs=placed,
        out_specs=(
            P(("groups", "narrow"), "wide"),
            P(("groups", "wide"), "narrow"),
            P(("groups", "narrow"), "wide"),
        ),
        check_vma=False,
    )
```

```python
import functools

import jax
import jax.numpy as jnp
from jax import lax
from jax.experimental import pallas as pl
from jax.experimental.pallas import tpu as pltpu
from jax.sharding import PartitionSpec as P

F32, BF16 = jnp.float32, jnp.bfloat16
MIB = 1 << 20
VMEM = pltpu.VMEM
NN = (((1,), (0,)), ((), ()))
NT = (((1,), (1,)), ((), ()))
TN = (((0,), (0,)), ((), ()))


def dot(a, b, dims):
    return lax.dot_general(a, b, dims, preferred_element_type=F32)


def in_vmem(x):
    return pltpu.with_memory_space_constraint(x, VMEM)


def in_hbm(x):
    return pltpu.with_memory_space_constraint(x, pltpu.HBM)


def tile_of(extent, largest=512):
    return next(t for t in (768, 512, 384, 256, 128) if t <= largest and extent % t == 0)


class Ordered:
    def __init__(self):
        self.last = None

    def __call__(self, body, args, outs, name, micros, limit=16, spaces=None, out_spaces=None, scratch=(), aliases=None, after=()):
        args = list(args)
        spaces = spaces or [None] * len(args)
        specs = [
            pl.BlockSpec(memory_space=pltpu.SMEM if a.dtype == jnp.int32 else space or VMEM) for a, space in zip(args, spaces)
        ]
        count = len(args)
        for waited in (*after, *([] if self.last is None else [self.last])):
            args.append(waited)
            specs.append(pl.BlockSpec(memory_space=pl.ANY))
        extra = len(args) - count

        def kernel(*refs):
            body(*refs[:count], *refs[count + extra :])

        result = pl.pallas_call(
            kernel,
            out_shape=outs,
            in_specs=specs,
            out_specs=[pl.BlockSpec(memory_space=s) for s in out_spaces or [VMEM] * len(outs)],
            scratch_shapes=scratch,
            input_output_aliases=aliases or {},
            compiler_params=pltpu.CompilerParams(vmem_limit_bytes=limit * MIB),
            cost_estimate=pl.CostEstimate(flops=int(micros * 4e9), bytes_accessed=0, transcendentals=0),
            name=name,
        )(*args)
        self.last = result[-1]
        return result


def first_product(ordered, core, other, chunk, up_weight, down_weight, name):
    _, rows, features = chunk.shape
    half = up_weight.shape[1] // 2
    tile = tile_of(half)
    pieces = half // tile

    def body(core_ref, chunk_ref, up_hbm, down_hbm, up_ref, down_ref, *refs):
        out_ref, sems = refs[-2:]
        side = 1 - core_ref[0] if other else core_ref[0]
        copies = []
        for i in range(pieces):
            units = pl.ds(pl.multiple_of(side * half + i * tile, tile), tile)
            part = pl.ds(i * tile, tile)
            copies.append(pltpu.make_async_copy(up_hbm.at[:, units], up_ref.at[:, part], sems.at[0, i]))
            copies.append(pltpu.make_async_copy(down_hbm.at[units, :], down_ref.at[part, :], sems.at[1, i]))
        for copy in copies:
            copy.start()
        if not other:
            refs[0][...] = chunk_ref[...]
        for i in range(pieces):
            part = slice(i * tile, (i + 1) * tile)
            copies[2 * i].wait()
            out_ref[0, :, part] = dot(chunk_ref[0], up_ref[:, part], NN).astype(BF16)
            copies[2 * i + 1].wait()
            out_ref[1, :, part] = dot(chunk_ref[1], down_ref[part, :], NT).astype(BF16)

    outs = [VMEM((features, half), BF16), VMEM((half, features), BF16)]
    outs += [] if other else [jax.ShapeDtypeStruct(chunk.shape, BF16)]
    return ordered(
        body,
        (core, chunk, in_hbm(up_weight), in_hbm(down_weight)),
        outs + [jax.ShapeDtypeStruct((2, rows, half), BF16)],
        name,
        4.5,
        spaces=[None, None, pl.ANY, pl.ANY],
        scratch=[pltpu.SemaphoreType.DMA((2, pieces))],
    )


def product(ordered, chunk, up_half, down_half, name, after=()):
    _, rows, features = chunk.shape
    half = up_half.shape[1]
    tile = tile_of(half)

    def body(chunk_ref, up_ref, down_ref, out_ref):
        for start in range(0, half, tile):
            part = slice(start, start + tile)
            out_ref[0, :, part] = dot(chunk_ref[0], up_ref[:, part], NN).astype(BF16)
            out_ref[1, :, part] = dot(chunk_ref[1], down_ref[part, :], NT).astype(BF16)

    args = (chunk, in_vmem(up_half), in_vmem(down_half))
    return ordered(body, args, [jax.ShapeDtypeStruct((2, rows, half), BF16)], name, 2.4, after=after)[0]


def product_terms(acts, up_refs, part, low):
    terms = [dot(act, up_ref[part, low : low + act.shape[1]], NT) for act, up_ref in zip(acts, up_refs)]
    return terms[0] + terms[1]


def input_product(ordered, rows, mine, other, up_mine, up_other, low, micros, partial=None, returned=()):
    features = up_mine.shape[0]
    tile = tile_of(features)
    count = len(mine)
    chunks = sum(a.shape[-2] for a in mine) // rows

    def body(up_mine_ref, up_other_ref, *refs):
        acts = [[r[...] if len(r.shape) == 2 else r[0] for r in part] for part in (refs[:count], refs[count : 2 * count])]
        acts = [a[0] if count == 1 else jnp.concatenate(a, axis=0) for a in acts]
        returned_refs, out_refs = refs[2 * count :][: len(returned)], refs[-chunks:]
        if returned:
            total = returned_refs[0][...].astype(F32)
            for ref in returned_refs[1:]:
                total = total + ref[...].astype(F32)
            refs[-chunks - 1][...] = total
        for start in range(0, features, tile):
            part = slice(start, start + tile)
            share = product_terms(acts, (up_mine_ref, up_other_ref), part, low)
            if partial is not None:
                share = share + refs[2 * count + len(returned)][:, part]
            for c, out_ref in enumerate(out_refs):
                out_ref[:, part] = share[c * rows : (c + 1) * rows].astype(BF16)

    args = (in_vmem(up_mine), in_vmem(up_other), *mine, *other, *returned, *([] if partial is None else [partial]))
    outs = [jax.ShapeDtypeStruct((rows, features), F32)] if returned else []
    return ordered(body, args, outs + [jax.ShapeDtypeStruct((rows, features), BF16)] * chunks, "input_product", micros)


def gelu(ordered, sums, apart=False):
    flat = [a for pair in sums for a in pair]
    _, rows, units = flat[0].shape

    def body(*refs):
        grad_ref, value_ref = refs[-2:] if apart else (refs[-1].at[0], refs[-1].at[1])
        for chunk in range(len(sums)):
            at = slice(chunk * rows, (chunk + 1) * rows)
            own_h, own_g, peer_h, peer_g = [refs[2 * chunk + side][i].astype(F32) for side in (0, 1) for i in (0, 1)]
            hidden, grad_hidden = own_h + peer_h, own_g + peer_g
            cdf = 0.5 * (1.0 + lax.erf(hidden * 0.7071067811865476))
            pdf = jnp.exp(-0.5 * hidden * hidden) * 0.3989422804014327
            grad_ref[at] = (grad_hidden * (cdf + hidden * pdf)).astype(BF16)
            value_ref[at] = (hidden * cdf).astype(BF16)

    outs = [jax.ShapeDtypeStruct((rows * len(sums), units), BF16)] * 2
    if not apart:
        outs = [jax.ShapeDtypeStruct((2, rows * len(sums), units), BF16)]
    return ordered(body, flat, outs, "gelu", 0.1)


def collect(ordered, chunks, after):
    count = len(chunks)
    _, rows, features = chunks[0].shape
    tile = tile_of(features, 256)

    def body(*refs):
        turned_ref, grads_ref, scratch = refs[count:]
        for i in range(count):
            scratch[i * rows : (i + 1) * rows, :] = refs[i][0]
            grads_ref[i * rows : (i + 1) * rows, :] = refs[i][1]
        for start in range(0, features, tile):
            turned_ref[start : start + tile, :] = scratch[:, start : start + tile].T

    outs = [VMEM((features, rows * count), BF16), VMEM((rows * count, features), BF16)]
    return ordered(body, chunks, outs, "collect", 0.1, scratch=[VMEM((rows * count, features), BF16)], after=after)


def weight_grads(ordered, core, blocks, turned, all_grads, half, scale, before, name, share=None):
    features, tokens = turned.shape
    width = min(a[0].shape[-1] for a, _ in blocks[0][2])
    up_tile, down_tile = tile_of(features), tile_of(width, 256)
    up_steps, down_steps = features // up_tile, width // down_tile
    slots = 3
    flat = [a for block in blocks for acts, _ in block[2] for a in acts]

    def body(core_ref, turned_ref, grads_ref, *refs):
        up_hbm, down_hbm = refs[outs_at : outs_at + 2]
        done_ref, act_g, act_v, up_stage, down_stage, sems = refs[-6:]
        done_ref[...] = jnp.zeros_like(done_ref)
        busy = {}

        def send(kind, index, value, stage, target):
            slot = index % slots
            if (kind, slot) in busy:
                busy[kind, slot].wait()
            stage[slot] = value * scale
            copy = pltpu.make_async_copy(stage.at[slot], target, sems.at[kind, slot])
            copy.start()
            busy[kind, slot] = copy

        left = refs[: len(flat)]
        for b, (other, first, acts) in enumerate(blocks):
            side = 1 - core_ref[0] if other else core_ref[0]
            base = side * half + first
            row = 0
            for arrays, column in acts:
                rows = slice(row, row + arrays[0].shape[-2])
                columns = slice(column, column + width)
                taken, left = left[: len(arrays)], left[len(arrays) :]
                act_g[rows, :] = taken[0][:, columns] if len(taken) == 2 else taken[0][0, :, columns]
                act_v[rows, :] = taken[1][:, columns] if len(taken) == 2 else taken[0][1, :, columns]
                row += arrays[0].shape[-2]
            for step in range(max(up_steps, down_steps)):
                if step < up_steps:
                    part = slice(step * up_tile, (step + 1) * up_tile)
                    value = dot(turned_ref[part, :], act_g[...], NN)
                    target = up_hbm.at[pl.ds(step * up_tile, up_tile), pl.ds(pl.multiple_of(base, 128), width)]
                    send(0, b * up_steps + step, value, up_stage, target)
                if step < down_steps:
                    part = slice(step * down_tile, (step + 1) * down_tile)
                    value = dot(act_v[:, part], grads_ref[...], TN)
                    target = down_hbm.at[pl.ds(pl.multiple_of(base + step * down_tile, 128), down_tile), :]
                    send(1, b * down_steps + step, value, down_stage, target)
                if share is not None and b == 0 and step < up_steps:
                    part = slice(step * up_tile, (step + 1) * up_tile)
                    mine_ref, other_ref, up_mine_ref, up_other_ref = refs[len(flat) : len(flat) + 4]
                    pair = [r[...] if len(r.shape) == 2 else r[0] for r in (mine_ref, other_ref)]
                    value = product_terms(pair, (up_mine_ref, up_other_ref), part, 0)
                    refs[outs_at + 2][:, part] = value.astype(share[4])
        for copy in busy.values():
            copy.wait()

    args = [core, turned, all_grads, *flat]
    outs = [pltpu.HBM((features, 2 * half), F32), pltpu.HBM((2 * half, features), F32)]
    if share is not None:
        args += [*share[:2], in_vmem(share[2]), in_vmem(share[3])]
        outs.append(jax.ShapeDtypeStruct((share[0].shape[-2], features), share[4]))
    spaces = [None] * len(args)
    outs_at = len(args) - 3 + (0 if before is None else 2)
    aliases = {}
    if before is not None:
        aliases = {len(args): 0, len(args) + 1: 1}
        args += [in_hbm(a) for a in before]
        spaces += [pl.ANY, pl.ANY]
    return ordered(
        body,
        args,
        [*outs, jax.ShapeDtypeStruct((8, 128), F32)],
        name,
        4.0 * len(blocks),
        spaces=spaces,
        out_spaces=[pl.ANY, pl.ANY] + [VMEM] * (len(outs) - 1),
        scratch=[
            VMEM((tokens, width), BF16),
            VMEM((tokens, width), BF16),
            VMEM((slots, up_tile, width), F32),
            VMEM((slots, down_tile, features), F32),
            pltpu.SemaphoreType.DMA((2, slots)),
        ],
        aliases=aliases,
    )


def per_device(wide, narrow, inputs, up_weight, down_weight, out_grad):
    rows = inputs.shape[0]
    half = up_weight.shape[1] // 2
    chips = wide // 2
    core = (lax.axis_index("wide") & 1).astype(jnp.int32).reshape(1)
    ordered = Ordered()

    def swap_cores(x):
        return lax.ppermute(x, "wide", [(i, i ^ 1) for i in range(wide)])

    def shift(x, places):
        return lax.ppermute(x, "narrow", [(i, (i + places) % narrow) for i in range(narrow)])

    def across_chips(keep, got):
        partial = (keep.astype(F32) + got.astype(F32)).astype(BF16)
        hop = 1
        while True:
            peer = lax.ppermute(partial, "wide", [(i, i ^ (2 * hop)) for i in range(wide)])
            hop *= 2
            if hop >= chips:
                return partial, peer
            partial = (partial.astype(F32) + peer.astype(F32)).astype(BF16)

    offsets = sorted(range(narrow // 2 - narrow + 1, narrow // 2 + 1), key=lambda places: (abs(places), -places))
    chunks = {0: jnp.stack([inputs, out_grad])}

    up_other, down_other, give = first_product(ordered, core, True, chunks[0], up_weight, down_weight, "give_first")
    got = swap_cores(give)
    up_mine, down_mine, sent_back, keep = first_product(ordered, core, False, chunks[0], up_weight, down_weight, "keep_first")
    sums = [across_chips(keep, got)]

    def acts_of(sums, apart=False):
        mine = gelu(ordered, sums, apart)
        return mine, [swap_cores(a) for a in mine]

    slices = 2 if half % 256 == 0 else 1
    width = half // slices
    for offset in offsets[1:]:
        places = 1 if offset > 0 else -1
        chunk = chunks[offset] = shift(sent_back if offset == -1 else chunks[offset - places], places)
        give = product(ordered, chunk, up_other, down_other, "give", after=[sums[-1][0]] + [sums[0][1]] * (len(sums) == 2))
        got = swap_cores(give)
        if offset == offsets[-1]:
            early = acts_of(sums[:-1])
        keep = product(ordered, chunk, up_mine, down_mine, "keep")
        if offset != offsets[-1]:
            sums.append(across_chips(keep, got))
        else:
            parts = [slice(i * width, (i + 1) * width) for i in range(slices)]
            late = [across_chips(keep[:, :, part], got[:, :, part]) for part in parts]

    turned, all_grads = collect(ordered, [chunks[offset] for offset in offsets], [own for own, _ in late])
    shares = input_product(ordered, rows, *early, up_mine, up_other, 0, 0.1)
    shares = [share if offset == 0 else shift(share, -offset) for offset, share in zip(offsets, shares)]
    middle = acts_of(sums[-1:], True)

    scale = (rows * narrow) ** -0.5
    late_acts = []

    def grads(places, before, share):
        blocks = [
            (side, i * width, [(early[side], i * width), (middle[side], i * width), (late_acts[i][side], 0)])
            for side, i in places
        ]
        return weight_grads(ordered, core, blocks, turned, all_grads, half, scale, before, "weight_grads", share)

    late_acts.append(acts_of(late[:1]))
    share = (middle[0][0], middle[1][0], up_mine, up_other, BF16)
    up_grad, down_grad, share, _ = grads([(0, 0)], None, share)
    shares.append(shift(share, -offsets[-2]))
    partial = None
    if slices > 1:
        late_acts.append(acts_of(late[1:]))
        share = (late_acts[0][0][0], late_acts[0][1][0], up_mine, up_other, F32)
        up_grad, down_grad, partial, _ = grads([(1, 0)], (up_grad, down_grad), share)
    low = width * (slices - 1)
    so_far, share = input_product(ordered, rows, *late_acts[-1], up_mine, up_other, low, 3.0, partial, shares)
    share = shift(share, -offsets[-1])
    last = [(0, 1), (1, 1)] if slices > 1 else [(1, 0)]
    up_grad, down_grad, _ = grads(last, (up_grad, down_grad), None)
    return (so_far + share.astype(F32)).astype(BF16), up_grad, down_grad


def solution(mesh):
    placed = (
        P(("groups", "narrow"), "wide"),
        P("wide", "narrow"),
        P("narrow", "wide"),
        P(("groups", "narrow"), "wide"),
    )
    return jax.shard_map(
        functools.partial(per_device, mesh.shape["wide"], mesh.shape["narrow"]),
        mesh=mesh,
        in_specs=placed,
        out_specs=(
            P(("groups", "narrow"), "wide"),
            P(("groups", "wide"), "narrow"),
            P(("groups", "narrow"), "wide"),
        ),
        check_vma=False,
    )
```

```python
import functools

import jax
import jax.numpy as jnp
from jax import lax
from jax.experimental import pallas as pl
from jax.experimental.pallas import tpu as pltpu
from jax.sharding import PartitionSpec as P

F32, BF16 = jnp.float32, jnp.bfloat16
MIB = 1 << 20
VMEM = pltpu.VMEM
NN = (((1,), (0,)), ((), ()))
NT = (((1,), (1,)), ((), ()))
TN = (((0,), (0,)), ((), ()))


def dot(a, b, dims):
    return lax.dot_general(a, b, dims, preferred_element_type=F32)


def in_vmem(x):
    return pltpu.with_memory_space_constraint(x, VMEM)


def in_hbm(x):
    return pltpu.with_memory_space_constraint(x, pltpu.HBM)


def tile_of(extent, largest=512):
    return next(t for t in (768, 512, 384, 256, 128) if t <= largest and extent % t == 0)


class Ordered:
    def __init__(self):
        self.last = None

    def __call__(self, body, args, outs, name, micros, limit=16, spaces=None, out_spaces=None, scratch=(), aliases=None, after=()):
        args = list(args)
        spaces = spaces or [None] * len(args)
        specs = [
            pl.BlockSpec(memory_space=pltpu.SMEM if a.dtype == jnp.int32 else space or VMEM) for a, space in zip(args, spaces)
        ]
        count = len(args)
        for waited in (*after, *([] if self.last is None else [self.last])):
            args.append(waited)
            specs.append(pl.BlockSpec(memory_space=pl.ANY))
        extra = len(args) - count

        def kernel(*refs):
            body(*refs[:count], *refs[count + extra :])

        result = pl.pallas_call(
            kernel,
            out_shape=outs,
            in_specs=specs,
            out_specs=[pl.BlockSpec(memory_space=s) for s in out_spaces or [VMEM] * len(outs)],
            scratch_shapes=scratch,
            input_output_aliases=aliases or {},
            compiler_params=pltpu.CompilerParams(vmem_limit_bytes=limit * MIB),
            cost_estimate=pl.CostEstimate(flops=int(micros * 4e9), bytes_accessed=0, transcendentals=0),
            name=name,
        )(*args)
        self.last = result[-1]
        return result


def stacked(ordered, inputs, out_grad):
    def body(inputs_hbm, grads_hbm, out_ref, sems):
        copies = [
            pltpu.make_async_copy(source, out_ref.at[i], sems.at[i]) for i, source in enumerate((inputs_hbm, grads_hbm))
        ]
        for copy in copies:
            copy.start()
        for copy in copies:
            copy.wait()

    return ordered(
        body,
        (in_hbm(inputs), in_hbm(out_grad)),
        [VMEM((2, *inputs.shape), BF16)],
        "stacked",
        0.5,
        spaces=[pl.ANY, pl.ANY],
        scratch=[pltpu.SemaphoreType.DMA((2,))],
    )[0]


def first_product(ordered, core, other, chunk, up_weight, down_weight, name):
    _, rows, features = chunk.shape
    half = up_weight.shape[1] // 2
    tile = tile_of(half)
    pieces = half // tile

    def body(core_ref, chunk_ref, up_hbm, down_hbm, up_ref, down_ref, *refs):
        out_ref, sems = refs[-2:]
        side = 1 - core_ref[0] if other else core_ref[0]
        copies = []
        for i in range(pieces):
            units = pl.ds(pl.multiple_of(side * half + i * tile, tile), tile)
            part = pl.ds(i * tile, tile)
            copies.append(pltpu.make_async_copy(up_hbm.at[:, units], up_ref.at[:, part], sems.at[0, i]))
            copies.append(pltpu.make_async_copy(down_hbm.at[units, :], down_ref.at[part, :], sems.at[1, i]))
        for copy in copies:
            copy.start()
        if not other:
            refs[0][...] = chunk_ref[...]
        for i in range(pieces):
            part = slice(i * tile, (i + 1) * tile)
            copies[2 * i].wait()
            out_ref[0, :, part] = dot(chunk_ref[0], up_ref[:, part], NN).astype(BF16)
            copies[2 * i + 1].wait()
            out_ref[1, :, part] = dot(chunk_ref[1], down_ref[part, :], NT).astype(BF16)

    outs = [VMEM((features, half), BF16), VMEM((half, features), BF16)]
    outs += [] if other else [jax.ShapeDtypeStruct(chunk.shape, BF16)]
    return ordered(
        body,
        (core, chunk, in_hbm(up_weight), in_hbm(down_weight)),
        outs + [jax.ShapeDtypeStruct((2, rows, half), BF16)],
        name,
        4.5,
        spaces=[None, None, pl.ANY, pl.ANY],
        scratch=[pltpu.SemaphoreType.DMA((2, pieces))],
    )


def product(ordered, chunk, up_half, down_half, name, after=()):
    _, rows, features = chunk.shape
    half = up_half.shape[1]
    tile = tile_of(half)

    def body(chunk_ref, up_ref, down_ref, out_ref):
        for start in range(0, half, tile):
            part = slice(start, start + tile)
            out_ref[0, :, part] = dot(chunk_ref[0], up_ref[:, part], NN).astype(BF16)
            out_ref[1, :, part] = dot(chunk_ref[1], down_ref[part, :], NT).astype(BF16)

    args = (chunk, in_vmem(up_half), in_vmem(down_half))
    return ordered(body, args, [jax.ShapeDtypeStruct((2, rows, half), BF16)], name, 2.4, after=after)[0]


def product_terms(terms, part):
    share = None
    for act, up_ref, low in terms:
        term = dot(act, up_ref[part, low : low + act.shape[1]], NT)
        share = term if share is None else share + term
    return share


def grad_of(ref):
    return ref[...] if len(ref.shape) == 2 else ref[0]


def input_product(ordered, rows, terms, micros, partial=None, returned=()):
    features = terms[0][1].shape[0]
    tile = tile_of(features)
    count = len(terms)
    chunks = terms[0][0].shape[-2] // rows

    def body(*refs):
        filled = [(grad_of(refs[i]), refs[count + i], low) for i, (_, _, low) in enumerate(terms)]
        returned_refs, out_refs = refs[2 * count :][: len(returned)], refs[-chunks:]
        if returned:
            total = returned_refs[0][...].astype(F32)
            for ref in returned_refs[1:]:
                total = total + ref[...].astype(F32)
            refs[-chunks - 1][...] = total
        for start in range(0, features, tile):
            part = slice(start, start + tile)
            share = product_terms(filled, part)
            if partial is not None:
                share = share + refs[2 * count + len(returned)][:, part]
            for c, out_ref in enumerate(out_refs):
                out_ref[:, part] = share[c * rows : (c + 1) * rows].astype(BF16)

    args = [act for act, _, _ in terms] + [in_vmem(weight) for _, weight, _ in terms]
    args += [*returned, *([] if partial is None else [partial])]
    outs = [jax.ShapeDtypeStruct((rows, features), F32)] if returned else []
    return ordered(body, args, outs + [jax.ShapeDtypeStruct((rows, features), BF16)] * chunks, "input_product", micros)


def gelu(ordered, sums, apart=False):
    flat = [a for pair in sums for a in pair]
    _, rows, units = flat[0].shape

    def body(*refs):
        grad_ref, value_ref = refs[-2:] if apart else (refs[-1].at[0], refs[-1].at[1])
        for chunk in range(len(sums)):
            at = slice(chunk * rows, (chunk + 1) * rows)
            own_h, own_g, peer_h, peer_g = [refs[2 * chunk + side][i].astype(F32) for side in (0, 1) for i in (0, 1)]
            hidden, grad_hidden = own_h + peer_h, own_g + peer_g
            cdf = 0.5 * (1.0 + lax.erf(hidden * 0.7071067811865476))
            pdf = jnp.exp(-0.5 * hidden * hidden) * 0.3989422804014327
            grad_ref[at] = (grad_hidden * (cdf + hidden * pdf)).astype(BF16)
            value_ref[at] = (hidden * cdf).astype(BF16)

    outs = [jax.ShapeDtypeStruct((rows * len(sums), units), BF16)] * 2
    if not apart:
        outs = [jax.ShapeDtypeStruct((2, rows * len(sums), units), BF16)]
    return ordered(body, flat, outs, "gelu", 0.1)


def collect(ordered, chunks, after):
    count = len(chunks)
    _, rows, features = chunks[0].shape
    tile = tile_of(features, 256)

    def body(*refs):
        turned_ref, grads_ref, scratch = refs[count:]
        for i in range(count):
            scratch[i * rows : (i + 1) * rows, :] = refs[i][0]
            grads_ref[i * rows : (i + 1) * rows, :] = refs[i][1]
        for start in range(0, features, tile):
            turned_ref[start : start + tile, :] = scratch[:, start : start + tile].T

    outs = [VMEM((features, rows * count), BF16), VMEM((rows * count, features), BF16)]
    return ordered(body, chunks, outs, "collect", 0.1, scratch=[VMEM((rows * count, features), BF16)], after=after)


def weight_grads(ordered, core, blocks, turned, all_grads, half, scale, before, name, share=None):
    features, tokens = turned.shape
    width = min(a[0].shape[-1] for a, _ in blocks[0][2])
    up_tile, down_tile = tile_of(features), tile_of(width, 256)
    up_steps, down_steps = features // up_tile, width // down_tile
    slots = 3
    flat = [a for block in blocks for acts, _ in block[2] for a in acts]

    def body(core_ref, turned_ref, grads_ref, *refs):
        up_hbm, down_hbm = refs[outs_at : outs_at + 2]
        done_ref, act_g, act_v, up_stage, down_stage, sems = refs[-6:]
        done_ref[...] = jnp.zeros_like(done_ref)
        busy = {}

        def send(kind, index, value, stage, target):
            slot = index % slots
            if (kind, slot) in busy:
                busy[kind, slot].wait()
            stage[slot] = value * scale
            copy = pltpu.make_async_copy(stage.at[slot], target, sems.at[kind, slot])
            copy.start()
            busy[kind, slot] = copy

        left = refs[: len(flat)]
        for b, (other, first, acts) in enumerate(blocks):
            side = 1 - core_ref[0] if other else core_ref[0]
            base = side * half + first
            row = 0
            for arrays, column in acts:
                rows = slice(row, row + arrays[0].shape[-2])
                columns = slice(column, column + width)
                taken, left = left[: len(arrays)], left[len(arrays) :]
                act_g[rows, :] = taken[0][:, columns] if len(taken) == 2 else taken[0][0, :, columns]
                act_v[rows, :] = taken[1][:, columns] if len(taken) == 2 else taken[0][1, :, columns]
                row += arrays[0].shape[-2]
            for step in range(max(up_steps, down_steps)):
                if step < up_steps:
                    part = slice(step * up_tile, (step + 1) * up_tile)
                    value = dot(turned_ref[part, :], act_g[...], NN)
                    target = up_hbm.at[pl.ds(step * up_tile, up_tile), pl.ds(pl.multiple_of(base, 128), width)]
                    send(0, b * up_steps + step, value, up_stage, target)
                if step < down_steps:
                    part = slice(step * down_tile, (step + 1) * down_tile)
                    value = dot(act_v[:, part], grads_ref[...], TN)
                    target = down_hbm.at[pl.ds(pl.multiple_of(base + step * down_tile, 128), down_tile), :]
                    send(1, b * down_steps + step, value, down_stage, target)
                if share is not None and b == 0 and step < up_steps:
                    part = slice(step * up_tile, (step + 1) * up_tile)
                    terms = [
                        (grad_of(refs[len(flat) + i]), refs[len(flat) + len(share[0]) + i], low)
                        for i, (_, _, low) in enumerate(share[0])
                    ]
                    refs[outs_at + 2][:, part] = product_terms(terms, part).astype(share[1])
        for copy in busy.values():
            copy.wait()

    args = [core, turned, all_grads, *flat]
    outs = [pltpu.HBM((features, 2 * half), F32), pltpu.HBM((2 * half, features), F32)]
    if share is not None:
        terms, kind = share
        args += [act for act, _, _ in terms] + [in_vmem(weight) for _, weight, _ in terms]
        outs.append(jax.ShapeDtypeStruct((terms[0][0].shape[-2], features), kind))
    spaces = [None] * len(args)
    outs_at = len(args) - 3 + (0 if before is None else 2)
    aliases = {}
    if before is not None:
        aliases = {len(args): 0, len(args) + 1: 1}
        args += [in_hbm(a) for a in before]
        spaces += [pl.ANY, pl.ANY]
    return ordered(
        body,
        args,
        [*outs, jax.ShapeDtypeStruct((8, 128), F32)],
        name,
        4.0 * len(blocks),
        spaces=spaces,
        out_spaces=[pl.ANY, pl.ANY] + [VMEM] * (len(outs) - 1),
        scratch=[
            VMEM((tokens, width), BF16),
            VMEM((tokens, width), BF16),
            VMEM((slots, up_tile, width), F32),
            VMEM((slots, down_tile, features), F32),
            pltpu.SemaphoreType.DMA((2, slots)),
        ],
        aliases=aliases,
    )


def per_device(wide, narrow, inputs, up_weight, down_weight, out_grad):
    rows = inputs.shape[0]
    half = up_weight.shape[1] // 2
    chips = wide // 2
    core = (lax.axis_index("wide") & 1).astype(jnp.int32).reshape(1)
    ordered = Ordered()

    def swap_cores(x):
        return lax.ppermute(x, "wide", [(i, i ^ 1) for i in range(wide)])

    def shift(x, places):
        return lax.ppermute(x, "narrow", [(i, (i + places) % narrow) for i in range(narrow)])

    def across_chips(keep, got):
        partial = (keep.astype(F32) + got.astype(F32)).astype(BF16)
        hop = 1
        while True:
            peer = lax.ppermute(partial, "wide", [(i, i ^ (2 * hop)) for i in range(wide)])
            hop *= 2
            if hop >= chips:
                return partial, peer
            partial = (partial.astype(F32) + peer.astype(F32)).astype(BF16)

    offsets = sorted(range(narrow // 2 - narrow + 1, narrow // 2 + 1), key=lambda places: (abs(places), -places))
    chunks = {0: stacked(ordered, inputs, out_grad)}

    up_other, down_other, give = first_product(ordered, core, True, chunks[0], up_weight, down_weight, "give_first")
    got = swap_cores(give)
    up_mine, down_mine, sent_back, keep = first_product(ordered, core, False, chunks[0], up_weight, down_weight, "keep_first")
    sums = [across_chips(keep, got)]

    def acts_of(sums, apart=False):
        mine = gelu(ordered, sums, apart)
        return mine, [swap_cores(a) for a in mine]

    slices = 2 if half % 256 == 0 else 1
    width = half // slices
    for offset in offsets[1:]:
        places = 1 if offset > 0 else -1
        chunk = chunks[offset] = shift(sent_back if offset == -1 else chunks[offset - places], places)
        give = product(ordered, chunk, up_other, down_other, "give", after=[sums[-1][0]] + [sums[0][1]] * (len(sums) == 2))
        got = swap_cores(give)
        if offset == offsets[-1]:
            early = acts_of(sums[:-1])
        keep = product(ordered, chunk, up_mine, down_mine, "keep")
        if offset != offsets[-1]:
            sums.append(across_chips(keep, got))
        else:
            parts = [slice(i * width, (i + 1) * width) for i in range(slices)]
            late = [across_chips(keep[:, :, part], got[:, :, part]) for part in parts]

    turned, all_grads = collect(ordered, [chunks[offset] for offset in offsets], [own for own, _ in late])
    both = (up_mine, up_other)
    shares = input_product(ordered, rows, [(early[side][0], both[side], 0) for side in (0, 1)], 0.1)
    shares = [share if offset == 0 else shift(share, -offset) for offset, share in zip(offsets, shares)]
    middle = acts_of(sums[-1:], True)

    scale = (rows * narrow) ** -0.5
    late_acts = []

    def grads(places, before, share):
        blocks = [
            (side, i * width, [(early[side], i * width), (middle[side], i * width), (late_acts[i][side], 0)])
            for side, i in places
        ]
        return weight_grads(ordered, core, blocks, turned, all_grads, half, scale, before, "weight_grads", share)

    late_acts.append(acts_of(late[:1]))
    up_grad, down_grad, share, _ = grads([(0, 0)], None, ([(middle[side][0], both[side], 0) for side in (0, 1)], BF16))
    middle_share = shift(share, -offsets[-2])
    partial = None
    terms = [(late_acts[0][side][0], both[side], 0) for side in (0, 1)]
    if slices > 1:
        late_acts.append(acts_of(late[1:]))
        terms.append((late_acts[1][0][0], up_mine, width))
        up_grad, down_grad, partial, _ = grads([(1, 0)], (up_grad, down_grad), (terms, F32))
        terms = [(late_acts[1][1][0], up_other, width)]
    so_far, share = input_product(ordered, rows, terms, 3.0, partial, shares)
    share = shift(share, -offsets[-1])
    last = [(0, 1), (1, 1)] if slices > 1 else [(1, 0)]
    up_grad, down_grad, _ = grads(last, (up_grad, down_grad), None)
    return (so_far + middle_share.astype(F32) + share.astype(F32)).astype(BF16), up_grad, down_grad


def solution(mesh):
    placed = (
        P(("groups", "narrow"), "wide"),
        P("wide", "narrow"),
        P("narrow", "wide"),
        P(("groups", "narrow"), "wide"),
    )
    return jax.shard_map(
        functools.partial(per_device, mesh.shape["wide"], mesh.shape["narrow"]),
        mesh=mesh,
        in_specs=placed,
        out_specs=(
            P(("groups", "narrow"), "wide"),
            P(("groups", "wide"), "narrow"),
            P(("groups", "narrow"), "wide"),
        ),
        check_vma=False,
    )
```

```python
import functools

import jax
import jax.numpy as jnp
from jax import lax
from jax.experimental import pallas as pl
from jax.experimental.pallas import tpu as pltpu
from jax.sharding import PartitionSpec as P

F32, BF16 = jnp.float32, jnp.bfloat16
MIB = 1 << 20
VMEM = pltpu.VMEM
NN = (((1,), (0,)), ((), ()))
NT = (((1,), (1,)), ((), ()))
TN = (((0,), (0,)), ((), ()))


def dot(a, b, dims):
    return lax.dot_general(a, b, dims, preferred_element_type=F32)


def in_vmem(x):
    return pltpu.with_memory_space_constraint(x, VMEM)


def in_hbm(x):
    return pltpu.with_memory_space_constraint(x, pltpu.HBM)


def tile_of(extent, largest=512):
    return next(t for t in (768, 512, 384, 256, 128) if t <= largest and extent % t == 0)


class Ordered:
    def __init__(self):
        self.last = None

    def __call__(self, body, args, outs, name, micros, limit=16, spaces=None, out_spaces=None, scratch=(), aliases=None, after=()):
        args = list(args)
        spaces = spaces or [None] * len(args)
        specs = [
            pl.BlockSpec(memory_space=pltpu.SMEM if a.dtype == jnp.int32 else space or VMEM) for a, space in zip(args, spaces)
        ]
        count = len(args)
        for waited in (*after, *([] if self.last is None else [self.last])):
            args.append(waited)
            specs.append(pl.BlockSpec(memory_space=pl.ANY))
        extra = len(args) - count

        def kernel(*refs):
            body(*refs[:count], *refs[count + extra :])

        result = pl.pallas_call(
            kernel,
            out_shape=outs,
            in_specs=specs,
            out_specs=[pl.BlockSpec(memory_space=s) for s in out_spaces or [VMEM] * len(outs)],
            scratch_shapes=scratch,
            input_output_aliases=aliases or {},
            compiler_params=pltpu.CompilerParams(vmem_limit_bytes=limit * MIB),
            cost_estimate=pl.CostEstimate(flops=int(micros * 4e9), bytes_accessed=0, transcendentals=0),
            name=name,
        )(*args)
        self.last = result[-1]
        return result


def stacked(ordered, inputs, out_grad):
    def body(inputs_hbm, grads_hbm, out_ref, sems):
        copies = [
            pltpu.make_async_copy(source, out_ref.at[i], sems.at[i]) for i, source in enumerate((inputs_hbm, grads_hbm))
        ]
        for copy in copies:
            copy.start()
        for copy in copies:
            copy.wait()

    return ordered(
        body,
        (in_hbm(inputs), in_hbm(out_grad)),
        [VMEM((2, *inputs.shape), BF16)],
        "stacked",
        0.5,
        spaces=[pl.ANY, pl.ANY],
        scratch=[pltpu.SemaphoreType.DMA((2,))],
    )[0]


def copied(ordered, chunk, after):
    def body(chunk_ref, out_ref):
        out_ref[...] = chunk_ref[...]

    return ordered(body, (chunk,), [jax.ShapeDtypeStruct(chunk.shape, BF16)], "copied", 0.1, after=after)[0]


def first_product(ordered, core, other, chunk, up_weight, down_weight, name):
    _, rows, features = chunk.shape
    half = up_weight.shape[1] // 2
    tile = tile_of(half)
    pieces = half // tile

    def body(core_ref, chunk_ref, up_hbm, down_hbm, up_ref, down_ref, out_ref, sems):
        side = 1 - core_ref[0] if other else core_ref[0]
        copies = []
        for i in range(pieces):
            units = pl.ds(pl.multiple_of(side * half + i * tile, tile), tile)
            part = pl.ds(i * tile, tile)
            copies.append(pltpu.make_async_copy(up_hbm.at[:, units], up_ref.at[:, part], sems.at[0, i]))
            copies.append(pltpu.make_async_copy(down_hbm.at[units, :], down_ref.at[part, :], sems.at[1, i]))
        for copy in copies:
            copy.start()
        for i in range(pieces):
            part = slice(i * tile, (i + 1) * tile)
            copies[2 * i].wait()
            out_ref[0, :, part] = dot(chunk_ref[0], up_ref[:, part], NN).astype(BF16)
            copies[2 * i + 1].wait()
            out_ref[1, :, part] = dot(chunk_ref[1], down_ref[part, :], NT).astype(BF16)

    outs = [VMEM((features, half), BF16), VMEM((half, features), BF16)]
    return ordered(
        body,
        (core, chunk, in_hbm(up_weight), in_hbm(down_weight)),
        outs + [jax.ShapeDtypeStruct((2, rows, half), BF16)],
        name,
        4.5,
        spaces=[None, None, pl.ANY, pl.ANY],
        scratch=[pltpu.SemaphoreType.DMA((2, pieces))],
    )


def product(ordered, chunk, up_half, down_half, name, after=()):
    _, rows, features = chunk.shape
    half = up_half.shape[1]
    tile = tile_of(half)

    def body(chunk_ref, up_ref, down_ref, out_ref):
        for start in range(0, half, tile):
            part = slice(start, start + tile)
            out_ref[0, :, part] = dot(chunk_ref[0], up_ref[:, part], NN).astype(BF16)
            out_ref[1, :, part] = dot(chunk_ref[1], down_ref[part, :], NT).astype(BF16)

    args = (chunk, in_vmem(up_half), in_vmem(down_half))
    return ordered(body, args, [jax.ShapeDtypeStruct((2, rows, half), BF16)], name, 2.4, after=after)[0]


def product_terms(terms, part):
    share = None
    for act, up_ref, low in terms:
        term = dot(act, up_ref[part, low : low + act.shape[1]], NT)
        share = term if share is None else share + term
    return share


def grad_of(ref):
    return ref[...] if len(ref.shape) == 2 else ref[0]


def input_product(ordered, rows, terms, micros, partial=None, returned=()):
    features = terms[0][1].shape[0]
    tile = tile_of(features)
    count = len(terms)
    chunks = terms[0][0].shape[-2] // rows

    def body(*refs):
        filled = [(grad_of(refs[i]), refs[count + i], low) for i, (_, _, low) in enumerate(terms)]
        returned_refs, out_refs = refs[2 * count :][: len(returned)], refs[-chunks:]
        if returned:
            total = returned_refs[0][...].astype(F32)
            for ref in returned_refs[1:]:
                total = total + ref[...].astype(F32)
            refs[-chunks - 1][...] = total
        for start in range(0, features, tile):
            part = slice(start, start + tile)
            share = product_terms(filled, part)
            if partial is not None:
                share = share + refs[2 * count + len(returned)][:, part]
            for c, out_ref in enumerate(out_refs):
                out_ref[:, part] = share[c * rows : (c + 1) * rows].astype(BF16)

    args = [act for act, _, _ in terms] + [in_vmem(weight) for _, weight, _ in terms]
    args += [*returned, *([] if partial is None else [partial])]
    outs = [jax.ShapeDtypeStruct((rows, features), F32)] if returned else []
    return ordered(body, args, outs + [jax.ShapeDtypeStruct((rows, features), BF16)] * chunks, "input_product", micros)


def gelu(ordered, sums, apart=False):
    flat = [a for pair in sums for a in pair]
    _, rows, units = flat[0].shape

    def body(*refs):
        grad_ref, value_ref = refs[-2:] if apart else (refs[-1].at[0], refs[-1].at[1])
        for chunk in range(len(sums)):
            at = slice(chunk * rows, (chunk + 1) * rows)
            own_h, own_g, peer_h, peer_g = [refs[2 * chunk + side][i].astype(F32) for side in (0, 1) for i in (0, 1)]
            hidden, grad_hidden = own_h + peer_h, own_g + peer_g
            cdf = 0.5 * (1.0 + lax.erf(hidden * 0.7071067811865476))
            pdf = jnp.exp(-0.5 * hidden * hidden) * 0.3989422804014327
            grad_ref[at] = (grad_hidden * (cdf + hidden * pdf)).astype(BF16)
            value_ref[at] = (hidden * cdf).astype(BF16)

    outs = [jax.ShapeDtypeStruct((rows * len(sums), units), BF16)] * 2
    if not apart:
        outs = [jax.ShapeDtypeStruct((2, rows * len(sums), units), BF16)]
    return ordered(body, flat, outs, "gelu", 0.1)


def collect(ordered, chunks, after):
    count = len(chunks)
    _, rows, features = chunks[0].shape
    tile = tile_of(features, 256)

    def body(*refs):
        turned_ref, grads_ref, scratch = refs[count:]
        for i in range(count):
            scratch[i * rows : (i + 1) * rows, :] = refs[i][0]
            grads_ref[i * rows : (i + 1) * rows, :] = refs[i][1]
        for start in range(0, features, tile):
            turned_ref[start : start + tile, :] = scratch[:, start : start + tile].T

    outs = [VMEM((features, rows * count), BF16), VMEM((rows * count, features), BF16)]
    return ordered(body, chunks, outs, "collect", 0.1, scratch=[VMEM((rows * count, features), BF16)], after=after)


def weight_grads(ordered, core, blocks, turned, all_grads, half, scale, before, name, share=None):
    features, tokens = turned.shape
    width = min(a[0].shape[-1] for a, _ in blocks[0][2])
    up_tile, down_tile = tile_of(features), tile_of(width, 256)
    up_steps, down_steps = features // up_tile, width // down_tile
    slots = 3
    flat = [a for block in blocks for acts, _ in block[2] for a in acts]

    def body(core_ref, turned_ref, grads_ref, *refs):
        up_hbm, down_hbm = refs[outs_at : outs_at + 2]
        done_ref, act_g, act_v, up_stage, down_stage, sems = refs[-6:]
        done_ref[...] = jnp.zeros_like(done_ref)
        busy = {}

        def send(kind, index, value, stage, target):
            slot = index % slots
            if (kind, slot) in busy:
                busy[kind, slot].wait()
            stage[slot] = value * scale
            copy = pltpu.make_async_copy(stage.at[slot], target, sems.at[kind, slot])
            copy.start()
            busy[kind, slot] = copy

        left = refs[: len(flat)]
        sent = [0, 0]
        for b, (other, first, acts, parts) in enumerate(blocks):
            side = 1 - core_ref[0] if other else core_ref[0]
            base = side * half + first
            row = 0
            for arrays, column in acts:
                rows = slice(row, row + arrays[0].shape[-2])
                columns = slice(column, column + width)
                taken, left = left[: len(arrays)], left[len(arrays) :]
                act_g[rows, :] = taken[0][:, columns] if len(taken) == 2 else taken[0][0, :, columns]
                act_v[rows, :] = taken[1][:, columns] if len(taken) == 2 else taken[0][1, :, columns]
                row += arrays[0].shape[-2]
            for step in range(max(up_steps, down_steps)):
                if step < up_steps and 0 in parts:
                    part = slice(step * up_tile, (step + 1) * up_tile)
                    value = dot(turned_ref[part, :], act_g[...], NN)
                    target = up_hbm.at[pl.ds(step * up_tile, up_tile), pl.ds(pl.multiple_of(base, 128), width)]
                    send(0, sent[0], value, up_stage, target)
                    sent[0] += 1
                if step < down_steps and 1 in parts:
                    part = slice(step * down_tile, (step + 1) * down_tile)
                    value = dot(act_v[:, part], grads_ref[...], TN)
                    target = down_hbm.at[pl.ds(pl.multiple_of(base + step * down_tile, 128), down_tile), :]
                    send(1, sent[1], value, down_stage, target)
                    sent[1] += 1
                if share is not None and b == 0 and step < up_steps:
                    part = slice(step * up_tile, (step + 1) * up_tile)
                    terms = [
                        (grad_of(refs[len(flat) + i]), refs[len(flat) + len(share[0]) + i], low)
                        for i, (_, _, low) in enumerate(share[0])
                    ]
                    refs[outs_at + 2][:, part] = product_terms(terms, part).astype(share[1])
        for copy in busy.values():
            copy.wait()

    args = [core, turned, all_grads, *flat]
    outs = [pltpu.HBM((features, 2 * half), F32), pltpu.HBM((2 * half, features), F32)]
    if share is not None:
        terms, kind = share
        args += [act for act, _, _ in terms] + [in_vmem(weight) for _, weight, _ in terms]
        outs.append(jax.ShapeDtypeStruct((terms[0][0].shape[-2], features), kind))
    spaces = [None] * len(args)
    outs_at = len(args) - 3 + (0 if before is None else 2)
    aliases = {}
    if before is not None:
        aliases = {len(args): 0, len(args) + 1: 1}
        args += [in_hbm(a) for a in before]
        spaces += [pl.ANY, pl.ANY]
    return ordered(
        body,
        args,
        [*outs, jax.ShapeDtypeStruct((8, 128), F32)],
        name,
        2.0 * sum(len(block[3]) for block in blocks),
        spaces=spaces,
        out_spaces=[pl.ANY, pl.ANY] + [VMEM] * (len(outs) - 1),
        scratch=[
            VMEM((tokens, width), BF16),
            VMEM((tokens, width), BF16),
            VMEM((slots, up_tile, width), F32),
            VMEM((slots, down_tile, features), F32),
            pltpu.SemaphoreType.DMA((2, slots)),
        ],
        aliases=aliases,
    )


def per_device(wide, narrow, inputs, up_weight, down_weight, out_grad):
    rows = inputs.shape[0]
    half = up_weight.shape[1] // 2
    chips = wide // 2
    core = (lax.axis_index("wide") & 1).astype(jnp.int32).reshape(1)
    ordered = Ordered()

    def swap_cores(x):
        return lax.ppermute(x, "wide", [(i, i ^ 1) for i in range(wide)])

    def shift(x, places):
        return lax.ppermute(x, "narrow", [(i, (i + places) % narrow) for i in range(narrow)])

    def across_chips(keep, got):
        partial = (keep.astype(F32) + got.astype(F32)).astype(BF16)
        hop = 1
        while True:
            peer = lax.ppermute(partial, "wide", [(i, i ^ (2 * hop)) for i in range(wide)])
            hop *= 2
            if hop >= chips:
                return partial, peer
            partial = (partial.astype(F32) + peer.astype(F32)).astype(BF16)

    offsets = sorted(range(narrow // 2 - narrow + 1, narrow // 2 + 1), key=lambda places: (abs(places), -places))
    chunks = {0: stacked(ordered, inputs, out_grad)}

    up_other, down_other, give = first_product(ordered, core, True, chunks[0], up_weight, down_weight, "give_first")
    got = swap_cores(give)
    up_mine, down_mine, keep = first_product(ordered, core, False, chunks[0], up_weight, down_weight, "keep_first")
    sums = [across_chips(keep, got)]
    sent_back = copied(ordered, chunks[0], [sums[0][0]])

    def acts_of(sums, apart=False):
        mine = gelu(ordered, sums, apart)
        return mine, [swap_cores(a) for a in mine]

    slices = 2 if half % 256 == 0 else 1
    width = half // slices
    for offset in offsets[1:]:
        places = 1 if offset > 0 else -1
        chunk = chunks[offset] = shift(sent_back if offset == -1 else chunks[offset - places], places)
        give = product(ordered, chunk, up_other, down_other, "give", after=[sums[-1][0]] + [sums[0][1]] * (len(sums) == 2))
        got = swap_cores(give)
        if offset == offsets[-1]:
            early = acts_of(sums[:-1])
        keep = product(ordered, chunk, up_mine, down_mine, "keep")
        if offset != offsets[-1]:
            sums.append(across_chips(keep, got))
        else:
            parts = [slice(i * width, (i + 1) * width) for i in range(slices)]
            late = [across_chips(keep[:, :, part], got[:, :, part]) for part in parts]

    turned, all_grads = collect(ordered, [chunks[offset] for offset in offsets], [own for own, _ in late])
    both = (up_mine, up_other)
    shares = input_product(ordered, rows, [(early[side][0], both[side], 0) for side in (0, 1)], 0.1)
    shares = [share if offset == 0 else shift(share, -offset) for offset, share in zip(offsets, shares)]
    middle = acts_of(sums[-1:], True)

    scale = (rows * narrow) ** -0.5
    late_acts = []

    def grads(places, before, share):
        blocks = [
            (side, i * width, [(early[side], i * width), (middle[side], i * width), (late_acts[i][side], 0)], parts)
            for side, i, parts in places
        ]
        return weight_grads(ordered, core, blocks, turned, all_grads, half, scale, before, "weight_grads", share)

    late_acts.append(acts_of(late[:1]))
    up_grad, down_grad, share, _ = grads([(0, 0, (0, 1))], None, ([(middle[side][0], both[side], 0) for side in (0, 1)], BF16))
    middle_share = shift(share, -offsets[-2])
    partial = None
    terms = [(late_acts[0][side][0], both[side], 0) for side in (0, 1)]
    if slices > 1:
        late_acts.append(acts_of(late[1:]))
        terms.append((late_acts[1][0][0], up_mine, width))
        up_grad, down_grad, partial, _ = grads([(1, 0, (0,))], (up_grad, down_grad), (terms, F32))
        terms = [(late_acts[1][1][0], up_other, width)]
    so_far, share = input_product(ordered, rows, terms, 3.0, partial, shares)
    share = shift(share, -offsets[-1])
    last = [(1, 0, (1,)), (0, 1, (0, 1)), (1, 1, (0, 1))] if slices > 1 else [(1, 0, (0, 1))]
    up_grad, down_grad, _ = grads(last, (up_grad, down_grad), None)
    return (so_far + middle_share.astype(F32) + share.astype(F32)).astype(BF16), up_grad, down_grad


def solution(mesh):
    placed = (
        P(("groups", "narrow"), "wide"),
        P("wide", "narrow"),
        P("narrow", "wide"),
        P(("groups", "narrow"), "wide"),
    )
    return jax.shard_map(
        functools.partial(per_device, mesh.shape["wide"], mesh.shape["narrow"]),
        mesh=mesh,
        in_specs=placed,
        out_specs=(
            P(("groups", "narrow"), "wide"),
            P(("groups", "wide"), "narrow"),
            P(("groups", "narrow"), "wide"),
        ),
        check_vma=False,
    )
```

```python
import functools

import jax
import jax.numpy as jnp
from jax import lax
from jax.experimental import pallas as pl
from jax.experimental.pallas import tpu as pltpu
from jax.sharding import PartitionSpec as P

F32, BF16 = jnp.float32, jnp.bfloat16
MIB = 1 << 20
VMEM = pltpu.VMEM
NN = (((1,), (0,)), ((), ()))
NT = (((1,), (1,)), ((), ()))
TN = (((0,), (0,)), ((), ()))


def dot(a, b, dims):
    return lax.dot_general(a, b, dims, preferred_element_type=F32)


def in_vmem(x):
    return pltpu.with_memory_space_constraint(x, VMEM)


def in_hbm(x):
    return pltpu.with_memory_space_constraint(x, pltpu.HBM)


def tile_of(extent, largest=512):
    return next(t for t in (768, 512, 384, 256, 128) if t <= largest and extent % t == 0)


class Ordered:
    def __init__(self):
        self.last = None

    def __call__(self, body, args, outs, name, micros, limit=16, spaces=None, out_spaces=None, scratch=(), aliases=None, after=()):
        args = list(args)
        spaces = spaces or [None] * len(args)
        specs = [
            pl.BlockSpec(memory_space=pltpu.SMEM if a.dtype == jnp.int32 else space or VMEM) for a, space in zip(args, spaces)
        ]
        count = len(args)
        for waited in (*after, *([] if self.last is None else [self.last])):
            args.append(waited)
            specs.append(pl.BlockSpec(memory_space=pl.ANY))
        extra = len(args) - count

        def kernel(*refs):
            body(*refs[:count], *refs[count + extra :])

        result = pl.pallas_call(
            kernel,
            out_shape=outs,
            in_specs=specs,
            out_specs=[pl.BlockSpec(memory_space=s) for s in out_spaces or [VMEM] * len(outs)],
            scratch_shapes=scratch,
            input_output_aliases=aliases or {},
            compiler_params=pltpu.CompilerParams(vmem_limit_bytes=limit * MIB),
            cost_estimate=pl.CostEstimate(flops=int(micros * 4e9), bytes_accessed=0, transcendentals=0),
            name=name,
        )(*args)
        self.last = result[-1]
        return result


def stacked(ordered, inputs, out_grad):
    def body(inputs_hbm, grads_hbm, out_ref, sems):
        copies = [
            pltpu.make_async_copy(source, out_ref.at[i], sems.at[i]) for i, source in enumerate((inputs_hbm, grads_hbm))
        ]
        for copy in copies:
            copy.start()
        for copy in copies:
            copy.wait()

    return ordered(
        body,
        (in_hbm(inputs), in_hbm(out_grad)),
        [VMEM((2, *inputs.shape), BF16)],
        "stacked",
        0.5,
        spaces=[pl.ANY, pl.ANY],
        scratch=[pltpu.SemaphoreType.DMA((2,))],
    )[0]


def first_product(ordered, core, other, chunk, up_weight, down_weight, name):
    _, rows, features = chunk.shape
    half = up_weight.shape[1] // 2
    tile = tile_of(half)
    pieces = half // tile

    def body(core_ref, chunk_ref, up_hbm, down_hbm, up_ref, down_ref, *refs):
        out_ref, sems = refs[-2:]
        side = 1 - core_ref[0] if other else core_ref[0]
        copies = []
        for i in range(pieces):
            units = pl.ds(pl.multiple_of(side * half + i * tile, tile), tile)
            part = pl.ds(i * tile, tile)
            copies.append(pltpu.make_async_copy(up_hbm.at[:, units], up_ref.at[:, part], sems.at[0, i]))
            copies.append(pltpu.make_async_copy(down_hbm.at[units, :], down_ref.at[part, :], sems.at[1, i]))
        for copy in copies:
            copy.start()
        if not other:
            refs[0][...] = chunk_ref[...]
        for i in range(pieces):
            part = slice(i * tile, (i + 1) * tile)
            copies[2 * i].wait()
            out_ref[0, :, part] = dot(chunk_ref[0], up_ref[:, part], NN).astype(BF16)
            copies[2 * i + 1].wait()
            out_ref[1, :, part] = dot(chunk_ref[1], down_ref[part, :], NT).astype(BF16)

    outs = [VMEM((features, half), BF16), VMEM((half, features), BF16)]
    outs += [] if other else [jax.ShapeDtypeStruct(chunk.shape, BF16)]
    return ordered(
        body,
        (core, chunk, in_hbm(up_weight), in_hbm(down_weight)),
        outs + [jax.ShapeDtypeStruct((2, rows, half), BF16)],
        name,
        4.5,
        spaces=[None, None, pl.ANY, pl.ANY],
        scratch=[pltpu.SemaphoreType.DMA((2, pieces))],
    )


def product(ordered, chunk, up_half, down_half, name, after=()):
    _, rows, features = chunk.shape
    half = up_half.shape[1]
    tile = tile_of(half)

    def body(chunk_ref, up_ref, down_ref, out_ref):
        for start in range(0, half, tile):
            part = slice(start, start + tile)
            out_ref[0, :, part] = dot(chunk_ref[0], up_ref[:, part], NN).astype(BF16)
            out_ref[1, :, part] = dot(chunk_ref[1], down_ref[part, :], NT).astype(BF16)

    args = (chunk, in_vmem(up_half), in_vmem(down_half))
    return ordered(body, args, [jax.ShapeDtypeStruct((2, rows, half), BF16)], name, 2.4, after=after)[0]


def product_terms(terms, part):
    share = None
    for act, up_ref, low in terms:
        term = dot(act, up_ref[part, low : low + act.shape[1]], NT)
        share = term if share is None else share + term
    return share


def grad_of(ref):
    return ref[...] if len(ref.shape) == 2 else ref[0]


def input_product(ordered, rows, terms, micros, partial=None, returned=()):
    features = terms[0][1].shape[0]
    tile = tile_of(features)
    count = len(terms)
    chunks = terms[0][0].shape[-2] // rows

    def body(*refs):
        filled = [(grad_of(refs[i]), refs[count + i], low) for i, (_, _, low) in enumerate(terms)]
        returned_refs, out_refs = refs[2 * count :][: len(returned)], refs[-chunks:]
        if returned:
            total = returned_refs[0][...].astype(F32)
            for ref in returned_refs[1:]:
                total = total + ref[...].astype(F32)
            refs[-chunks - 1][...] = total
        for start in range(0, features, tile):
            part = slice(start, start + tile)
            share = product_terms(filled, part)
            if partial is not None:
                share = share + refs[2 * count + len(returned)][:, part]
            for c, out_ref in enumerate(out_refs):
                out_ref[:, part] = share[c * rows : (c + 1) * rows].astype(BF16)

    args = [act for act, _, _ in terms] + [in_vmem(weight) for _, weight, _ in terms]
    args += [*returned, *([] if partial is None else [partial])]
    outs = [jax.ShapeDtypeStruct((rows, features), F32)] if returned else []
    return ordered(body, args, outs + [jax.ShapeDtypeStruct((rows, features), BF16)] * chunks, "input_product", micros)


def gelu(ordered, sums, apart=False):
    flat = [a for pair in sums for a in pair]
    _, rows, units = flat[0].shape

    def body(*refs):
        grad_ref, value_ref = refs[-2:] if apart else (refs[-1].at[0], refs[-1].at[1])
        for chunk in range(len(sums)):
            at = slice(chunk * rows, (chunk + 1) * rows)
            own_h, own_g, peer_h, peer_g = [refs[2 * chunk + side][i].astype(F32) for side in (0, 1) for i in (0, 1)]
            hidden, grad_hidden = own_h + peer_h, own_g + peer_g
            cdf = 0.5 * (1.0 + lax.erf(hidden * 0.7071067811865476))
            pdf = jnp.exp(-0.5 * hidden * hidden) * 0.3989422804014327
            grad_ref[at] = (grad_hidden * (cdf + hidden * pdf)).astype(BF16)
            value_ref[at] = (hidden * cdf).astype(BF16)

    outs = [jax.ShapeDtypeStruct((rows * len(sums), units), BF16)] * 2
    if not apart:
        outs = [jax.ShapeDtypeStruct((2, rows * len(sums), units), BF16)]
    return ordered(body, flat, outs, "gelu", 0.1)


def collect(ordered, chunks, after):
    count = len(chunks)
    _, rows, features = chunks[0].shape
    tile = tile_of(features, 256)

    def body(*refs):
        turned_ref, grads_ref, scratch = refs[count:]
        for i in range(count):
            scratch[i * rows : (i + 1) * rows, :] = refs[i][0]
            grads_ref[i * rows : (i + 1) * rows, :] = refs[i][1]
        for start in range(0, features, tile):
            turned_ref[start : start + tile, :] = scratch[:, start : start + tile].T

    outs = [VMEM((features, rows * count), BF16), VMEM((rows * count, features), BF16)]
    return ordered(body, chunks, outs, "collect", 0.1, scratch=[VMEM((rows * count, features), BF16)], after=after)


def weight_grads(ordered, core, blocks, turned, all_grads, half, scale, before, name, share=None):
    features, tokens = turned.shape
    width = min(a[0].shape[-1] for a, _ in blocks[0][2])
    up_tile, down_tile = tile_of(features), tile_of(width, 256)
    up_steps, down_steps = features // up_tile, width // down_tile
    slots = 3
    flat = [a for block in blocks for acts, _ in block[2] for a in acts]

    def body(core_ref, turned_ref, grads_ref, *refs):
        up_hbm, down_hbm = refs[outs_at : outs_at + 2]
        done_ref, act_g, act_v, up_stage, down_stage, sems = refs[-6:]
        done_ref[...] = jnp.zeros_like(done_ref)
        busy = {}

        def send(kind, index, value, stage, target):
            slot = index % slots
            if (kind, slot) in busy:
                busy[kind, slot].wait()
            stage[slot] = value * scale
            copy = pltpu.make_async_copy(stage.at[slot], target, sems.at[kind, slot])
            copy.start()
            busy[kind, slot] = copy

        left = refs[: len(flat)]
        sent = [0, 0]
        for b, (other, first, acts, parts) in enumerate(blocks):
            side = 1 - core_ref[0] if other else core_ref[0]
            base = side * half + first
            row = 0
            for arrays, column in acts:
                rows = slice(row, row + arrays[0].shape[-2])
                columns = slice(column, column + width)
                taken, left = left[: len(arrays)], left[len(arrays) :]
                act_g[rows, :] = taken[0][:, columns] if len(taken) == 2 else taken[0][0, :, columns]
                act_v[rows, :] = taken[1][:, columns] if len(taken) == 2 else taken[0][1, :, columns]
                row += arrays[0].shape[-2]
            for step in range(max(up_steps, down_steps)):
                if step < up_steps and 0 in parts:
                    part = slice(step * up_tile, (step + 1) * up_tile)
                    value = dot(turned_ref[part, :], act_g[...], NN)
                    target = up_hbm.at[pl.ds(step * up_tile, up_tile), pl.ds(pl.multiple_of(base, 128), width)]
                    send(0, sent[0], value, up_stage, target)
                    sent[0] += 1
                if step < down_steps and 1 in parts:
                    part = slice(step * down_tile, (step + 1) * down_tile)
                    value = dot(act_v[:, part], grads_ref[...], TN)
                    target = down_hbm.at[pl.ds(pl.multiple_of(base + step * down_tile, 128), down_tile), :]
                    send(1, sent[1], value, down_stage, target)
                    sent[1] += 1
                if share is not None and b == 0 and step < up_steps:
                    part = slice(step * up_tile, (step + 1) * up_tile)
                    given = list(refs[len(flat) :])
                    filled = []
                    for acts, _, low in share[0]:
                        rows = [grad_of(given.pop(0)) for _ in acts]
                        filled.append((rows[0] if len(rows) == 1 else jnp.concatenate(rows, axis=0), given.pop(0), low))
                    value = product_terms(filled, part).astype(share[1])
                    height = value.shape[0] // share[2]
                    for i in range(share[2]):
                        refs[outs_at + 2 + i][:, part] = value[i * height : (i + 1) * height]
        for copy in busy.values():
            copy.wait()

    args = [core, turned, all_grads, *flat]
    outs = [pltpu.HBM((features, 2 * half), F32), pltpu.HBM((2 * half, features), F32)]
    if share is not None:
        terms, kind, count = share
        for acts, weight, _ in terms:
            args += [*acts, in_vmem(weight)]
        height = sum(a.shape[-2] for a in terms[0][0]) // count
        outs += [jax.ShapeDtypeStruct((height, features), kind)] * count
    spaces = [None] * len(args)
    outs_at = len(args) - 3 + (0 if before is None else 2)
    aliases = {}
    if before is not None:
        aliases = {len(args): 0, len(args) + 1: 1}
        args += [in_hbm(a) for a in before]
        spaces += [pl.ANY, pl.ANY]
    return ordered(
        body,
        args,
        [*outs, jax.ShapeDtypeStruct((8, 128), F32)],
        name,
        2.0 * sum(len(block[3]) for block in blocks),
        spaces=spaces,
        out_spaces=[pl.ANY, pl.ANY] + [VMEM] * (len(outs) - 1),
        scratch=[
            VMEM((tokens, width), BF16),
            VMEM((tokens, width), BF16),
            VMEM((slots, up_tile, width), F32),
            VMEM((slots, down_tile, features), F32),
            pltpu.SemaphoreType.DMA((2, slots)),
        ],
        aliases=aliases,
    )


def per_device(wide, narrow, inputs, up_weight, down_weight, out_grad):
    rows = inputs.shape[0]
    half = up_weight.shape[1] // 2
    chips = wide // 2
    core = (lax.axis_index("wide") & 1).astype(jnp.int32).reshape(1)
    ordered = Ordered()

    def swap_cores(x):
        return lax.ppermute(x, "wide", [(i, i ^ 1) for i in range(wide)])

    def shift(x, places):
        return lax.ppermute(x, "narrow", [(i, (i + places) % narrow) for i in range(narrow)])

    def across_chips(keep, got):
        partial = (keep.astype(F32) + got.astype(F32)).astype(BF16)
        hop = 1
        while True:
            peer = lax.ppermute(partial, "wide", [(i, i ^ (2 * hop)) for i in range(wide)])
            hop *= 2
            if hop >= chips:
                return partial, peer
            partial = (partial.astype(F32) + peer.astype(F32)).astype(BF16)

    offsets = sorted(range(narrow // 2 - narrow + 1, narrow // 2 + 1), key=lambda places: (abs(places), -places))
    chunks = {0: stacked(ordered, inputs, out_grad)}

    up_other, down_other, give = first_product(ordered, core, True, chunks[0], up_weight, down_weight, "give_first")
    got = swap_cores(give)
    up_mine, down_mine, sent_back, keep = first_product(ordered, core, False, chunks[0], up_weight, down_weight, "keep_first")
    sums = [across_chips(keep, got)]

    def acts_of(sums, apart=False):
        mine = gelu(ordered, sums, apart)
        return mine, [swap_cores(a) for a in mine]

    slices = 2 if half % 256 == 0 else 1
    width = half // slices
    for offset in offsets[1:]:
        places = 1 if offset > 0 else -1
        chunk = chunks[offset] = shift(sent_back if offset == -1 else chunks[offset - places], places)
        give = product(ordered, chunk, up_other, down_other, "give", after=[sums[-1][0]] + [sums[0][1]] * (len(sums) == 2))
        got = swap_cores(give)
        if offset == offsets[-1]:
            early = acts_of(sums[:-1])
        keep = product(ordered, chunk, up_mine, down_mine, "keep")
        if offset != offsets[-1]:
            sums.append(across_chips(keep, got))
        else:
            parts = [slice(i * width, (i + 1) * width) for i in range(slices)]
            late = [across_chips(keep[:, :, part], got[:, :, part]) for part in parts]

    turned, all_grads = collect(ordered, [chunks[offset] for offset in offsets], [own for own, _ in late])
    both = (up_mine, up_other)
    middle = acts_of(sums[-1:], True)

    both = (up_mine, up_other)
    scale = (rows * narrow) ** -0.5
    late_acts = []

    def grads(places, before, share):
        blocks = [
            (side, i * width, [(early[side], i * width), (middle[side], i * width), (late_acts[i][side], 0)], parts)
            for side, i, parts in places
        ]
        return weight_grads(ordered, core, blocks, turned, all_grads, half, scale, before, "weight_grads", share)

    late_acts.append(acts_of(late[:1]))
    terms = [((early[side][0], middle[side][0]), both[side], 0) for side in (0, 1)]
    up_grad, down_grad, *shares, _ = grads([(0, 0, (0, 1))], None, (terms, BF16, narrow - 1))
    kept, *shares = [share if offset == 0 else shift(share, -offset) for offset, share in zip(offsets, shares)]
    partial = None
    terms = [(late_acts[0][side][0], both[side], 0) for side in (0, 1)]
    if slices > 1:
        late_acts.append(acts_of(late[1:]))
        terms = [((act,), weight, low) for act, weight, low in [*terms, (late_acts[1][0][0], up_mine, width)]]
        up_grad, down_grad, partial, _ = grads([(1, 0, (0,))], (up_grad, down_grad), (terms, F32, 1))
        terms = [(late_acts[1][1][0], up_other, width)]
    (share,) = input_product(ordered, rows, terms, 3.0, partial)
    share = shift(share, -offsets[-1])
    last = [(1, 0, (1,)), (0, 1, (0, 1)), (1, 1, (0, 1))] if slices > 1 else [(1, 0, (0, 1))]
    up_grad, down_grad, _ = grads(last, (up_grad, down_grad), None)
    return sum(share.astype(F32) for share in (kept, *shares, share)).astype(BF16), up_grad, down_grad


def solution(mesh):
    placed = (
        P(("groups", "narrow"), "wide"),
        P("wide", "narrow"),
        P("narrow", "wide"),
        P(("groups", "narrow"), "wide"),
    )
    return jax.shard_map(
        functools.partial(per_device, mesh.shape["wide"], mesh.shape["narrow"]),
        mesh=mesh,
        in_specs=placed,
        out_specs=(
            P(("groups", "narrow"), "wide"),
            P(("groups", "wide"), "narrow"),
            P(("groups", "narrow"), "wide"),
        ),
        check_vma=False,
    )
```

```python
import functools

import jax
import jax.numpy as jnp
from jax import lax
from jax.experimental import pallas as pl
from jax.experimental.pallas import tpu as pltpu
from jax.sharding import PartitionSpec as P

F32, BF16 = jnp.float32, jnp.bfloat16
MIB = 1 << 20
VMEM = pltpu.VMEM
NN = (((1,), (0,)), ((), ()))
NT = (((1,), (1,)), ((), ()))
TN = (((0,), (0,)), ((), ()))


def dot(a, b, dims):
    return lax.dot_general(a, b, dims, preferred_element_type=F32)


def in_vmem(x):
    return pltpu.with_memory_space_constraint(x, VMEM)


def in_hbm(x):
    return pltpu.with_memory_space_constraint(x, pltpu.HBM)


def tile_of(extent, largest=512):
    return next(t for t in (768, 512, 384, 256, 128) if t <= largest and extent % t == 0)


class Ordered:
    def __init__(self):
        self.last = None

    def __call__(self, body, args, outs, name, micros, limit=16, spaces=None, out_spaces=None, scratch=(), aliases=None, after=()):
        args = list(args)
        spaces = spaces or [None] * len(args)
        specs = [
            pl.BlockSpec(memory_space=pltpu.SMEM if a.dtype == jnp.int32 else space or VMEM) for a, space in zip(args, spaces)
        ]
        count = len(args)
        for waited in (*after, *([] if self.last is None else [self.last])):
            args.append(waited)
            specs.append(pl.BlockSpec(memory_space=pl.ANY))
        extra = len(args) - count

        def kernel(*refs):
            body(*refs[:count], *refs[count + extra :])

        result = pl.pallas_call(
            kernel,
            out_shape=outs,
            in_specs=specs,
            out_specs=[pl.BlockSpec(memory_space=s) for s in out_spaces or [VMEM] * len(outs)],
            scratch_shapes=scratch,
            input_output_aliases=aliases or {},
            compiler_params=pltpu.CompilerParams(vmem_limit_bytes=limit * MIB),
            cost_estimate=pl.CostEstimate(flops=int(micros * 4e9), bytes_accessed=0, transcendentals=0),
            name=name,
        )(*args)
        self.last = result[-1]
        return result


def stacked(ordered, inputs, out_grad):
    def body(inputs_hbm, grads_hbm, out_ref, sems):
        copies = [
            pltpu.make_async_copy(source, out_ref.at[i], sems.at[i]) for i, source in enumerate((inputs_hbm, grads_hbm))
        ]
        for copy in copies:
            copy.start()
        for copy in copies:
            copy.wait()

    return ordered(
        body,
        (in_hbm(inputs), in_hbm(out_grad)),
        [VMEM((2, *inputs.shape), BF16)],
        "stacked",
        0.5,
        spaces=[pl.ANY, pl.ANY],
        scratch=[pltpu.SemaphoreType.DMA((2,))],
    )[0]


def first_product(ordered, core, other, chunk, up_weight, down_weight, name):
    _, rows, features = chunk.shape
    half = up_weight.shape[1] // 2
    tile = tile_of(half)
    pieces = half // tile

    def body(core_ref, chunk_ref, up_hbm, down_hbm, up_ref, down_ref, *refs):
        out_ref, sems = refs[-2:]
        side = 1 - core_ref[0] if other else core_ref[0]
        copies = []
        for i in range(pieces):
            units = pl.ds(pl.multiple_of(side * half + i * tile, tile), tile)
            part = pl.ds(i * tile, tile)
            copies.append(pltpu.make_async_copy(up_hbm.at[:, units], up_ref.at[:, part], sems.at[0, i]))
            copies.append(pltpu.make_async_copy(down_hbm.at[units, :], down_ref.at[part, :], sems.at[1, i]))
        for i, copy in enumerate(copies):
            copy.start(priority=i % 2)
        if not other:
            refs[0][...] = chunk_ref[...]
        for i in range(pieces):
            part = slice(i * tile, (i + 1) * tile)
            copies[2 * i].wait()
            out_ref[0, :, part] = dot(chunk_ref[0], up_ref[:, part], NN).astype(BF16)
            copies[2 * i + 1].wait()
            out_ref[1, :, part] = dot(chunk_ref[1], down_ref[part, :], NT).astype(BF16)

    outs = [VMEM((features, half), BF16), VMEM((half, features), BF16)]
    outs += [] if other else [jax.ShapeDtypeStruct(chunk.shape, BF16)]
    return ordered(
        body,
        (core, chunk, in_hbm(up_weight), in_hbm(down_weight)),
        outs + [jax.ShapeDtypeStruct((2, rows, half), BF16)],
        name,
        4.5,
        spaces=[None, None, pl.ANY, pl.ANY],
        scratch=[pltpu.SemaphoreType.DMA((2, pieces))],
    )


def product(ordered, chunk, up_half, down_half, name, after=()):
    _, rows, features = chunk.shape
    half = up_half.shape[1]
    tile = tile_of(half)

    def body(chunk_ref, up_ref, down_ref, out_ref):
        for start in range(0, half, tile):
            part = slice(start, start + tile)
            out_ref[0, :, part] = dot(chunk_ref[0], up_ref[:, part], NN).astype(BF16)
            out_ref[1, :, part] = dot(chunk_ref[1], down_ref[part, :], NT).astype(BF16)

    args = (chunk, in_vmem(up_half), in_vmem(down_half))
    return ordered(body, args, [jax.ShapeDtypeStruct((2, rows, half), BF16)], name, 2.4, after=after)[0]


def product_terms(terms, part):
    share = None
    for act, up_ref, low in terms:
        term = dot(act, up_ref[part, low : low + act.shape[1]], NT)
        share = term if share is None else share + term
    return share


def grad_of(ref):
    return ref[...] if len(ref.shape) == 2 else ref[0]


def input_product(ordered, rows, terms, micros, partial=None, returned=()):
    features = terms[0][1].shape[0]
    tile = tile_of(features)
    count = len(terms)
    chunks = terms[0][0].shape[-2] // rows

    def body(*refs):
        filled = [(grad_of(refs[i]), refs[count + i], low) for i, (_, _, low) in enumerate(terms)]
        returned_refs, out_refs = refs[2 * count :][: len(returned)], refs[-chunks:]
        if returned:
            total = returned_refs[0][...].astype(F32)
            for ref in returned_refs[1:]:
                total = total + ref[...].astype(F32)
            refs[-chunks - 1][...] = total
        for start in range(0, features, tile):
            part = slice(start, start + tile)
            share = product_terms(filled, part)
            if partial is not None:
                share = share + refs[2 * count + len(returned)][:, part]
            for c, out_ref in enumerate(out_refs):
                out_ref[:, part] = share[c * rows : (c + 1) * rows].astype(BF16)

    args = [act for act, _, _ in terms] + [in_vmem(weight) for _, weight, _ in terms]
    args += [*returned, *([] if partial is None else [partial])]
    outs = [jax.ShapeDtypeStruct((rows, features), F32)] if returned else []
    return ordered(body, args, outs + [jax.ShapeDtypeStruct((rows, features), BF16)] * chunks, "input_product", micros)


def gelu(ordered, sums, apart=False):
    flat = [a for pair in sums for a in pair]
    _, rows, units = flat[0].shape

    def body(*refs):
        grad_ref, value_ref = refs[-2:] if apart else (refs[-1].at[0], refs[-1].at[1])
        for chunk in range(len(sums)):
            at = slice(chunk * rows, (chunk + 1) * rows)
            own_h, own_g, peer_h, peer_g = [refs[2 * chunk + side][i].astype(F32) for side in (0, 1) for i in (0, 1)]
            hidden, grad_hidden = own_h + peer_h, own_g + peer_g
            cdf = 0.5 * (1.0 + lax.erf(hidden * 0.7071067811865476))
            pdf = jnp.exp(-0.5 * hidden * hidden) * 0.3989422804014327
            grad_ref[at] = (grad_hidden * (cdf + hidden * pdf)).astype(BF16)
            value_ref[at] = (hidden * cdf).astype(BF16)

    outs = [jax.ShapeDtypeStruct((rows * len(sums), units), BF16)] * 2
    if not apart:
        outs = [jax.ShapeDtypeStruct((2, rows * len(sums), units), BF16)]
    return ordered(body, flat, outs, "gelu", 0.1)


def collect(ordered, chunks, after):
    count = len(chunks)
    _, rows, features = chunks[0].shape
    tile = tile_of(features, 256)

    def body(*refs):
        turned_ref, grads_ref, scratch = refs[count:]
        for i in range(count):
            scratch[i * rows : (i + 1) * rows, :] = refs[i][0]
            grads_ref[i * rows : (i + 1) * rows, :] = refs[i][1]
        for start in range(0, features, tile):
            turned_ref[start : start + tile, :] = scratch[:, start : start + tile].T

    outs = [VMEM((features, rows * count), BF16), VMEM((rows * count, features), BF16)]
    return ordered(body, chunks, outs, "collect", 0.1, scratch=[VMEM((rows * count, features), BF16)], after=after)


def weight_grads(ordered, core, blocks, turned, all_grads, half, scale, before, name, share=None):
    features, tokens = turned.shape
    width = min(a[0].shape[-1] for a, _ in blocks[0][2])
    up_tile, down_tile = tile_of(features), tile_of(width, 256)
    up_steps, down_steps = features // up_tile, width // down_tile
    slots = 3
    flat = [a for block in blocks for acts, _ in block[2] for a in acts]

    def body(core_ref, turned_ref, grads_ref, *refs):
        up_hbm, down_hbm = refs[outs_at : outs_at + 2]
        done_ref, act_g, act_v, up_stage, down_stage, sems = refs[-6:]
        done_ref[...] = jnp.zeros_like(done_ref)
        busy = {}

        def send(kind, index, value, stage, target):
            slot = index % slots
            if (kind, slot) in busy:
                busy[kind, slot].wait()
            stage[slot] = value * scale
            copy = pltpu.make_async_copy(stage.at[slot], target, sems.at[kind, slot])
            copy.start(priority=kind)
            busy[kind, slot] = copy

        left = refs[: len(flat)]
        for b, (other, first, acts) in enumerate(blocks):
            side = 1 - core_ref[0] if other else core_ref[0]
            base = side * half + first
            row = 0
            for arrays, column in acts:
                rows = slice(row, row + arrays[0].shape[-2])
                columns = slice(column, column + width)
                taken, left = left[: len(arrays)], left[len(arrays) :]
                act_g[rows, :] = taken[0][:, columns] if len(taken) == 2 else taken[0][0, :, columns]
                act_v[rows, :] = taken[1][:, columns] if len(taken) == 2 else taken[0][1, :, columns]
                row += arrays[0].shape[-2]
            for step in range(max(up_steps, down_steps)):
                if step < up_steps:
                    part = slice(step * up_tile, (step + 1) * up_tile)
                    value = dot(turned_ref[part, :], act_g[...], NN)
                    target = up_hbm.at[pl.ds(step * up_tile, up_tile), pl.ds(pl.multiple_of(base, 128), width)]
                    send(0, b * up_steps + step, value, up_stage, target)
                if step < down_steps:
                    part = slice(step * down_tile, (step + 1) * down_tile)
                    value = dot(act_v[:, part], grads_ref[...], TN)
                    target = down_hbm.at[pl.ds(pl.multiple_of(base + step * down_tile, 128), down_tile), :]
                    send(1, b * down_steps + step, value, down_stage, target)
                if share is not None and b == 0 and step < up_steps:
                    part = slice(step * up_tile, (step + 1) * up_tile)
                    terms = [
                        (grad_of(refs[len(flat) + i]), refs[len(flat) + len(share[0]) + i], low)
                        for i, (_, _, low) in enumerate(share[0])
                    ]
                    refs[outs_at + 2][:, part] = product_terms(terms, part).astype(share[1])
        for copy in busy.values():
            copy.wait()

    args = [core, turned, all_grads, *flat]
    outs = [pltpu.HBM((features, 2 * half), F32), pltpu.HBM((2 * half, features), F32)]
    if share is not None:
        terms, kind = share
        args += [act for act, _, _ in terms] + [in_vmem(weight) for _, weight, _ in terms]
        outs.append(jax.ShapeDtypeStruct((terms[0][0].shape[-2], features), kind))
    spaces = [None] * len(args)
    outs_at = len(args) - 3 + (0 if before is None else 2)
    aliases = {}
    if before is not None:
        aliases = {len(args): 0, len(args) + 1: 1}
        args += [in_hbm(a) for a in before]
        spaces += [pl.ANY, pl.ANY]
    return ordered(
        body,
        args,
        [*outs, jax.ShapeDtypeStruct((8, 128), F32)],
        name,
        4.0 * len(blocks),
        spaces=spaces,
        out_spaces=[pl.ANY, pl.ANY] + [VMEM] * (len(outs) - 1),
        scratch=[
            VMEM((tokens, width), BF16),
            VMEM((tokens, width), BF16),
            VMEM((slots, up_tile, width), F32),
            VMEM((slots, down_tile, features), F32),
            pltpu.SemaphoreType.DMA((2, slots)),
        ],
        aliases=aliases,
    )


def per_device(wide, narrow, inputs, up_weight, down_weight, out_grad):
    rows = inputs.shape[0]
    half = up_weight.shape[1] // 2
    chips = wide // 2
    core = (lax.axis_index("wide") & 1).astype(jnp.int32).reshape(1)
    ordered = Ordered()

    def swap_cores(x):
        return lax.ppermute(x, "wide", [(i, i ^ 1) for i in range(wide)])

    def shift(x, places):
        return lax.ppermute(x, "narrow", [(i, (i + places) % narrow) for i in range(narrow)])

    def across_chips(keep, got):
        partial = (keep.astype(F32) + got.astype(F32)).astype(BF16)
        hop = 1
        while True:
            peer = lax.ppermute(partial, "wide", [(i, i ^ (2 * hop)) for i in range(wide)])
            hop *= 2
            if hop >= chips:
                return partial, peer
            partial = (partial.astype(F32) + peer.astype(F32)).astype(BF16)

    offsets = sorted(range(narrow // 2 - narrow + 1, narrow // 2 + 1), key=lambda places: (abs(places), -places))
    chunks = {0: stacked(ordered, inputs, out_grad)}

    up_other, down_other, give = first_product(ordered, core, True, chunks[0], up_weight, down_weight, "give_first")
    got = swap_cores(give)
    up_mine, down_mine, sent_back, keep = first_product(ordered, core, False, chunks[0], up_weight, down_weight, "keep_first")
    sums = [across_chips(keep, got)]

    def acts_of(sums, apart=False):
        mine = gelu(ordered, sums, apart)
        return mine, [swap_cores(a) for a in mine]

    slices = 2 if half % 256 == 0 else 1
    width = half // slices
    for offset in offsets[1:]:
        places = 1 if offset > 0 else -1
        chunk = chunks[offset] = shift(sent_back if offset == -1 else chunks[offset - places], places)
        give = product(ordered, chunk, up_other, down_other, "give", after=[sums[-1][0]] + [sums[0][1]] * (len(sums) == 2))
        got = swap_cores(give)
        if offset == offsets[-1]:
            early = acts_of(sums[:-1])
        keep = product(ordered, chunk, up_mine, down_mine, "keep")
        if offset != offsets[-1]:
            sums.append(across_chips(keep, got))
        else:
            parts = [slice(i * width, (i + 1) * width) for i in range(slices)]
            late = [across_chips(keep[:, :, part], got[:, :, part]) for part in parts]

    turned, all_grads = collect(ordered, [chunks[offset] for offset in offsets], [own for own, _ in late])
    both = (up_mine, up_other)
    shares = input_product(ordered, rows, [(early[side][0], both[side], 0) for side in (0, 1)], 0.1)
    shares = [share if offset == 0 else shift(share, -offset) for offset, share in zip(offsets, shares)]
    middle = acts_of(sums[-1:], True)

    scale = (rows * narrow) ** -0.5
    late_acts = []

    def grads(places, before, share):
        blocks = [
            (side, i * width, [(early[side], i * width), (middle[side], i * width), (late_acts[i][side], 0)])
            for side, i in places
        ]
        return weight_grads(ordered, core, blocks, turned, all_grads, half, scale, before, "weight_grads", share)

    late_acts.append(acts_of(late[:1]))
    up_grad, down_grad, share, _ = grads([(0, 0)], None, ([(middle[side][0], both[side], 0) for side in (0, 1)], BF16))
    middle_share = shift(share, -offsets[-2])
    partial = None
    terms = [(late_acts[0][side][0], both[side], 0) for side in (0, 1)]
    if slices > 1:
        late_acts.append(acts_of(late[1:]))
        terms.append((late_acts[1][0][0], up_mine, width))
        up_grad, down_grad, partial, _ = grads([(1, 0)], (up_grad, down_grad), (terms, F32))
        terms = [(late_acts[1][1][0], up_other, width)]
    so_far, share = input_product(ordered, rows, terms, 3.0, partial, shares)
    share = shift(share, -offsets[-1])
    last = [(0, 1), (1, 1)] if slices > 1 else [(1, 0)]
    up_grad, down_grad, _ = grads(last, (up_grad, down_grad), None)
    return (so_far + middle_share.astype(F32) + share.astype(F32)).astype(BF16), up_grad, down_grad


def solution(mesh):
    placed = (
        P(("groups", "narrow"), "wide"),
        P("wide", "narrow"),
        P("narrow", "wide"),
        P(("groups", "narrow"), "wide"),
    )
    return jax.shard_map(
        functools.partial(per_device, mesh.shape["wide"], mesh.shape["narrow"]),
        mesh=mesh,
        in_specs=placed,
        out_specs=(
            P(("groups", "narrow"), "wide"),
            P(("groups", "wide"), "narrow"),
            P(("groups", "narrow"), "wide"),
        ),
        check_vma=False,
    )
```

```python
import functools

import jax
import jax.numpy as jnp
from jax import lax
from jax.experimental import pallas as pl
from jax.experimental.pallas import tpu as pltpu
from jax.sharding import PartitionSpec as P

F32, BF16 = jnp.float32, jnp.bfloat16
MIB = 1 << 20
VMEM = pltpu.VMEM
NN = (((1,), (0,)), ((), ()))
NT = (((1,), (1,)), ((), ()))
TN = (((0,), (0,)), ((), ()))


def dot(a, b, dims):
    return lax.dot_general(a, b, dims, preferred_element_type=F32)


def in_vmem(x):
    return pltpu.with_memory_space_constraint(x, VMEM)


def in_hbm(x):
    return pltpu.with_memory_space_constraint(x, pltpu.HBM)


def tile_of(extent, largest=512):
    return next(t for t in (768, 512, 384, 256, 128) if t <= largest and extent % t == 0)


class Ordered:
    def __init__(self):
        self.last = None

    def __call__(self, body, args, outs, name, micros, limit=16, spaces=None, out_spaces=None, scratch=(), aliases=None, after=()):
        args = list(args)
        spaces = spaces or [None] * len(args)
        specs = [
            pl.BlockSpec(memory_space=pltpu.SMEM if a.dtype == jnp.int32 else space or VMEM) for a, space in zip(args, spaces)
        ]
        count = len(args)
        for waited in (*after, *([] if self.last is None else [self.last])):
            args.append(waited)
            specs.append(pl.BlockSpec(memory_space=pl.ANY))
        extra = len(args) - count

        def kernel(*refs):
            body(*refs[:count], *refs[count + extra :])

        result = pl.pallas_call(
            kernel,
            out_shape=outs,
            in_specs=specs,
            out_specs=[pl.BlockSpec(memory_space=s) for s in out_spaces or [VMEM] * len(outs)],
            scratch_shapes=scratch,
            input_output_aliases=aliases or {},
            compiler_params=pltpu.CompilerParams(vmem_limit_bytes=limit * MIB),
            cost_estimate=pl.CostEstimate(flops=int(micros * 4e9), bytes_accessed=0, transcendentals=0),
            name=name,
        )(*args)
        self.last = result[-1]
        return result


def stacked(ordered, inputs, out_grad):
    def body(inputs_hbm, grads_hbm, out_ref, sems):
        copies = [
            pltpu.make_async_copy(source, out_ref.at[i], sems.at[i]) for i, source in enumerate((inputs_hbm, grads_hbm))
        ]
        for copy in copies:
            copy.start()
        for copy in copies:
            copy.wait()

    return ordered(
        body,
        (in_hbm(inputs), in_hbm(out_grad)),
        [VMEM((2, *inputs.shape), BF16)],
        "stacked",
        0.5,
        spaces=[pl.ANY, pl.ANY],
        scratch=[pltpu.SemaphoreType.DMA((2,))],
    )[0]


def first_product(ordered, core, other, chunk, up_weight, down_weight, name):
    _, rows, features = chunk.shape
    half = up_weight.shape[1] // 2
    tile = tile_of(half)
    pieces = half // tile

    def body(core_ref, chunk_ref, up_hbm, down_hbm, up_ref, down_ref, *refs):
        out_ref, sems = refs[-2:]
        side = 1 - core_ref[0] if other else core_ref[0]
        copies = []
        for i in range(pieces):
            units = pl.ds(pl.multiple_of(side * half + i * tile, tile), tile)
            part = pl.ds(i * tile, tile)
            copies.append(pltpu.make_async_copy(up_hbm.at[:, units], up_ref.at[:, part], sems.at[0, i]))
            copies.append(pltpu.make_async_copy(down_hbm.at[units, :], down_ref.at[part, :], sems.at[1, i]))
        for copy in copies:
            copy.start()
        if not other:
            refs[0][...] = chunk_ref[...]
        for i in range(pieces):
            part = slice(i * tile, (i + 1) * tile)
            copies[2 * i].wait()
            out_ref[0, :, part] = dot(chunk_ref[0], up_ref[:, part], NN).astype(BF16)
            copies[2 * i + 1].wait()
            out_ref[1, :, part] = dot(chunk_ref[1], down_ref[part, :], NT).astype(BF16)

    outs = [VMEM((features, half), BF16), VMEM((half, features), BF16)]
    outs += [] if other else [jax.ShapeDtypeStruct(chunk.shape, BF16)]
    return ordered(
        body,
        (core, chunk, in_hbm(up_weight), in_hbm(down_weight)),
        outs + [jax.ShapeDtypeStruct((2, rows, half), BF16)],
        name,
        4.5,
        spaces=[None, None, pl.ANY, pl.ANY],
        scratch=[pltpu.SemaphoreType.DMA((2, pieces))],
    )


def product(ordered, chunk, up_half, down_half, name, after=()):
    _, rows, features = chunk.shape
    half = up_half.shape[1]
    tile = tile_of(half)

    def body(chunk_ref, up_ref, down_ref, out_ref):
        for start in range(0, half, tile):
            part = slice(start, start + tile)
            out_ref[0, :, part] = dot(chunk_ref[0], up_ref[:, part], NN).astype(BF16)
            out_ref[1, :, part] = dot(chunk_ref[1], down_ref[part, :], NT).astype(BF16)

    args = (chunk, in_vmem(up_half), in_vmem(down_half))
    return ordered(body, args, [jax.ShapeDtypeStruct((2, rows, half), BF16)], name, 2.4, after=after)[0]


def product_terms(terms, part):
    share = None
    for act, up_ref, low in terms:
        term = dot(act, up_ref[part, low : low + act.shape[1]], NT)
        share = term if share is None else share + term
    return share


def grad_of(ref):
    return ref[...] if len(ref.shape) == 2 else ref[0]


def input_product(ordered, rows, terms, micros, partial=None, returned=()):
    features = terms[0][1].shape[0]
    tile = tile_of(features)
    count = len(terms)
    chunks = terms[0][0].shape[-2] // rows

    def body(*refs):
        filled = [(grad_of(refs[i]), refs[count + i], low) for i, (_, _, low) in enumerate(terms)]
        returned_refs, out_refs = refs[2 * count :][: len(returned)], refs[-chunks:]
        if returned:
            total = returned_refs[0][...].astype(F32)
            for ref in returned_refs[1:]:
                total = total + ref[...].astype(F32)
            refs[-chunks - 1][...] = total
        for start in range(0, features, tile):
            part = slice(start, start + tile)
            share = product_terms(filled, part)
            if partial is not None:
                share = share + refs[2 * count + len(returned)][:, part]
            for c, out_ref in enumerate(out_refs):
                out_ref[:, part] = share[c * rows : (c + 1) * rows].astype(BF16)

    args = [act for act, _, _ in terms] + [in_vmem(weight) for _, weight, _ in terms]
    args += [*returned, *([] if partial is None else [partial])]
    outs = [jax.ShapeDtypeStruct((rows, features), F32)] if returned else []
    return ordered(body, args, outs + [jax.ShapeDtypeStruct((rows, features), BF16)] * chunks, "input_product", micros)


def gelu(ordered, sums, apart=False):
    flat = [a for pair in sums for a in pair]
    _, rows, units = flat[0].shape

    def body(*refs):
        grad_ref, value_ref = refs[-2:] if apart else (refs[-1].at[0], refs[-1].at[1])
        for chunk in range(len(sums)):
            at = slice(chunk * rows, (chunk + 1) * rows)
            own_h, own_g, peer_h, peer_g = [refs[2 * chunk + side][i].astype(F32) for side in (0, 1) for i in (0, 1)]
            hidden, grad_hidden = own_h + peer_h, own_g + peer_g
            cdf = 0.5 * (1.0 + lax.erf(hidden * 0.7071067811865476))
            pdf = jnp.exp(-0.5 * hidden * hidden) * 0.3989422804014327
            grad_ref[at] = (grad_hidden * (cdf + hidden * pdf)).astype(BF16)
            value_ref[at] = (hidden * cdf).astype(BF16)

    outs = [jax.ShapeDtypeStruct((rows * len(sums), units), BF16)] * 2
    if not apart:
        outs = [jax.ShapeDtypeStruct((2, rows * len(sums), units), BF16)]
    return ordered(body, flat, outs, "gelu", 0.1)


def collect(ordered, chunks, after):
    count = len(chunks)
    _, rows, features = chunks[0].shape
    tile = tile_of(features, 256)

    def body(*refs):
        turned_ref, grads_ref, scratch = refs[count:]
        for i in range(count):
            scratch[i * rows : (i + 1) * rows, :] = refs[i][0]
            grads_ref[i * rows : (i + 1) * rows, :] = refs[i][1]
        for start in range(0, features, tile):
            turned_ref[start : start + tile, :] = scratch[:, start : start + tile].T

    outs = [VMEM((features, rows * count), BF16), VMEM((rows * count, features), BF16)]
    return ordered(body, chunks, outs, "collect", 0.1, scratch=[VMEM((rows * count, features), BF16)], after=after)


def weight_grads(ordered, core, blocks, turned, all_grads, half, scale, before, name, share=None):
    features, tokens = turned.shape
    width = min(a[0].shape[-1] for a, _ in blocks[0][2])
    up_tile, down_tile = tile_of(features), tile_of(width, 256)
    up_steps, down_steps = features // up_tile, width // down_tile
    slots = 3
    flat = [a for block in blocks for acts, _ in block[2] for a in acts]

    def body(core_ref, turned_ref, grads_ref, *refs):
        up_hbm, down_hbm = refs[outs_at : outs_at + 2]
        done_ref, act_g, act_v, up_stage, down_stage, sems = refs[-6:]
        done_ref[...] = jnp.zeros_like(done_ref)
        busy = {}

        def send(kind, index, value, stage, target):
            slot = index % slots
            if (kind, slot) in busy:
                busy[kind, slot].wait()
            stage[slot] = value * scale
            copy = pltpu.make_async_copy(stage.at[slot], target, sems.at[kind, slot])
            copy.start()
            busy[kind, slot] = copy

        left = refs[: len(flat)]
        for b, (other, first, acts) in enumerate(blocks):
            side = 1 - core_ref[0] if other else core_ref[0]
            base = side * half + first
            row = 0
            for arrays, column in acts:
                rows = slice(row, row + arrays[0].shape[-2])
                columns = slice(column, column + width)
                taken, left = left[: len(arrays)], left[len(arrays) :]
                act_g[rows, :] = taken[0][:, columns] if len(taken) == 2 else taken[0][0, :, columns]
                act_v[rows, :] = taken[1][:, columns] if len(taken) == 2 else taken[0][1, :, columns]
                row += arrays[0].shape[-2]
            for step in range(max(up_steps, down_steps)):
                if step < up_steps:
                    part = slice(step * up_tile, (step + 1) * up_tile)
                    value = dot(turned_ref[part, :], act_g[...], NN)
                    target = up_hbm.at[pl.ds(step * up_tile, up_tile), pl.ds(pl.multiple_of(base, 128), width)]
                    send(0, b * up_steps + step, value, up_stage, target)
                if step < down_steps:
                    part = slice(step * down_tile, (step + 1) * down_tile)
                    value = dot(act_v[:, part], grads_ref[...], TN)
                    target = down_hbm.at[pl.ds(pl.multiple_of(base + step * down_tile, 128), down_tile), :]
                    send(1, b * down_steps + step, value, down_stage, target)
                if share is not None and b == 0 and step < up_steps:
                    part = slice(step * up_tile, (step + 1) * up_tile)
                    terms = [
                        (grad_of(refs[len(flat) + i]), refs[len(flat) + len(share[0]) + i], low)
                        for i, (_, _, low) in enumerate(share[0])
                    ]
                    refs[outs_at + 2][:, part] = product_terms(terms, part).astype(share[1])
        for copy in busy.values():
            copy.wait()

    args = [core, turned, all_grads, *flat]
    outs = [pltpu.HBM((features, 2 * half), F32), pltpu.HBM((2 * half, features), F32)]
    if share is not None:
        terms, kind = share
        args += [act for act, _, _ in terms] + [in_vmem(weight) for _, weight, _ in terms]
        outs.append(jax.ShapeDtypeStruct((terms[0][0].shape[-2], features), kind))
    spaces = [None] * len(args)
    outs_at = len(args) - 3 + (0 if before is None else 2)
    aliases = {}
    if before is not None:
        aliases = {len(args): 0, len(args) + 1: 1}
        args += [in_hbm(a) for a in before]
        spaces += [pl.ANY, pl.ANY]
    return ordered(
        body,
        args,
        [*outs, jax.ShapeDtypeStruct((8, 128), F32)],
        name,
        4.0 * len(blocks),
        spaces=spaces,
        out_spaces=[pl.ANY, pl.ANY] + [VMEM] * (len(outs) - 1),
        scratch=[
            VMEM((tokens, width), BF16),
            VMEM((tokens, width), BF16),
            VMEM((slots, up_tile, width), F32),
            VMEM((slots, down_tile, features), F32),
            pltpu.SemaphoreType.DMA((2, slots)),
        ],
        aliases=aliases,
    )


def per_device(wide, narrow, inputs, up_weight, down_weight, out_grad):
    rows = inputs.shape[0]
    half = up_weight.shape[1] // 2
    chips = wide // 2
    core = (lax.axis_index("wide") & 1).astype(jnp.int32).reshape(1)
    ordered = Ordered()

    def swap_cores(x):
        return lax.ppermute(x, "wide", [(i, i ^ 1) for i in range(wide)])

    ring = [*range(0, narrow, 2), *range(narrow - 1, 0, -2)]

    def shift(x, places):
        return lax.ppermute(x, "narrow", [(ring[i], ring[(i + places) % narrow]) for i in range(narrow)])

    def across_chips(keep, got):
        partial = (keep.astype(F32) + got.astype(F32)).astype(BF16)
        hop = 1
        while True:
            peer = lax.ppermute(partial, "wide", [(i, i ^ (2 * hop)) for i in range(wide)])
            hop *= 2
            if hop >= chips:
                return partial, peer
            partial = (partial.astype(F32) + peer.astype(F32)).astype(BF16)

    offsets = sorted(range(narrow // 2 - narrow + 1, narrow // 2 + 1), key=lambda places: (abs(places), -places))
    chunks = {0: stacked(ordered, inputs, out_grad)}

    up_other, down_other, give = first_product(ordered, core, True, chunks[0], up_weight, down_weight, "give_first")
    got = swap_cores(give)
    up_mine, down_mine, sent_back, keep = first_product(ordered, core, False, chunks[0], up_weight, down_weight, "keep_first")
    sums = [across_chips(keep, got)]

    def acts_of(sums, apart=False):
        mine = gelu(ordered, sums, apart)
        return mine, [swap_cores(a) for a in mine]

    slices = 2 if half % 256 == 0 else 1
    width = half // slices
    for offset in offsets[1:]:
        places = 1 if offset > 0 else -1
        chunk = chunks[offset] = shift(sent_back if offset == -1 else chunks[offset - places], places)
        give = product(ordered, chunk, up_other, down_other, "give", after=[sums[-1][0]] + [sums[0][1]] * (len(sums) == 2))
        got = swap_cores(give)
        if offset == offsets[-1]:
            early = acts_of(sums[:-1])
        keep = product(ordered, chunk, up_mine, down_mine, "keep")
        if offset != offsets[-1]:
            sums.append(across_chips(keep, got))
        else:
            parts = [slice(i * width, (i + 1) * width) for i in range(slices)]
            late = [across_chips(keep[:, :, part], got[:, :, part]) for part in parts]

    turned, all_grads = collect(ordered, [chunks[offset] for offset in offsets], [own for own, _ in late])
    both = (up_mine, up_other)
    shares = input_product(ordered, rows, [(early[side][0], both[side], 0) for side in (0, 1)], 0.1)
    shares = [share if offset == 0 else shift(share, -offset) for offset, share in zip(offsets, shares)]
    middle = acts_of(sums[-1:], True)

    scale = (rows * narrow) ** -0.5
    late_acts = []

    def grads(places, before, share):
        blocks = [
            (side, i * width, [(early[side], i * width), (middle[side], i * width), (late_acts[i][side], 0)])
            for side, i in places
        ]
        return weight_grads(ordered, core, blocks, turned, all_grads, half, scale, before, "weight_grads", share)

    late_acts.append(acts_of(late[:1]))
    up_grad, down_grad, share, _ = grads([(0, 0)], None, ([(middle[side][0], both[side], 0) for side in (0, 1)], BF16))
    middle_share = shift(share, -offsets[-2])
    partial = None
    terms = [(late_acts[0][side][0], both[side], 0) for side in (0, 1)]
    if slices > 1:
        late_acts.append(acts_of(late[1:]))
        terms.append((late_acts[1][0][0], up_mine, width))
        up_grad, down_grad, partial, _ = grads([(1, 0)], (up_grad, down_grad), (terms, F32))
        terms = [(late_acts[1][1][0], up_other, width)]
    so_far, share = input_product(ordered, rows, terms, 3.0, partial, shares)
    share = shift(share, -offsets[-1])
    last = [(0, 1), (1, 1)] if slices > 1 else [(1, 0)]
    up_grad, down_grad, _ = grads(last, (up_grad, down_grad), None)
    return (so_far + middle_share.astype(F32) + share.astype(F32)).astype(BF16), up_grad, down_grad


def solution(mesh):
    placed = (
        P(("groups", "narrow"), "wide"),
        P("wide", "narrow"),
        P("narrow", "wide"),
        P(("groups", "narrow"), "wide"),
    )
    return jax.shard_map(
        functools.partial(per_device, mesh.shape["wide"], mesh.shape["narrow"]),
        mesh=mesh,
        in_specs=placed,
        out_specs=(
            P(("groups", "narrow"), "wide"),
            P(("groups", "wide"), "narrow"),
            P(("groups", "narrow"), "wide"),
        ),
        check_vma=False,
    )
```

```python
import functools

import jax
import jax.numpy as jnp
from jax import lax
from jax.experimental import pallas as pl
from jax.experimental.pallas import tpu as pltpu
from jax.sharding import PartitionSpec as P

F32, BF16 = jnp.float32, jnp.bfloat16
MIB = 1 << 20
VMEM = pltpu.VMEM
NN = (((1,), (0,)), ((), ()))
NT = (((1,), (1,)), ((), ()))
TN = (((0,), (0,)), ((), ()))


def dot(a, b, dims):
    return lax.dot_general(a, b, dims, preferred_element_type=F32)


def in_vmem(x):
    return pltpu.with_memory_space_constraint(x, VMEM)


def in_hbm(x):
    return pltpu.with_memory_space_constraint(x, pltpu.HBM)


def tile_of(extent, largest=512):
    return next(t for t in (768, 512, 384, 256, 128) if t <= largest and extent % t == 0)


class Ordered:
    def __init__(self):
        self.last = None

    def __call__(self, body, args, outs, name, micros, limit=16, spaces=None, out_spaces=None, scratch=(), aliases=None, after=()):
        args = list(args)
        spaces = spaces or [None] * len(args)
        specs = [
            pl.BlockSpec(memory_space=pltpu.SMEM if a.dtype == jnp.int32 else space or VMEM) for a, space in zip(args, spaces)
        ]
        count = len(args)
        for waited in (*after, *([] if self.last is None else [self.last])):
            args.append(waited)
            specs.append(pl.BlockSpec(memory_space=pl.ANY))
        extra = len(args) - count

        def kernel(*refs):
            body(*refs[:count], *refs[count + extra :])

        result = pl.pallas_call(
            kernel,
            out_shape=outs,
            in_specs=specs,
            out_specs=[pl.BlockSpec(memory_space=s) for s in out_spaces or [VMEM] * len(outs)],
            scratch_shapes=scratch,
            input_output_aliases=aliases or {},
            compiler_params=pltpu.CompilerParams(vmem_limit_bytes=limit * MIB),
            cost_estimate=pl.CostEstimate(flops=int(micros * 4e9), bytes_accessed=0, transcendentals=0),
            name=name,
        )(*args)
        self.last = result[-1]
        return result


def stacked(ordered, inputs, out_grad):
    def body(inputs_hbm, grads_hbm, out_ref, sems):
        copies = [
            pltpu.make_async_copy(source, out_ref.at[i], sems.at[i]) for i, source in enumerate((inputs_hbm, grads_hbm))
        ]
        for copy in copies:
            copy.start()
        for copy in copies:
            copy.wait()

    return ordered(
        body,
        (in_hbm(inputs), in_hbm(out_grad)),
        [VMEM((2, *inputs.shape), BF16)],
        "stacked",
        0.5,
        spaces=[pl.ANY, pl.ANY],
        scratch=[pltpu.SemaphoreType.DMA((2,))],
    )[0]


def copied(ordered, chunk):
    def body(chunk_ref, out_ref):
        out_ref[...] = chunk_ref[...]

    return ordered(body, (chunk,), [jax.ShapeDtypeStruct(chunk.shape, BF16)], "copied", 0.1)[0]


def first_product(ordered, core, other, chunk, up_weight, down_weight, name):
    _, rows, features = chunk.shape
    half = up_weight.shape[1] // 2
    tile = tile_of(half)
    pieces = half // tile

    def body(core_ref, chunk_ref, up_hbm, down_hbm, up_ref, down_ref, *refs):
        out_ref, sems = refs[-2:]
        side = 1 - core_ref[0] if other else core_ref[0]
        copies = []
        for i in range(pieces):
            units = pl.ds(pl.multiple_of(side * half + i * tile, tile), tile)
            part = pl.ds(i * tile, tile)
            copies.append(pltpu.make_async_copy(up_hbm.at[:, units], up_ref.at[:, part], sems.at[0, i]))
            copies.append(pltpu.make_async_copy(down_hbm.at[units, :], down_ref.at[part, :], sems.at[1, i]))
        for copy in copies:
            copy.start()
        if not other:
            refs[0][...] = chunk_ref[...]
        for i in range(pieces):
            part = slice(i * tile, (i + 1) * tile)
            copies[2 * i].wait()
            out_ref[0, :, part] = dot(chunk_ref[0], up_ref[:, part], NN).astype(BF16)
            copies[2 * i + 1].wait()
            out_ref[1, :, part] = dot(chunk_ref[1], down_ref[part, :], NT).astype(BF16)

    outs = [VMEM((features, half), BF16), VMEM((half, features), BF16)]
    outs += [] if other else [jax.ShapeDtypeStruct(chunk.shape, BF16)]
    return ordered(
        body,
        (core, chunk, in_hbm(up_weight), in_hbm(down_weight)),
        outs + [jax.ShapeDtypeStruct((2, rows, half), BF16)],
        name,
        4.5,
        spaces=[None, None, pl.ANY, pl.ANY],
        scratch=[pltpu.SemaphoreType.DMA((2, pieces))],
    )


def product(ordered, chunk, up_half, down_half, name, after=()):
    _, rows, features = chunk.shape
    half = up_half.shape[1]
    tile = tile_of(half)

    def body(chunk_ref, up_ref, down_ref, out_ref):
        for start in range(0, half, tile):
            part = slice(start, start + tile)
            out_ref[0, :, part] = dot(chunk_ref[0], up_ref[:, part], NN).astype(BF16)
            out_ref[1, :, part] = dot(chunk_ref[1], down_ref[part, :], NT).astype(BF16)

    args = (chunk, in_vmem(up_half), in_vmem(down_half))
    return ordered(body, args, [jax.ShapeDtypeStruct((2, rows, half), BF16)], name, 2.4, after=after)[0]


def product_terms(terms, part):
    share = None
    for act, up_ref, low in terms:
        term = dot(act, up_ref[part, low : low + act.shape[1]], NT)
        share = term if share is None else share + term
    return share


def grad_of(ref):
    return ref[...] if len(ref.shape) == 2 else ref[0]


def input_product(ordered, rows, terms, micros, partial=None, returned=()):
    features = terms[0][1].shape[0]
    tile = tile_of(features)
    count = len(terms)
    chunks = terms[0][0].shape[-2] // rows

    def body(*refs):
        filled = [(grad_of(refs[i]), refs[count + i], low) for i, (_, _, low) in enumerate(terms)]
        returned_refs, out_refs = refs[2 * count :][: len(returned)], refs[-chunks:]
        if returned:
            total = returned_refs[0][...].astype(F32)
            for ref in returned_refs[1:]:
                total = total + ref[...].astype(F32)
            refs[-chunks - 1][...] = total
        for start in range(0, features, tile):
            part = slice(start, start + tile)
            share = product_terms(filled, part)
            if partial is not None:
                share = share + refs[2 * count + len(returned)][:, part]
            for c, out_ref in enumerate(out_refs):
                out_ref[:, part] = share[c * rows : (c + 1) * rows].astype(BF16)

    args = [act for act, _, _ in terms] + [in_vmem(weight) for _, weight, _ in terms]
    args += [*returned, *([] if partial is None else [partial])]
    outs = [jax.ShapeDtypeStruct((rows, features), F32)] if returned else []
    return ordered(body, args, outs + [jax.ShapeDtypeStruct((rows, features), BF16)] * chunks, "input_product", micros)


def gelu(ordered, sums, apart=False):
    flat = [a for pair in sums for a in pair]
    _, rows, units = flat[0].shape

    def body(*refs):
        grad_ref, value_ref = refs[-2:] if apart else (refs[-1].at[0], refs[-1].at[1])
        for chunk in range(len(sums)):
            at = slice(chunk * rows, (chunk + 1) * rows)
            own_h, own_g, peer_h, peer_g = [refs[2 * chunk + side][i].astype(F32) for side in (0, 1) for i in (0, 1)]
            hidden, grad_hidden = own_h + peer_h, own_g + peer_g
            cdf = 0.5 * (1.0 + lax.erf(hidden * 0.7071067811865476))
            pdf = jnp.exp(-0.5 * hidden * hidden) * 0.3989422804014327
            grad_ref[at] = (grad_hidden * (cdf + hidden * pdf)).astype(BF16)
            value_ref[at] = (hidden * cdf).astype(BF16)

    outs = [jax.ShapeDtypeStruct((rows * len(sums), units), BF16)] * 2
    if not apart:
        outs = [jax.ShapeDtypeStruct((2, rows * len(sums), units), BF16)]
    return ordered(body, flat, outs, "gelu", 0.1)


def collect(ordered, chunks, after):
    count = len(chunks)
    _, rows, features = chunks[0].shape
    tile = tile_of(features, 256)

    def body(*refs):
        turned_ref, grads_ref, scratch = refs[count:]
        for i in range(count):
            scratch[i * rows : (i + 1) * rows, :] = refs[i][0]
            grads_ref[i * rows : (i + 1) * rows, :] = refs[i][1]
        for start in range(0, features, tile):
            turned_ref[start : start + tile, :] = scratch[:, start : start + tile].T

    outs = [VMEM((features, rows * count), BF16), VMEM((rows * count, features), BF16)]
    return ordered(body, chunks, outs, "collect", 0.1, scratch=[VMEM((rows * count, features), BF16)], after=after)


def weight_grads(ordered, core, blocks, turned, all_grads, half, scale, before, name, share=None):
    features, tokens = turned.shape
    width = min(a[0].shape[-1] for a, _ in blocks[0][2])
    up_tile, down_tile = tile_of(features), tile_of(width, 256)
    up_steps, down_steps = features // up_tile, width // down_tile
    slots = 3
    flat = [a for block in blocks for acts, _ in block[2] for a in acts]

    def body(core_ref, turned_ref, grads_ref, *refs):
        up_hbm, down_hbm = refs[outs_at : outs_at + 2]
        done_ref, act_g, act_v, up_stage, down_stage, sems = refs[-6:]
        done_ref[...] = jnp.zeros_like(done_ref)
        busy = {}

        def send(kind, index, value, stage, target):
            slot = index % slots
            if (kind, slot) in busy:
                busy[kind, slot].wait()
            stage[slot] = value * scale
            copy = pltpu.make_async_copy(stage.at[slot], target, sems.at[kind, slot])
            copy.start()
            busy[kind, slot] = copy

        left = refs[: len(flat)]
        for b, (other, first, acts) in enumerate(blocks):
            side = 1 - core_ref[0] if other else core_ref[0]
            base = side * half + first
            row = 0
            for arrays, column in acts:
                rows = slice(row, row + arrays[0].shape[-2])
                columns = slice(column, column + width)
                taken, left = left[: len(arrays)], left[len(arrays) :]
                act_g[rows, :] = taken[0][:, columns] if len(taken) == 2 else taken[0][0, :, columns]
                act_v[rows, :] = taken[1][:, columns] if len(taken) == 2 else taken[0][1, :, columns]
                row += arrays[0].shape[-2]
            for step in range(max(up_steps, down_steps)):
                if step < up_steps:
                    part = slice(step * up_tile, (step + 1) * up_tile)
                    value = dot(turned_ref[part, :], act_g[...], NN)
                    target = up_hbm.at[pl.ds(step * up_tile, up_tile), pl.ds(pl.multiple_of(base, 128), width)]
                    send(0, b * up_steps + step, value, up_stage, target)
                if step < down_steps:
                    part = slice(step * down_tile, (step + 1) * down_tile)
                    value = dot(act_v[:, part], grads_ref[...], TN)
                    target = down_hbm.at[pl.ds(pl.multiple_of(base + step * down_tile, 128), down_tile), :]
                    send(1, b * down_steps + step, value, down_stage, target)
                if share is not None and b == 0 and step < up_steps:
                    part = slice(step * up_tile, (step + 1) * up_tile)
                    terms = [
                        (grad_of(refs[len(flat) + i]), refs[len(flat) + len(share[0]) + i], low)
                        for i, (_, _, low) in enumerate(share[0])
                    ]
                    refs[outs_at + 2][:, part] = product_terms(terms, part).astype(share[1])
        for copy in busy.values():
            copy.wait()

    args = [core, turned, all_grads, *flat]
    outs = [pltpu.HBM((features, 2 * half), F32), pltpu.HBM((2 * half, features), F32)]
    if share is not None:
        terms, kind = share
        args += [act for act, _, _ in terms] + [in_vmem(weight) for _, weight, _ in terms]
        outs.append(jax.ShapeDtypeStruct((terms[0][0].shape[-2], features), kind))
    spaces = [None] * len(args)
    outs_at = len(args) - 3 + (0 if before is None else 2)
    aliases = {}
    if before is not None:
        aliases = {len(args): 0, len(args) + 1: 1}
        args += [in_hbm(a) for a in before]
        spaces += [pl.ANY, pl.ANY]
    return ordered(
        body,
        args,
        [*outs, jax.ShapeDtypeStruct((8, 128), F32)],
        name,
        4.0 * len(blocks),
        spaces=spaces,
        out_spaces=[pl.ANY, pl.ANY] + [VMEM] * (len(outs) - 1),
        scratch=[
            VMEM((tokens, width), BF16),
            VMEM((tokens, width), BF16),
            VMEM((slots, up_tile, width), F32),
            VMEM((slots, down_tile, features), F32),
            pltpu.SemaphoreType.DMA((2, slots)),
        ],
        aliases=aliases,
    )


def per_device(wide, narrow, inputs, up_weight, down_weight, out_grad):
    rows = inputs.shape[0]
    half = up_weight.shape[1] // 2
    chips = wide // 2
    core = (lax.axis_index("wide") & 1).astype(jnp.int32).reshape(1)
    ordered = Ordered()

    def swap_cores(x):
        return lax.ppermute(x, "wide", [(i, i ^ 1) for i in range(wide)])

    ring = [*range(0, narrow, 2), *range(narrow - 1, 0, -2)]

    def shift(x, places):
        return lax.ppermute(x, "narrow", [(ring[i], ring[(i + places) % narrow]) for i in range(narrow)])

    def across_chips(keep, got):
        partial = (keep.astype(F32) + got.astype(F32)).astype(BF16)
        hop = 1
        while True:
            peer = lax.ppermute(partial, "wide", [(i, i ^ (2 * hop)) for i in range(wide)])
            hop *= 2
            if hop >= chips:
                return partial, peer
            partial = (partial.astype(F32) + peer.astype(F32)).astype(BF16)

    offsets = sorted(range(narrow // 2 - narrow + 1, narrow // 2 + 1), key=lambda places: (abs(places), -places))
    chunks = {0: stacked(ordered, inputs, out_grad)}

    up_other, down_other, give = first_product(ordered, core, True, chunks[0], up_weight, down_weight, "give_first")
    got = swap_cores(give)
    up_mine, down_mine, sent_back, keep = first_product(ordered, core, False, chunks[0], up_weight, down_weight, "keep_first")
    sums = [across_chips(keep, got)]
    forward = {-1: sent_back}

    def acts_of(sums, apart=False):
        mine = gelu(ordered, sums, apart)
        return mine, [swap_cores(a) for a in mine]

    slices = 2 if half % 256 == 0 else 1
    width = half // slices
    for offset in offsets[1:]:
        places = 1 if offset > 0 else -1
        chunk = chunks[offset] = shift(forward.get(offset, chunks[offset - places]), places)
        give = product(ordered, chunk, up_other, down_other, "give", after=[sums[-1][0]] + [sums[0][1]] * (len(sums) == 2))
        got = swap_cores(give)
        if offset == offsets[-1]:
            early = acts_of(sums[:-1])
        keep = product(ordered, chunk, up_mine, down_mine, "keep")
        if offset == 1:
            forward[2] = copied(ordered, chunk)
        if offset != offsets[-1]:
            sums.append(across_chips(keep, got))
        else:
            parts = [slice(i * width, (i + 1) * width) for i in range(slices)]
            late = [across_chips(keep[:, :, part], got[:, :, part]) for part in parts]

    turned, all_grads = collect(ordered, [chunks[offset] for offset in offsets], [own for own, _ in late])
    both = (up_mine, up_other)
    shares = input_product(ordered, rows, [(early[side][0], both[side], 0) for side in (0, 1)], 0.1)
    shares = [share if offset == 0 else shift(share, -offset) for offset, share in zip(offsets, shares)]
    middle = acts_of(sums[-1:], True)

    scale = (rows * narrow) ** -0.5
    late_acts = []

    def grads(places, before, share):
        blocks = [
            (side, i * width, [(early[side], i * width), (middle[side], i * width), (late_acts[i][side], 0)])
            for side, i in places
        ]
        return weight_grads(ordered, core, blocks, turned, all_grads, half, scale, before, "weight_grads", share)

    late_acts.append(acts_of(late[:1]))
    up_grad, down_grad, share, _ = grads([(0, 0)], None, ([(middle[side][0], both[side], 0) for side in (0, 1)], BF16))
    middle_share = shift(share, -offsets[-2])
    partial = None
    terms = [(late_acts[0][side][0], both[side], 0) for side in (0, 1)]
    if slices > 1:
        late_acts.append(acts_of(late[1:]))
        terms.append((late_acts[1][0][0], up_mine, width))
        up_grad, down_grad, partial, _ = grads([(1, 0)], (up_grad, down_grad), (terms, F32))
        terms = [(late_acts[1][1][0], up_other, width)]
    so_far, share = input_product(ordered, rows, terms, 3.0, partial, shares)
    share = shift(share, -offsets[-1])
    last = [(0, 1), (1, 1)] if slices > 1 else [(1, 0)]
    up_grad, down_grad, _ = grads(last, (up_grad, down_grad), None)
    return (so_far + middle_share.astype(F32) + share.astype(F32)).astype(BF16), up_grad, down_grad


def solution(mesh):
    placed = (
        P(("groups", "narrow"), "wide"),
        P("wide", "narrow"),
        P("narrow", "wide"),
        P(("groups", "narrow"), "wide"),
    )
    return jax.shard_map(
        functools.partial(per_device, mesh.shape["wide"], mesh.shape["narrow"]),
        mesh=mesh,
        in_specs=placed,
        out_specs=(
            P(("groups", "narrow"), "wide"),
            P(("groups", "wide"), "narrow"),
            P(("groups", "narrow"), "wide"),
        ),
        check_vma=False,
    )
```

```python
import functools

import jax
import jax.numpy as jnp
from jax import lax
from jax.experimental import pallas as pl
from jax.experimental.pallas import tpu as pltpu
from jax.sharding import PartitionSpec as P

F32, BF16 = jnp.float32, jnp.bfloat16
MIB = 1 << 20
VMEM = pltpu.VMEM
NN = (((1,), (0,)), ((), ()))
NT = (((1,), (1,)), ((), ()))
TN = (((0,), (0,)), ((), ()))


def dot(a, b, dims):
    return lax.dot_general(a, b, dims, preferred_element_type=F32)


def in_vmem(x):
    return pltpu.with_memory_space_constraint(x, VMEM)


def in_hbm(x):
    return pltpu.with_memory_space_constraint(x, pltpu.HBM)


def tile_of(extent, largest=512):
    return next(t for t in (768, 512, 384, 256, 128) if t <= largest and extent % t == 0)


class Ordered:
    def __init__(self):
        self.last = None

    def __call__(self, body, args, outs, name, micros, limit=16, spaces=None, out_spaces=None, scratch=(), aliases=None, after=()):
        args = list(args)
        spaces = spaces or [None] * len(args)
        specs = [
            pl.BlockSpec(memory_space=pltpu.SMEM if a.dtype == jnp.int32 else space or VMEM) for a, space in zip(args, spaces)
        ]
        count = len(args)
        for waited in (*after, *([] if self.last is None else [self.last])):
            args.append(waited)
            specs.append(pl.BlockSpec(memory_space=pl.ANY))
        extra = len(args) - count

        def kernel(*refs):
            body(*refs[:count], *refs[count + extra :])

        result = pl.pallas_call(
            kernel,
            out_shape=outs,
            in_specs=specs,
            out_specs=[pl.BlockSpec(memory_space=s) for s in out_spaces or [VMEM] * len(outs)],
            scratch_shapes=scratch,
            input_output_aliases=aliases or {},
            compiler_params=pltpu.CompilerParams(vmem_limit_bytes=limit * MIB),
            cost_estimate=pl.CostEstimate(flops=int(micros * 4e9), bytes_accessed=0, transcendentals=0),
            name=name,
        )(*args)
        self.last = result[-1]
        return result


def stacked(ordered, inputs, out_grad):
    def body(inputs_hbm, grads_hbm, out_ref, sems):
        copies = [
            pltpu.make_async_copy(source, out_ref.at[i], sems.at[i]) for i, source in enumerate((inputs_hbm, grads_hbm))
        ]
        for copy in copies:
            copy.start()
        for copy in copies:
            copy.wait()

    return ordered(
        body,
        (in_hbm(inputs), in_hbm(out_grad)),
        [VMEM((2, *inputs.shape), BF16)],
        "stacked",
        0.5,
        spaces=[pl.ANY, pl.ANY],
        scratch=[pltpu.SemaphoreType.DMA((2,))],
    )[0]


def copied(ordered, chunk, after):
    def body(chunk_ref, out_ref):
        out_ref[...] = chunk_ref[...]

    return ordered(body, (chunk,), [jax.ShapeDtypeStruct(chunk.shape, BF16)], "copied", 0.1, after=after)[0]


def first_product(ordered, core, other, chunk, up_weight, down_weight, name):
    _, rows, features = chunk.shape
    half = up_weight.shape[1] // 2
    tile = tile_of(half)
    pieces = half // tile

    def body(core_ref, chunk_ref, up_hbm, down_hbm, up_ref, down_ref, *refs):
        out_ref, sems = refs[-2:]
        side = 1 - core_ref[0] if other else core_ref[0]
        copies = []
        for i in range(pieces):
            units = pl.ds(pl.multiple_of(side * half + i * tile, tile), tile)
            part = pl.ds(i * tile, tile)
            copies.append(pltpu.make_async_copy(up_hbm.at[:, units], up_ref.at[:, part], sems.at[0, i]))
            copies.append(pltpu.make_async_copy(down_hbm.at[units, :], down_ref.at[part, :], sems.at[1, i]))
        for copy in copies:
            copy.start()
        if not other:
            refs[0][...] = chunk_ref[...]
        for i in range(pieces):
            part = slice(i * tile, (i + 1) * tile)
            copies[2 * i].wait()
            out_ref[0, :, part] = dot(chunk_ref[0], up_ref[:, part], NN).astype(BF16)
            copies[2 * i + 1].wait()
            out_ref[1, :, part] = dot(chunk_ref[1], down_ref[part, :], NT).astype(BF16)

    outs = [VMEM((features, half), BF16), VMEM((half, features), BF16)]
    outs += [] if other else [jax.ShapeDtypeStruct(chunk.shape, BF16)]
    return ordered(
        body,
        (core, chunk, in_hbm(up_weight), in_hbm(down_weight)),
        outs + [jax.ShapeDtypeStruct((2, rows, half), BF16)],
        name,
        4.5,
        spaces=[None, None, pl.ANY, pl.ANY],
        scratch=[pltpu.SemaphoreType.DMA((2, pieces))],
    )


def product(ordered, chunk, up_half, down_half, name, after=()):
    _, rows, features = chunk.shape
    half = up_half.shape[1]
    tile = tile_of(half)

    def body(chunk_ref, up_ref, down_ref, out_ref):
        for start in range(0, half, tile):
            part = slice(start, start + tile)
            out_ref[0, :, part] = dot(chunk_ref[0], up_ref[:, part], NN).astype(BF16)
            out_ref[1, :, part] = dot(chunk_ref[1], down_ref[part, :], NT).astype(BF16)

    args = (chunk, in_vmem(up_half), in_vmem(down_half))
    return ordered(body, args, [jax.ShapeDtypeStruct((2, rows, half), BF16)], name, 2.4, after=after)[0]


def product_terms(terms, part):
    share = None
    for act, up_ref, low in terms:
        term = dot(act, up_ref[part, low : low + act.shape[1]], NT)
        share = term if share is None else share + term
    return share


def grad_of(ref):
    return ref[...] if len(ref.shape) == 2 else ref[0]


def input_product(ordered, rows, terms, micros, partial=None, returned=()):
    features = terms[0][1].shape[0]
    tile = tile_of(features)
    count = len(terms)
    chunks = terms[0][0].shape[-2] // rows

    def body(*refs):
        filled = [(grad_of(refs[i]), refs[count + i], low) for i, (_, _, low) in enumerate(terms)]
        returned_refs, out_refs = refs[2 * count :][: len(returned)], refs[-chunks:]
        if returned:
            total = returned_refs[0][...].astype(F32)
            for ref in returned_refs[1:]:
                total = total + ref[...].astype(F32)
            refs[-chunks - 1][...] = total
        for start in range(0, features, tile):
            part = slice(start, start + tile)
            share = product_terms(filled, part)
            if partial is not None:
                share = share + refs[2 * count + len(returned)][:, part]
            for c, out_ref in enumerate(out_refs):
                out_ref[:, part] = share[c * rows : (c + 1) * rows].astype(BF16)

    args = [act for act, _, _ in terms] + [in_vmem(weight) for _, weight, _ in terms]
    args += [*returned, *([] if partial is None else [partial])]
    outs = [jax.ShapeDtypeStruct((rows, features), F32)] if returned else []
    return ordered(body, args, outs + [jax.ShapeDtypeStruct((rows, features), BF16)] * chunks, "input_product", micros)


def gelu(ordered, sums, apart=False):
    flat = [a for pair in sums for a in pair]
    _, rows, units = flat[0].shape

    def body(*refs):
        grad_ref, value_ref = refs[-2:] if apart else (refs[-1].at[0], refs[-1].at[1])
        for chunk in range(len(sums)):
            at = slice(chunk * rows, (chunk + 1) * rows)
            own_h, own_g, peer_h, peer_g = [refs[2 * chunk + side][i].astype(F32) for side in (0, 1) for i in (0, 1)]
            hidden, grad_hidden = own_h + peer_h, own_g + peer_g
            cdf = 0.5 * (1.0 + lax.erf(hidden * 0.7071067811865476))
            pdf = jnp.exp(-0.5 * hidden * hidden) * 0.3989422804014327
            grad_ref[at] = (grad_hidden * (cdf + hidden * pdf)).astype(BF16)
            value_ref[at] = (hidden * cdf).astype(BF16)

    outs = [jax.ShapeDtypeStruct((rows * len(sums), units), BF16)] * 2
    if not apart:
        outs = [jax.ShapeDtypeStruct((2, rows * len(sums), units), BF16)]
    return ordered(body, flat, outs, "gelu", 0.1)


def collect(ordered, chunks, after):
    count = len(chunks)
    _, rows, features = chunks[0].shape
    tile = tile_of(features, 256)

    def body(*refs):
        turned_ref, grads_ref, scratch = refs[count:]
        for i in range(count):
            scratch[i * rows : (i + 1) * rows, :] = refs[i][0]
            grads_ref[i * rows : (i + 1) * rows, :] = refs[i][1]
        for start in range(0, features, tile):
            turned_ref[start : start + tile, :] = scratch[:, start : start + tile].T

    outs = [VMEM((features, rows * count), BF16), VMEM((rows * count, features), BF16)]
    return ordered(body, chunks, outs, "collect", 0.1, scratch=[VMEM((rows * count, features), BF16)], after=after)


def weight_grads(ordered, core, blocks, turned, all_grads, half, scale, before, name, share=None):
    features, tokens = turned.shape
    width = min(a[0].shape[-1] for a, _ in blocks[0][2])
    up_tile, down_tile = tile_of(features), tile_of(width, 256)
    up_steps, down_steps = features // up_tile, width // down_tile
    slots = 3
    flat = [a for block in blocks for acts, _ in block[2] for a in acts]

    def body(core_ref, turned_ref, grads_ref, *refs):
        up_hbm, down_hbm = refs[outs_at : outs_at + 2]
        done_ref, act_g, act_v, up_stage, down_stage, sems = refs[-6:]
        done_ref[...] = jnp.zeros_like(done_ref)
        busy = {}

        def send(kind, index, value, stage, target):
            slot = index % slots
            if (kind, slot) in busy:
                busy[kind, slot].wait()
            stage[slot] = value * scale
            copy = pltpu.make_async_copy(stage.at[slot], target, sems.at[kind, slot])
            copy.start()
            busy[kind, slot] = copy

        left = refs[: len(flat)]
        for b, (other, first, acts) in enumerate(blocks):
            side = 1 - core_ref[0] if other else core_ref[0]
            base = side * half + first
            row = 0
            for arrays, column in acts:
                rows = slice(row, row + arrays[0].shape[-2])
                columns = slice(column, column + width)
                taken, left = left[: len(arrays)], left[len(arrays) :]
                act_g[rows, :] = taken[0][:, columns] if len(taken) == 2 else taken[0][0, :, columns]
                act_v[rows, :] = taken[1][:, columns] if len(taken) == 2 else taken[0][1, :, columns]
                row += arrays[0].shape[-2]
            for step in range(max(up_steps, down_steps)):
                if step < up_steps:
                    part = slice(step * up_tile, (step + 1) * up_tile)
                    value = dot(turned_ref[part, :], act_g[...], NN)
                    target = up_hbm.at[pl.ds(step * up_tile, up_tile), pl.ds(pl.multiple_of(base, 128), width)]
                    send(0, b * up_steps + step, value, up_stage, target)
                if step < down_steps:
                    part = slice(step * down_tile, (step + 1) * down_tile)
                    value = dot(act_v[:, part], grads_ref[...], TN)
                    target = down_hbm.at[pl.ds(pl.multiple_of(base + step * down_tile, 128), down_tile), :]
                    send(1, b * down_steps + step, value, down_stage, target)
                if share is not None and b == 0 and step < up_steps:
                    part = slice(step * up_tile, (step + 1) * up_tile)
                    terms = [
                        (grad_of(refs[len(flat) + i]), refs[len(flat) + len(share[0]) + i], low)
                        for i, (_, _, low) in enumerate(share[0])
                    ]
                    refs[outs_at + 2][:, part] = product_terms(terms, part).astype(share[1])
        for copy in busy.values():
            copy.wait()

    args = [core, turned, all_grads, *flat]
    outs = [pltpu.HBM((features, 2 * half), F32), pltpu.HBM((2 * half, features), F32)]
    if share is not None:
        terms, kind = share
        args += [act for act, _, _ in terms] + [in_vmem(weight) for _, weight, _ in terms]
        outs.append(jax.ShapeDtypeStruct((terms[0][0].shape[-2], features), kind))
    spaces = [None] * len(args)
    outs_at = len(args) - 3 + (0 if before is None else 2)
    aliases = {}
    if before is not None:
        aliases = {len(args): 0, len(args) + 1: 1}
        args += [in_hbm(a) for a in before]
        spaces += [pl.ANY, pl.ANY]
    return ordered(
        body,
        args,
        [*outs, jax.ShapeDtypeStruct((8, 128), F32)],
        name,
        4.0 * len(blocks),
        spaces=spaces,
        out_spaces=[pl.ANY, pl.ANY] + [VMEM] * (len(outs) - 1),
        scratch=[
            VMEM((tokens, width), BF16),
            VMEM((tokens, width), BF16),
            VMEM((slots, up_tile, width), F32),
            VMEM((slots, down_tile, features), F32),
            pltpu.SemaphoreType.DMA((2, slots)),
        ],
        aliases=aliases,
    )


def per_device(wide, narrow, inputs, up_weight, down_weight, out_grad):
    rows = inputs.shape[0]
    half = up_weight.shape[1] // 2
    chips = wide // 2
    core = (lax.axis_index("wide") & 1).astype(jnp.int32).reshape(1)
    ordered = Ordered()

    def swap_cores(x):
        return lax.ppermute(x, "wide", [(i, i ^ 1) for i in range(wide)])

    ring = [*range(0, narrow, 2), *range(narrow - 1, 0, -2)]

    def shift(x, places):
        return lax.ppermute(x, "narrow", [(ring[i], ring[(i + places) % narrow]) for i in range(narrow)])

    def across_chips(keep, got):
        partial = (keep.astype(F32) + got.astype(F32)).astype(BF16)
        hop = 1
        while True:
            peer = lax.ppermute(partial, "wide", [(i, i ^ (2 * hop)) for i in range(wide)])
            hop *= 2
            if hop >= chips:
                return partial, peer
            partial = (partial.astype(F32) + peer.astype(F32)).astype(BF16)

    offsets = sorted(range(narrow // 2 - narrow + 1, narrow // 2 + 1), key=lambda places: (abs(places), -places))
    chunks = {0: stacked(ordered, inputs, out_grad)}

    up_other, down_other, give = first_product(ordered, core, True, chunks[0], up_weight, down_weight, "give_first")
    got = swap_cores(give)
    up_mine, down_mine, sent_back, keep = first_product(ordered, core, False, chunks[0], up_weight, down_weight, "keep_first")
    sums = [across_chips(keep, got)]
    forward = {-1: sent_back}

    def acts_of(sums, apart=False):
        mine = gelu(ordered, sums, apart)
        return mine, [swap_cores(a) for a in mine]

    slices = 2 if half % 256 == 0 else 1
    width = half // slices
    for offset in offsets[1:]:
        places = 1 if offset > 0 else -1
        chunk = chunks[offset] = shift(forward.get(offset, chunks[offset - places]), places)
        give = product(ordered, chunk, up_other, down_other, "give", after=[sums[-1][0]] + [sums[0][1]] * (len(sums) == 2))
        got = swap_cores(give)
        if offset == offsets[-1]:
            early = acts_of(sums[:-1])
        keep = product(ordered, chunk, up_mine, down_mine, "keep")
        if offset != offsets[-1]:
            sums.append(across_chips(keep, got))
            if offset == 1:
                forward[2] = copied(ordered, chunk, [sums[1][0]])
        else:
            parts = [slice(i * width, (i + 1) * width) for i in range(slices)]
            late = [across_chips(keep[:, :, part], got[:, :, part]) for part in parts]

    turned, all_grads = collect(ordered, [chunks[offset] for offset in offsets], [own for own, _ in late])
    both = (up_mine, up_other)
    shares = input_product(ordered, rows, [(early[side][0], both[side], 0) for side in (0, 1)], 0.1)
    shares = [share if offset == 0 else shift(share, -offset) for offset, share in zip(offsets, shares)]
    middle = acts_of(sums[-1:], True)

    scale = (rows * narrow) ** -0.5
    late_acts = []

    def grads(places, before, share):
        blocks = [
            (side, i * width, [(early[side], i * width), (middle[side], i * width), (late_acts[i][side], 0)])
            for side, i in places
        ]
        return weight_grads(ordered, core, blocks, turned, all_grads, half, scale, before, "weight_grads", share)

    late_acts.append(acts_of(late[:1]))
    up_grad, down_grad, share, _ = grads([(0, 0)], None, ([(middle[side][0], both[side], 0) for side in (0, 1)], BF16))
    middle_share = shift(share, -offsets[-2])
    partial = None
    terms = [(late_acts[0][side][0], both[side], 0) for side in (0, 1)]
    if slices > 1:
        late_acts.append(acts_of(late[1:]))
        terms.append((late_acts[1][0][0], up_mine, width))
        up_grad, down_grad, partial, _ = grads([(1, 0)], (up_grad, down_grad), (terms, F32))
        terms = [(late_acts[1][1][0], up_other, width)]
    so_far, share = input_product(ordered, rows, terms, 3.0, partial, shares)
    share = shift(share, -offsets[-1])
    last = [(0, 1), (1, 1)] if slices > 1 else [(1, 0)]
    up_grad, down_grad, _ = grads(last, (up_grad, down_grad), None)
    return (so_far + middle_share.astype(F32) + share.astype(F32)).astype(BF16), up_grad, down_grad


def solution(mesh):
    placed = (
        P(("groups", "narrow"), "wide"),
        P("wide", "narrow"),
        P("narrow", "wide"),
        P(("groups", "narrow"), "wide"),
    )
    return jax.shard_map(
        functools.partial(per_device, mesh.shape["wide"], mesh.shape["narrow"]),
        mesh=mesh,
        in_specs=placed,
        out_specs=(
            P(("groups", "narrow"), "wide"),
            P(("groups", "wide"), "narrow"),
            P(("groups", "narrow"), "wide"),
        ),
        check_vma=False,
    )
```

```python
import functools

import jax
import jax.numpy as jnp
from jax import lax
from jax.experimental import pallas as pl
from jax.experimental.pallas import tpu as pltpu
from jax.sharding import PartitionSpec as P

F32, BF16 = jnp.float32, jnp.bfloat16
MIB = 1 << 20
VMEM = pltpu.VMEM
NN = (((1,), (0,)), ((), ()))
NT = (((1,), (1,)), ((), ()))
TN = (((0,), (0,)), ((), ()))


def dot(a, b, dims):
    return lax.dot_general(a, b, dims, preferred_element_type=F32)


def in_vmem(x):
    return pltpu.with_memory_space_constraint(x, VMEM)


def in_hbm(x):
    return pltpu.with_memory_space_constraint(x, pltpu.HBM)


def tile_of(extent, largest=512):
    return next(t for t in (768, 512, 384, 256, 128) if t <= largest and extent % t == 0)


class Ordered:
    def __init__(self):
        self.last = None

    def __call__(self, body, args, outs, name, micros, limit=16, spaces=None, out_spaces=None, scratch=(), aliases=None, after=()):
        args = list(args)
        spaces = spaces or [None] * len(args)
        specs = [
            pl.BlockSpec(memory_space=pltpu.SMEM if a.dtype == jnp.int32 else space or VMEM) for a, space in zip(args, spaces)
        ]
        count = len(args)
        for waited in (*after, *([] if self.last is None else [self.last])):
            args.append(waited)
            specs.append(pl.BlockSpec(memory_space=pl.ANY))
        extra = len(args) - count

        def kernel(*refs):
            body(*refs[:count], *refs[count + extra :])

        result = pl.pallas_call(
            kernel,
            out_shape=outs,
            in_specs=specs,
            out_specs=[pl.BlockSpec(memory_space=s) for s in out_spaces or [VMEM] * len(outs)],
            scratch_shapes=scratch,
            input_output_aliases=aliases or {},
            compiler_params=pltpu.CompilerParams(vmem_limit_bytes=limit * MIB),
            cost_estimate=pl.CostEstimate(flops=int(micros * 4e9), bytes_accessed=0, transcendentals=0),
            name=name,
        )(*args)
        self.last = result[-1]
        return result


def stacked(ordered, inputs, out_grad):
    def body(inputs_hbm, grads_hbm, out_ref, sems):
        copies = [
            pltpu.make_async_copy(source, out_ref.at[i], sems.at[i]) for i, source in enumerate((inputs_hbm, grads_hbm))
        ]
        for copy in copies:
            copy.start()
        for copy in copies:
            copy.wait()

    return ordered(
        body,
        (in_hbm(inputs), in_hbm(out_grad)),
        [VMEM((2, *inputs.shape), BF16)],
        "stacked",
        0.5,
        spaces=[pl.ANY, pl.ANY],
        scratch=[pltpu.SemaphoreType.DMA((2,))],
    )[0]


def copied(ordered, chunk, after):
    def body(chunk_ref, out_ref):
        out_ref[...] = chunk_ref[...]

    return ordered(body, (chunk,), [jax.ShapeDtypeStruct(chunk.shape, BF16)], "copied", 0.1, after=after)[0]


def first_product(ordered, core, other, chunk, up_weight, down_weight, name):
    _, rows, features = chunk.shape
    half = up_weight.shape[1] // 2
    tile = tile_of(half)
    pieces = half // tile

    def body(core_ref, chunk_ref, up_hbm, down_hbm, up_ref, down_ref, *refs):
        out_ref, sems = refs[-2:]
        side = 1 - core_ref[0] if other else core_ref[0]
        copies = []
        for i in range(pieces):
            units = pl.ds(pl.multiple_of(side * half + i * tile, tile), tile)
            part = pl.ds(i * tile, tile)
            copies.append(pltpu.make_async_copy(up_hbm.at[:, units], up_ref.at[:, part], sems.at[0, i]))
            copies.append(pltpu.make_async_copy(down_hbm.at[units, :], down_ref.at[part, :], sems.at[1, i]))
        for copy in copies:
            copy.start()
        if not other:
            refs[0][...] = chunk_ref[...]
        for i in range(pieces):
            part = slice(i * tile, (i + 1) * tile)
            copies[2 * i].wait()
            out_ref[0, :, part] = dot(chunk_ref[0], up_ref[:, part], NN).astype(BF16)
            copies[2 * i + 1].wait()
            out_ref[1, :, part] = dot(chunk_ref[1], down_ref[part, :], NT).astype(BF16)

    outs = [VMEM((features, half), BF16), VMEM((half, features), BF16)]
    outs += [] if other else [jax.ShapeDtypeStruct(chunk.shape, BF16)]
    return ordered(
        body,
        (core, chunk, in_hbm(up_weight), in_hbm(down_weight)),
        outs + [jax.ShapeDtypeStruct((2, rows, half), BF16)],
        name,
        4.5,
        spaces=[None, None, pl.ANY, pl.ANY],
        scratch=[pltpu.SemaphoreType.DMA((2, pieces))],
    )


def product(ordered, chunk, up_half, down_half, name, after=()):
    _, rows, features = chunk.shape
    half = up_half.shape[1]
    tile = tile_of(half)

    def body(chunk_ref, up_ref, down_ref, out_ref):
        for start in range(0, half, tile):
            part = slice(start, start + tile)
            out_ref[0, :, part] = dot(chunk_ref[0], up_ref[:, part], NN).astype(BF16)
            out_ref[1, :, part] = dot(chunk_ref[1], down_ref[part, :], NT).astype(BF16)

    args = (chunk, in_vmem(up_half), in_vmem(down_half))
    return ordered(body, args, [jax.ShapeDtypeStruct((2, rows, half), BF16)], name, 2.4, after=after)[0]


def product_terms(terms, part):
    share = None
    for act, up_ref, low in terms:
        term = dot(act, up_ref[part, low : low + act.shape[1]], NT)
        share = term if share is None else share + term
    return share


def grad_of(ref):
    return ref[...] if len(ref.shape) == 2 else ref[0]


def input_product(ordered, rows, terms, micros, partial=None, returned=()):
    features = terms[0][1].shape[0]
    tile = tile_of(features)
    count = len(terms)
    chunks = terms[0][0].shape[-2] // rows

    def body(*refs):
        filled = [(grad_of(refs[i]), refs[count + i], low) for i, (_, _, low) in enumerate(terms)]
        returned_refs, out_refs = refs[2 * count :][: len(returned)], refs[-chunks:]
        if returned:
            total = returned_refs[0][...].astype(F32)
            for ref in returned_refs[1:]:
                total = total + ref[...].astype(F32)
            refs[-chunks - 1][...] = total
        for start in range(0, features, tile):
            part = slice(start, start + tile)
            share = product_terms(filled, part)
            if partial is not None:
                share = share + refs[2 * count + len(returned)][:, part]
            for c, out_ref in enumerate(out_refs):
                out_ref[:, part] = share[c * rows : (c + 1) * rows].astype(BF16)

    args = [act for act, _, _ in terms] + [in_vmem(weight) for _, weight, _ in terms]
    args += [*returned, *([] if partial is None else [partial])]
    outs = [jax.ShapeDtypeStruct((rows, features), F32)] if returned else []
    return ordered(body, args, outs + [jax.ShapeDtypeStruct((rows, features), BF16)] * chunks, "input_product", micros)


def gelu(ordered, sums, apart=False):
    flat = [a for pair in sums for a in pair]
    _, rows, units = flat[0].shape

    def body(*refs):
        grad_ref, value_ref = refs[-2:] if apart else (refs[-1].at[0], refs[-1].at[1])
        for chunk in range(len(sums)):
            at = slice(chunk * rows, (chunk + 1) * rows)
            own_h, own_g, peer_h, peer_g = [refs[2 * chunk + side][i].astype(F32) for side in (0, 1) for i in (0, 1)]
            hidden, grad_hidden = own_h + peer_h, own_g + peer_g
            cdf = 0.5 * (1.0 + lax.erf(hidden * 0.7071067811865476))
            pdf = jnp.exp(-0.5 * hidden * hidden) * 0.3989422804014327
            grad_ref[at] = (grad_hidden * (cdf + hidden * pdf)).astype(BF16)
            value_ref[at] = (hidden * cdf).astype(BF16)

    outs = [jax.ShapeDtypeStruct((rows * len(sums), units), BF16)] * 2
    if not apart:
        outs = [jax.ShapeDtypeStruct((2, rows * len(sums), units), BF16)]
    return ordered(body, flat, outs, "gelu", 0.1)


def collect(ordered, chunks, after):
    count = len(chunks)
    _, rows, features = chunks[0].shape
    tile = tile_of(features, 256)

    def body(*refs):
        turned_ref, grads_ref, scratch = refs[count:]
        for i in range(count):
            scratch[i * rows : (i + 1) * rows, :] = refs[i][0]
            grads_ref[i * rows : (i + 1) * rows, :] = refs[i][1]
        for start in range(0, features, tile):
            turned_ref[start : start + tile, :] = scratch[:, start : start + tile].T

    outs = [VMEM((features, rows * count), BF16), VMEM((rows * count, features), BF16)]
    return ordered(body, chunks, outs, "collect", 0.1, scratch=[VMEM((rows * count, features), BF16)], after=after)


def weight_grads(ordered, core, blocks, turned, all_grads, half, scale, before, name, share=None):
    features, tokens = turned.shape
    width = min(a[0].shape[-1] for a, _ in blocks[0][2])
    up_tile, down_tile = tile_of(features), tile_of(width, 256)
    up_steps, down_steps = features // up_tile, width // down_tile
    slots = 3
    flat = [a for block in blocks for acts, _ in block[2] for a in acts]

    def body(core_ref, turned_ref, grads_ref, *refs):
        up_hbm, down_hbm = refs[outs_at : outs_at + 2]
        done_ref, act_g, act_v, up_stage, down_stage, sems = refs[-6:]
        done_ref[...] = jnp.zeros_like(done_ref)
        busy = {}

        def send(kind, index, value, stage, target):
            slot = index % slots
            if (kind, slot) in busy:
                busy[kind, slot].wait()
            stage[slot] = value * scale
            copy = pltpu.make_async_copy(stage.at[slot], target, sems.at[kind, slot])
            copy.start()
            busy[kind, slot] = copy

        left = refs[: len(flat)]
        for b, (other, first, acts) in enumerate(blocks):
            side = 1 - core_ref[0] if other else core_ref[0]
            base = side * half + first
            row = 0
            for arrays, column in acts:
                rows = slice(row, row + arrays[0].shape[-2])
                columns = slice(column, column + width)
                taken, left = left[: len(arrays)], left[len(arrays) :]
                act_g[rows, :] = taken[0][:, columns] if len(taken) == 2 else taken[0][0, :, columns]
                act_v[rows, :] = taken[1][:, columns] if len(taken) == 2 else taken[0][1, :, columns]
                row += arrays[0].shape[-2]
            for step in range(max(up_steps, down_steps)):
                if step < up_steps:
                    part = slice(step * up_tile, (step + 1) * up_tile)
                    value = dot(turned_ref[part, :], act_g[...], NN)
                    target = up_hbm.at[pl.ds(step * up_tile, up_tile), pl.ds(pl.multiple_of(base, 128), width)]
                    send(0, b * up_steps + step, value, up_stage, target)
                if step < down_steps:
                    part = slice(step * down_tile, (step + 1) * down_tile)
                    value = dot(act_v[:, part], grads_ref[...], TN)
                    target = down_hbm.at[pl.ds(pl.multiple_of(base + step * down_tile, 128), down_tile), :]
                    send(1, b * down_steps + step, value, down_stage, target)
                if share is not None and b == 0 and step < up_steps:
                    part = slice(step * up_tile, (step + 1) * up_tile)
                    terms = [
                        (grad_of(refs[len(flat) + i]), refs[len(flat) + len(share[0]) + i], low)
                        for i, (_, _, low) in enumerate(share[0])
                    ]
                    refs[outs_at + 2][:, part] = product_terms(terms, part).astype(share[1])
        for copy in busy.values():
            copy.wait()

    args = [core, turned, all_grads, *flat]
    outs = [pltpu.HBM((features, 2 * half), F32), pltpu.HBM((2 * half, features), F32)]
    if share is not None:
        terms, kind = share
        args += [act for act, _, _ in terms] + [in_vmem(weight) for _, weight, _ in terms]
        outs.append(jax.ShapeDtypeStruct((terms[0][0].shape[-2], features), kind))
    spaces = [None] * len(args)
    outs_at = len(args) - 3 + (0 if before is None else 2)
    aliases = {}
    if before is not None:
        aliases = {len(args): 0, len(args) + 1: 1}
        args += [in_hbm(a) for a in before]
        spaces += [pl.ANY, pl.ANY]
    return ordered(
        body,
        args,
        [*outs, jax.ShapeDtypeStruct((8, 128), F32)],
        name,
        4.0 * len(blocks),
        spaces=spaces,
        out_spaces=[pl.ANY, pl.ANY] + [VMEM] * (len(outs) - 1),
        scratch=[
            VMEM((tokens, width), BF16),
            VMEM((tokens, width), BF16),
            VMEM((slots, up_tile, width), F32),
            VMEM((slots, down_tile, features), F32),
            pltpu.SemaphoreType.DMA((2, slots)),
        ],
        aliases=aliases,
    )


def per_device(wide, narrow, inputs, up_weight, down_weight, out_grad):
    rows = inputs.shape[0]
    half = up_weight.shape[1] // 2
    chips = wide // 2
    core = (lax.axis_index("wide") & 1).astype(jnp.int32).reshape(1)
    ordered = Ordered()

    def swap_cores(x):
        return lax.ppermute(x, "wide", [(i, i ^ 1) for i in range(wide)])

    ring = [0, *range(1, narrow, 2), *range(narrow - 2, 0, -2)]

    def shift(x, places):
        return lax.ppermute(x, "narrow", [(ring[i], ring[(i + places) % narrow]) for i in range(narrow)])

    def across_chips(keep, got):
        partial = (keep.astype(F32) + got.astype(F32)).astype(BF16)
        hop = 1
        while True:
            peer = lax.ppermute(partial, "wide", [(i, i ^ (2 * hop)) for i in range(wide)])
            hop *= 2
            if hop >= chips:
                return partial, peer
            partial = (partial.astype(F32) + peer.astype(F32)).astype(BF16)

    offsets = sorted(range(narrow // 2 - narrow + 1, narrow // 2 + 1), key=lambda places: (abs(places), -places))
    chunks = {0: stacked(ordered, inputs, out_grad)}

    up_other, down_other, give = first_product(ordered, core, True, chunks[0], up_weight, down_weight, "give_first")
    got = swap_cores(give)
    up_mine, down_mine, sent_back, keep = first_product(ordered, core, False, chunks[0], up_weight, down_weight, "keep_first")
    sums = [across_chips(keep, got)]
    forward = {-1: sent_back}

    def acts_of(sums, apart=False):
        mine = gelu(ordered, sums, apart)
        return mine, [swap_cores(a) for a in mine]

    slices = 2 if half % 256 == 0 else 1
    width = half // slices
    for offset in offsets[1:]:
        places = 1 if offset > 0 else -1
        chunk = chunks[offset] = shift(forward.get(offset, chunks[offset - places]), places)
        if offset == -1:
            forward[2] = copied(ordered, chunks[1], [sums[1][0], chunk])
        give = product(ordered, chunk, up_other, down_other, "give", after=[sums[-1][0]] + [sums[0][1]] * (len(sums) == 2))
        got = swap_cores(give)
        if offset == offsets[-1]:
            early = acts_of(sums[:-1])
        keep = product(ordered, chunk, up_mine, down_mine, "keep")
        if offset != offsets[-1]:
            sums.append(across_chips(keep, got))
        else:
            parts = [slice(i * width, (i + 1) * width) for i in range(slices)]
            late = [across_chips(keep[:, :, part], got[:, :, part]) for part in parts]

    turned, all_grads = collect(ordered, [chunks[offset] for offset in offsets], [own for own, _ in late])
    both = (up_mine, up_other)
    shares = input_product(ordered, rows, [(early[side][0], both[side], 0) for side in (0, 1)], 0.1)
    shares = [share if offset == 0 else shift(share, -offset) for offset, share in zip(offsets, shares)]
    middle = acts_of(sums[-1:], True)

    scale = (rows * narrow) ** -0.5
    late_acts = []

    def grads(places, before, share):
        blocks = [
            (side, i * width, [(early[side], i * width), (middle[side], i * width), (late_acts[i][side], 0)])
            for side, i in places
        ]
        return weight_grads(ordered, core, blocks, turned, all_grads, half, scale, before, "weight_grads", share)

    late_acts.append(acts_of(late[:1]))
    up_grad, down_grad, share, _ = grads([(0, 0)], None, ([(middle[side][0], both[side], 0) for side in (0, 1)], BF16))
    middle_share = shift(share, -offsets[-2])
    partial = None
    terms = [(late_acts[0][side][0], both[side], 0) for side in (0, 1)]
    if slices > 1:
        late_acts.append(acts_of(late[1:]))
        terms.append((late_acts[1][0][0], up_mine, width))
        up_grad, down_grad, partial, _ = grads([(1, 0)], (up_grad, down_grad), (terms, F32))
        terms = [(late_acts[1][1][0], up_other, width)]
    so_far, share = input_product(ordered, rows, terms, 3.0, partial, shares)
    share = shift(share, -offsets[-1])
    last = [(0, 1), (1, 1)] if slices > 1 else [(1, 0)]
    up_grad, down_grad, _ = grads(last, (up_grad, down_grad), None)
    return (so_far + middle_share.astype(F32) + share.astype(F32)).astype(BF16), up_grad, down_grad


def solution(mesh):
    placed = (
        P(("groups", "narrow"), "wide"),
        P("wide", "narrow"),
        P("narrow", "wide"),
        P(("groups", "narrow"), "wide"),
    )
    return jax.shard_map(
        functools.partial(per_device, mesh.shape["wide"], mesh.shape["narrow"]),
        mesh=mesh,
        in_specs=placed,
        out_specs=(
            P(("groups", "narrow"), "wide"),
            P(("groups", "wide"), "narrow"),
            P(("groups", "narrow"), "wide"),
        ),
        check_vma=False,
    )
```
